32 devices in a mesh: img: 8 (over y, x, core), cap: 4 (over z).
Axes of the slice: x: 2, y: 2, z: 4, core: 2. Of those that a mesh axis runs over, the one named last changes fastest.
Arguments:
- image_student: bfloat16 [2560, 1024], P(('img', 'cap')), may hold values from -64 to 64
- caption_student: bfloat16 [2560, 1024], P(('cap', 'img')), may hold values from -64 to 64
- image_teacher: bfloat16 [2560, 768], P(('img', 'cap')), may hold values from -64 to 64
- caption_teacher: bfloat16 [2560, 768], P(('cap', 'img')), may hold values from -64 to 64
Outputs:
- image_grad: float32 [2560, 1024], P(('img', 'cap'))
- caption_grad: float32 [2560, 1024], P(('cap', 'img'))
The draws below stay inside these ranges and needn't reach their ends.
All inputs are finite; a program needn't handle non-finite values.
Results may differ from the reference program's by a relative error of at most 0.004.
Values may be sent and summed in bfloat16 or wider, within the bound.
No kernel may reach another device: no remote copies, remote signals or barrier semaphores. Data moves between devices by JAX's collectives and lax.ppermute only.
A program may use at most 64 MiB of HBM per device.

```python
import math
import jax
import jax.numpy as jnp
from jax import lax

DS = 1024
DT = 768
ROWS = 320
BATCH = 2560


def aligned_pair(key, salt, width):
    key = jax.random.fold_in(key, salt)
    keys = jax.random.split(key, 5)
    images = jax.random.normal(keys[0], (BATCH, width), jnp.float32)
    captions = jax.random.normal(keys[1], (BATCH, width), jnp.float32)
    groups = 8
    stride = BATCH // 16
    first_col = jnp.arange(groups, dtype=jnp.int32) * stride + jax.random.randint(keys[4], (groups,), 0, stride)
    second_col = first_col + BATCH // 2
    first_row = first_col + BATCH // 4
    second_row = (first_col + 3 * (BATCH // 4)) % BATCH
    captions = captions.at[first_col].set(captions[first_col])
    captions = captions.at[second_col].set(captions[second_col])
    images = images.at[first_row].set(images[first_row])
    images = images.at[second_row].set(images[second_row])
    return (jnp.clip(images, -64.0, 64.0), jnp.clip(captions, -64.0, 64.0))


def draw_image_student(key, part):
    pair = aligned_pair(key, 101, DS)
    return pair[0].astype(jnp.bfloat16)


def draw_caption_student(key, part):
    pair = aligned_pair(key, 101, DS)
    return pair[1].astype(jnp.bfloat16)


def draw_image_teacher(key, part):
    pair = aligned_pair(key, 202, DT)
    return pair[0].astype(jnp.bfloat16)


def draw_caption_teacher(key, part):
    pair = aligned_pair(key, 202, DT)
    return pair[1].astype(jnp.bfloat16)


def setup_inputs(seed: int = 0) -> dict:
    splits = jax.random.split(jax.random.key(seed), 5)
    image_student = draw_image_student(jax.random.fold_in(splits[4], 71), 0)
    caption_student = draw_caption_student(jax.random.fold_in(splits[4], 71), 0)
    image_teacher = draw_image_teacher(jax.random.fold_in(splits[4], 71), 0)
    caption_teacher = draw_caption_teacher(jax.random.fold_in(splits[4], 71), 0)
    return dict(image_student=image_student, caption_student=caption_student, image_teacher=image_teacher, caption_teacher=caption_teacher)


def logits(left, right, factor):
    return factor * jnp.dot(left, right.T, preferred_element_type=jnp.float32)

def reference(image_student, caption_student, image_teacher, caption_teacher):
    student_gain = 3.0 / math.sqrt(DS)
    teacher_gain = 3.0 / math.sqrt(DT)
    blocks = BATCH // ROWS
    block_student = image_student.reshape(blocks, ROWS, DS)
    block_teacher = image_teacher.reshape(blocks, ROWS, DT)
    block_index = jnp.arange(blocks, dtype=jnp.int32)

    def first_pass(running, inputs):
        peak_s, total_s, peak_t, total_t = running
        rows_student, rows_teacher = inputs
        student = logits(rows_student, caption_student, student_gain)
        teacher = logits(rows_teacher, caption_teacher, teacher_gain)
        results = []
        for matrix in (student, teacher):
            row_peak = lax.optimization_barrier(jnp.max(matrix, axis=1))
            results.append(row_peak + jnp.log(lax.optimization_barrier(jnp.sum(jnp.exp(matrix - row_peak[:, None]), axis=1))))
        new_state = []
        for matrix, old_peak, old_total in ((student, peak_s, total_s), (teacher, peak_t, total_t)):
            col_peak = lax.optimization_barrier(jnp.max(matrix, axis=0))
            col_total = lax.optimization_barrier(jnp.sum(jnp.exp(matrix - col_peak[None, :]), axis=0))
            merged = jnp.maximum(old_peak, col_peak)
            new_state.append(merged)
            new_state.append(old_total * jnp.exp(old_peak - merged) + col_total * jnp.exp(col_peak - merged))
        return (tuple(new_state), (results[0], results[1]))
    start_peak = jnp.full((BATCH,), -jnp.inf, jnp.float32)
    start_total = jnp.zeros((BATCH,), jnp.float32)
    state, row_lses = lax.scan(first_pass, (start_peak, start_total, start_peak, start_total), (block_student, block_teacher))
    col_lse_student = state[0] + jnp.log(state[1])
    col_lse_teacher = state[2] + jnp.log(state[3])
    column_ids = jnp.arange(BATCH, dtype=jnp.int32)

    def second_pass(caption_acc, inputs):
        rows_student, rows_teacher, lse_student, lse_teacher, which = inputs
        student = logits(rows_student, caption_student, student_gain)
        teacher = logits(rows_teacher, caption_teacher, teacher_gain)
        row_ids = which * ROWS + jnp.arange(ROWS, dtype=jnp.int32)
        diag_mask = (row_ids[:, None] == column_ids[None, :]).astype(jnp.float32)
        tile_grad = 0.5 * (jnp.exp(student - lse_student[:, None]) + jnp.exp(student - col_lse_student[None, :]))
        tile_grad = tile_grad - 0.25 * (jnp.exp(teacher - lse_teacher[:, None]) + jnp.exp(teacher - col_lse_teacher[None, :]))
        tile_grad = (tile_grad - 0.5 * diag_mask).astype(jnp.bfloat16)
        image_part = jnp.dot(tile_grad, caption_student, preferred_element_type=jnp.float32)
        caption_acc = caption_acc + jnp.dot(tile_grad.T, rows_student, preferred_element_type=jnp.float32)
        return (caption_acc, image_part)
    caption_grad, image_parts = lax.scan(second_pass, jnp.zeros((BATCH, DS), jnp.float32), (block_student, block_teacher, row_lses[0], row_lses[1], block_index))
    return (image_parts.reshape(BATCH, DS), caption_grad)
```

```python
import math

import jax
import jax.numpy as jnp
from jax import lax
from jax.sharding import Mesh, PartitionSpec as P

logit_gain = 3.0
ROW_AXES = ("ilo", "clo")
COL_AXES = ("ihi", "chi", "core")


def swap(value, axis, mask):
    size = lax.axis_size(axis)
    return lax.ppermute(value, axis, [(j, j ^ mask) for j in range(size)])


def flip(value, axes, first):
    for d, axis in enumerate(axes):
        bit = 1
        while bit < lax.axis_size(axis):
            size = lax.axis_size(axis)
            swapped = jnp.stack([lax.index_in_dim(value, s ^ bit, first + d, False) for s in range(size)], first + d)
            value = jnp.where((lax.axis_index(axis) & bit) != 0, swapped, value)
            bit *= 2
    return value


def scores(left, right, factor):
    return factor * lax.dot_general(
        left, right, (((1,), (1,)), ((), ())), preferred_element_type=jnp.float32
    )


def partial(matrix, dim):
    peak = jnp.max(matrix, axis=dim)
    total = jnp.sum(jnp.exp(matrix - jnp.expand_dims(peak, dim)), axis=dim)
    return peak, total


def pool(stats, axes, rows):
    shape = tuple(lax.axis_size(a) for a in axes)
    count = math.prod(shape)
    mine = flip(stats.reshape((4,) + shape + (rows,)), axes, 1).reshape(4, count * rows)
    every = lax.all_to_all(
        jnp.broadcast_to(mine[None], (count,) + mine.shape), axes, split_axis=0, concat_axis=0, tiled=True
    )
    result = []
    for k in (0, 2):
        peak = jnp.max(every[:, k], axis=0)
        total = jnp.sum(every[:, k + 1] * jnp.exp(every[:, k] - peak[None]), axis=0)
        result.append(peak + jnp.log(total))
    return flip(jnp.stack(result).reshape((2,) + shape + (rows,)), axes, 1).reshape(2, count * rows)


def owners(shape, axes):
    result = []
    for d, axis in enumerate(axes):
        index = lax.axis_index(axis) ^ jnp.arange(shape[d], dtype=jnp.int32)
        result.append(index.reshape([-1 if e == d else 1 for e in range(len(axes))]))
    return result


def local(image_student, caption_student, image_teacher, caption_teacher):
    ilo, clo, ihi, chi, core = (lax.axis_size(a) for a in ROW_AXES + COL_AXES)
    n_img, n_cap = ihi * ilo * core, chi * clo
    my = {a: lax.axis_index(a) for a in ROW_AXES + COL_AXES}
    rows, width = image_student.shape
    student_gain = logit_gain / math.sqrt(width)
    teacher_gain = logit_gain / math.sqrt(image_teacher.shape[1])

    image = jnp.concatenate([image_student, image_teacher], axis=1)
    caption = jnp.concatenate([caption_student, caption_teacher], axis=1)
    image_far = [image] + [swap(image, "clo", m) for m in range(1, clo)]
    caption_far = [caption] + [swap(caption, "chi", m) for m in range(1, chi)]
    image_slots = image_far + [swap(part, "ilo", m) for m in range(1, ilo) for part in image_far]
    caption_even = caption_far + [swap(part, "ihi", m) for m in range(1, ihi) for part in caption_far]
    caption_slots = [s for part in caption_even for s in (part, swap(part, "core", 1))]
    images = jnp.concatenate(image_slots, axis=0)
    captions = jnp.concatenate(caption_slots, axis=0)
    img_s, img_t = images[:, :width], images[:, width:]
    cap_s, cap_t = captions[:, :width], captions[:, width:]

    student = scores(img_s, cap_s, student_gain)
    teacher = scores(img_t, cap_t, teacher_gain)
    row_s, row_t = pool(jnp.stack(partial(student, 1) + partial(teacher, 1)), ROW_AXES, rows)
    col_s, col_t = pool(jnp.stack(partial(student, 0) + partial(teacher, 0)), COL_AXES, rows)

    inner = jnp.arange(rows, dtype=jnp.int32)
    oi, oc = owners((ilo, clo), ROW_AXES)
    row_owner = (((my["ihi"] * ilo + oi) * core + my["core"]) * chi + my["chi"]) * clo + oc
    oh, oc, ok = owners((ihi, chi, core), COL_AXES)
    col_owner = (((oc * clo + my["clo"]) * ihi + oh) * ilo + my["ilo"]) * core + ok
    row_ids = (row_owner.reshape(-1, 1) * rows + inner[None, :]).reshape(-1)
    col_ids = (col_owner.reshape(-1, 1) * rows + inner[None, :]).reshape(-1)
    diag = (row_ids[:, None] == col_ids[None, :]).astype(jnp.float32)

    tile = 0.5 * (jnp.exp(student - row_s[:, None]) + jnp.exp(student - col_s[None, :]))
    tile = tile - 0.25 * (jnp.exp(teacher - row_t[:, None]) + jnp.exp(teacher - col_t[None, :]))
    tile = (tile - 0.5 * diag).astype(jnp.bfloat16)

    def collect(part, near, far):
        sent = part.astype(jnp.bfloat16)
        held = [part[0, m] for m in range(part.shape[1])]
        for f in reversed(range(part.shape[1])):
            for m in range(1, part.shape[0]):
                held[f] = held[f] + swap(sent[m, f], near, m).astype(jnp.float32)
        total = held[0]
        for f in range(1, part.shape[1]):
            total = total + swap(held[f].astype(jnp.bfloat16), far, f).astype(jnp.float32)
        return total

    caption_part = lax.dot_general(
        tile, img_s, (((0,), (0,)), ((), ())), preferred_element_type=jnp.float32
    ).reshape(ihi, chi, 2, rows, width)
    pair = caption_part[:, :, 0] + swap(caption_part[:, :, 1].astype(jnp.bfloat16), "core", 1).astype(jnp.float32)
    image_part = jnp.dot(tile, cap_s, preferred_element_type=jnp.float32).reshape(ilo, clo, rows, width)
    return (collect(image_part, "ilo", "clo"), collect(pair, "ihi", "chi"))


def split(count):
    low = 1 << ((count.bit_length() - 1) // 2)
    return count // low, low


def solution(mesh):
    ihi, ilo = split(mesh.shape["img"] // 2)
    chi, clo = split(mesh.shape["cap"])
    fine = Mesh(mesh.devices.reshape(ihi, ilo, 2, chi, clo), ("ihi", "ilo", "core", "chi", "clo"))
    by_image = P(("ihi", "ilo", "core", "chi", "clo"), None)
    by_caption = P(("chi", "clo", "ihi", "ilo", "core"), None)
    return jax.shard_map(
        local,
        mesh=fine,
        in_specs=(by_image, by_caption, by_image, by_caption),
        out_specs=(by_image, by_caption),
        check_vma=False,
    )
```

```python
import functools
import math

import jax
import jax.numpy as jnp
from jax import lax
from jax.experimental import pallas as pl
from jax.experimental.pallas import tpu as pltpu
from jax.sharding import Mesh, PartitionSpec as P

logit_gain = 3.0
ROW_AXES = ("ilo", "clo")
COL_AXES = ("core", "ihi", "chi")
LANES = 128
PEAK_S, TOTAL_S, PEAK_T, TOTAL_T, INDEX = range(5)


def swap(value, axis, mask):
    size = lax.axis_size(axis)
    return lax.ppermute(value, axis, [(j, j ^ mask) for j in range(size)])


def bits(axis):
    size = lax.axis_size(axis)
    return [1 << b for b in range(size.bit_length() - 1)]


def joined(refs):
    parts = [ref[...] for ref in refs]
    return parts[0] if len(parts) == 1 else jnp.concatenate(parts, axis=0)


def lines_of(columns):
    count = columns[0].shape[0]
    lane = lax.broadcasted_iota(jnp.int32, (count, LANES), 1)
    wide = jnp.zeros((count, LANES), jnp.float32)
    for k, column in enumerate(columns):
        wide = jnp.where(lane == k, column, wide)
    spare = -count % LANES
    if spare:
        wide = jnp.concatenate([wide, jnp.zeros((spare, LANES), jnp.float32)], axis=0)
    return wide.T[:8, :count]


def columns_of(lines):
    count = lines.shape[1]
    spare = -count % LANES
    if spare:
        lines = jnp.concatenate([lines, jnp.zeros((8, spare), jnp.float32)], axis=1)
    tall = jnp.concatenate([lines, jnp.zeros((LANES - 8, count + spare), jnp.float32)], axis=0)
    return tall.T[:count]


def store_slots(ref, lines, rows):
    ref[...] = jnp.zeros_like(ref)
    for s in range(ref.shape[0]):
        ref[s, :, :rows] = lines[:, s * rows : (s + 1) * rows]


def load_slots(ref, rows):
    return jnp.concatenate([ref[s, :, :rows] for s in range(ref.shape[0])], axis=1)


def logits_kernel(counts, rows, *refs):
    groups, start = [], 0
    for count in counts:
        groups.append(refs[start : start + count])
        start += count
    img_s, img_t, cap_s, cap_t = groups
    student_ref, teacher_ref, row_ref, col_ref = refs[start:]
    row_columns, col_lines = [], []
    for left, right, out in ((img_t, cap_t, teacher_ref), (img_s, cap_s, student_ref)):
        left, right = joined(left), joined(right)
        gain = logit_gain / math.sqrt(left.shape[1])
        out[...] = gain * lax.dot_general(
            left, right, (((1,), (1,)), ((), ())), preferred_element_type=jnp.float32
        )
        matrix = out[...]
        peak = jnp.max(matrix, axis=1, keepdims=True)
        row_columns = [peak, jnp.sum(jnp.exp(matrix - peak), axis=1, keepdims=True)] + row_columns
        peak = jnp.max(matrix, axis=0, keepdims=True)
        col_lines = [peak, jnp.sum(jnp.exp(matrix - peak), axis=0, keepdims=True)] + col_lines
    store_slots(row_ref, lines_of(row_columns), rows)
    blank = jnp.zeros((4, col_lines[0].shape[1]), jnp.float32)
    store_slots(col_ref, jnp.concatenate(col_lines + [blank], axis=0), rows)


def tile_kernel(n_img, rows, *refs):
    student_ref, teacher_ref, row_ref, row_id_ref, col_ref, col_id_ref = refs[:6]
    images = refs[6 : 6 + n_img]
    tile_ref, held_ref, sent_ref = refs[6 + n_img :]

    def finish(ref, id_ref):
        lines = load_slots(ref, rows)
        ids = load_slots(id_ref, rows)
        line = lax.broadcasted_iota(jnp.int32, lines.shape, 0)
        lse_s = lines[PEAK_S : PEAK_S + 1] + jnp.log(lines[TOTAL_S : TOTAL_S + 1])
        lse_t = lines[PEAK_T : PEAK_T + 1] + jnp.log(lines[TOTAL_T : TOTAL_T + 1])
        return jnp.where(line == 0, lse_s, jnp.where(line == 1, lse_t, ids))

    across = finish(col_ref, col_id_ref)
    down = columns_of(finish(row_ref, row_id_ref))
    total = student_ref.shape[0]
    step = 64 if total % 64 == 0 else total
    for r in range(0, total, step):
        at = slice(r, r + step)
        s, t = student_ref[at], teacher_ref[at]
        grad = 0.5 * (jnp.exp(s - down[at, 0:1]) + jnp.exp(s - across[0:1]))
        grad = grad - 0.25 * (jnp.exp(t - down[at, 1:2]) + jnp.exp(t - across[1:2]))
        grad = grad - jnp.where(down[at, INDEX : INDEX + 1] == across[INDEX : INDEX + 1], 0.5, 0.0)
        tile_ref[at] = grad.astype(jnp.bfloat16)
    part = lax.dot_general(
        tile_ref[...], joined(images), (((0,), (0,)), ((), ())), preferred_element_type=jnp.float32
    )
    held = held_ref.shape[0]
    held_ref[...] = part[:held]
    sent_ref[...] = part[held:].astype(jnp.bfloat16)


def image_kernel(tile_ref, *refs):
    held_ref, sent_ref = refs[-2:]
    part = jnp.dot(tile_ref[...], joined(refs[:-2]), preferred_element_type=jnp.float32)
    held = held_ref.shape[0]
    held_ref[...] = part[:held]
    sent_ref[...] = part[held:].astype(jnp.bfloat16)


def call(kernel, outs, args, flops):
    moved = sum(math.prod(a.shape) * a.dtype.itemsize for a in list(args) + list(outs))
    return pl.pallas_call(
        kernel,
        out_shape=outs,
        in_specs=[pl.BlockSpec(memory_space=pltpu.VMEM)] * len(args),
        out_specs=[pl.BlockSpec(memory_space=pltpu.VMEM)] * len(outs),
        compiler_params=pltpu.CompilerParams(vmem_limit_bytes=32 * 2**20),
        cost_estimate=pl.CostEstimate(flops=flops, bytes_accessed=moved, transcendentals=0),
    )(*args)


def merge(one, two):
    result = []
    for k in (PEAK_S, PEAK_T):
        peak = jnp.maximum(one[..., k, :], two[..., k, :])
        result.append(peak)
        result.append(
            one[..., k + 1, :] * jnp.exp(one[..., k, :] - peak) + two[..., k + 1, :] * jnp.exp(two[..., k, :] - peak)
        )
    result += [jnp.zeros_like(result[0])] * 4
    return jnp.stack(result, axis=-2)


def pool_step(stats, axes, d, bit):
    shape = tuple(lax.axis_size(a) for a in axes)
    other = swap(stats, axes[d], bit)
    before = math.prod(shape[:d]) * (shape[d] // (2 * bit))
    after = bit * math.prod(shape[d + 1 :])
    other = jnp.flip(other.reshape((before, 2, after) + stats.shape[1:]), axis=1).reshape(stats.shape)
    return merge(stats, other)


def owners(axes):
    result = {}
    for d, axis in enumerate(axes):
        index = lax.axis_index(axis) ^ jnp.arange(lax.axis_size(axis), dtype=jnp.int32)
        result[axis] = index.reshape([-1 if e == d else 1 for e in range(len(axes))])
    return result


def identity_block(axes, order, rows):
    place = {a: lax.axis_index(a) for a in order}
    place.update(owners(axes))
    owner = 0
    for axis in order:
        owner = owner * lax.axis_size(axis) + place[axis]
    index = owner.reshape(-1, 1, 1) * rows + jnp.arange(LANES, dtype=jnp.int32)[None, None, :]
    line = jnp.arange(8, dtype=jnp.int32)[None, :, None]
    return jnp.where(line == INDEX, index, 0).astype(jnp.float32)


def local(image_student, caption_student, image_teacher, caption_teacher):
    ilo, clo, core, ihi, chi = (lax.axis_size(a) for a in ROW_AXES + COL_AXES)
    rows, width = image_student.shape
    assert rows <= LANES and core == 2
    n_img, n_cap = ilo * clo, core * ihi * chi
    total, columns = n_img * rows, n_cap * rows

    def gather_images(own):
        far = [own] + [swap(own, "clo", m) for m in range(1, clo)]
        return far + [swap(part, "ilo", m) for m in range(1, ilo) for part in far]

    def gather_captions(own):
        far = [own] + [swap(own, "chi", m) for m in range(1, chi)]
        far = far + [swap(part, "ihi", m) for m in range(1, ihi) for part in far]
        return far + [swap(part, "core", 1) for part in far]

    def shards(parts):
        return parts if rows % 16 == 0 else [jnp.concatenate(parts, axis=0)]

    img_t, cap_t = shards(gather_images(image_teacher)), shards(gather_captions(caption_teacher))
    img_s, cap_s = shards(gather_images(image_student)), shards(gather_captions(caption_student))

    f32, bf16 = jnp.float32, jnp.bfloat16
    shape = jax.ShapeDtypeStruct
    student, teacher, row_stats, col_stats = call(
        functools.partial(logits_kernel, [len(g) for g in (img_s, img_t, cap_s, cap_t)], rows),
        [
            shape((total, columns), f32),
            shape((total, columns), f32),
            shape((n_img, 8, LANES), f32),
            shape((n_cap, 8, LANES), f32),
        ],
        img_s + img_t + cap_s + cap_t,
        2 * total * columns * (width + image_teacher.shape[1]),
    )
    for d, axis in enumerate(ROW_AXES):
        for bit in bits(axis):
            row_stats = pool_step(row_stats, ROW_AXES, d, bit)
    for d, axis in enumerate(COL_AXES):
        for bit in bits(axis):
            col_stats = pool_step(col_stats, COL_AXES, d, bit)
    row_ids = identity_block(ROW_AXES, ("ihi", "ilo", "core", "chi", "clo"), rows)
    col_ids = identity_block(COL_AXES, ("chi", "clo", "ihi", "ilo", "core"), rows)

    tile, held, sent = call(
        functools.partial(tile_kernel, len(img_s), rows),
        [shape((total, columns), bf16), shape((columns // 2, width), f32), shape((columns // 2, width), bf16)],
        [student, teacher, row_stats, row_ids, col_stats, col_ids] + img_s,
        2 * total * columns * width,
    )
    image_held, image_sent = call(
        image_kernel,
        [shape((total // ilo, width), f32), shape((total - total // ilo, width), bf16)],
        [tile] + cap_s,
        2 * total * columns * width,
    )

    def collect(held, sent, near, far):
        near, far, count = near, far, held.shape[0]
        held = [held[f] for f in range(count)]
        for f in reversed(range(count)):
            for m in range(1, lax.axis_size(near)):
                held[f] = held[f] + swap(sent[m - 1, f], near, m).astype(f32)
        result = held[0]
        for f in range(1, count):
            result = result + swap(held[f].astype(bf16), far, f).astype(f32)
        return result

    pair = (held + swap(sent, "core", 1).astype(f32)).reshape(ihi, chi, rows, width)
    caption_grad = collect(pair[0], pair[1:].astype(bf16), "ihi", "chi")
    image_grad = collect(
        image_held.reshape(clo, rows, width), image_sent.reshape(ilo - 1, clo, rows, width), "ilo", "clo"
    )
    return (image_grad, caption_grad)


def split(count):
    low = 1 << ((count.bit_length() - 1) // 2)
    return count // low, low


def solution(mesh):
    ihi, ilo = split(mesh.shape["img"] // 2)
    chi, clo = split(mesh.shape["cap"])
    fine = Mesh(mesh.devices.reshape(ihi, ilo, 2, chi, clo), ("ihi", "ilo", "core", "chi", "clo"))
    by_image = P(("ihi", "ilo", "core", "chi", "clo"), None)
    by_caption = P(("chi", "clo", "ihi", "ilo", "core"), None)
    return jax.shard_map(
        local,
        mesh=fine,
        in_specs=(by_image, by_caption, by_image, by_caption),
        out_specs=(by_image, by_caption),
        check_vma=False,
    )
```

```python
import functools
import math

import jax
import jax.numpy as jnp
from jax import lax
from jax.experimental import pallas as pl
from jax.experimental.pallas import tpu as pltpu
from jax.sharding import Mesh, PartitionSpec as P

logit_gain = 3.0
ROW_AXES = ("ilo", "chi")
COL_AXES = ("core", "ihi", "clo")
LANES = 128
PEAK_S, TOTAL_S, PEAK_T, TOTAL_T, INDEX = range(5)


def swap(value, axis, mask):
    size = lax.axis_size(axis)
    return lax.ppermute(value, axis, [(j, j ^ mask) for j in range(size)])


def bits(axis):
    size = lax.axis_size(axis)
    return [1 << b for b in range(size.bit_length() - 1)]


def lines_of(columns):
    count = columns[0].shape[0]
    lane = lax.broadcasted_iota(jnp.int32, (count, LANES), 1)
    wide = jnp.zeros((count, LANES), jnp.float32)
    for k, column in enumerate(columns):
        wide = jnp.where(lane == k, column, wide)
    spare = -count % LANES
    if spare:
        wide = jnp.concatenate([wide, jnp.zeros((spare, LANES), jnp.float32)], axis=0)
    return wide.T[:8, :count]


def columns_of(lines):
    count = lines.shape[1]
    spare = -count % LANES
    if spare:
        lines = jnp.concatenate([lines, jnp.zeros((8, spare), jnp.float32)], axis=1)
    tall = jnp.concatenate([lines, jnp.zeros((LANES - 8, count + spare), jnp.float32)], axis=0)
    return tall.T[:count]


def store_slots(ref, lines, rows):
    ref[...] = jnp.zeros_like(ref)
    for s in range(ref.shape[0]):
        ref[s, :, :rows] = lines[:, s * rows : (s + 1) * rows]


def load_slots(ref, rows):
    return jnp.concatenate([ref[s, :, :rows] for s in range(ref.shape[0])], axis=1)


def pack_kernel(left, right, out, sem):
    width = left.shape[1]
    copies = [
        pltpu.make_async_copy(left, out.at[:, :width], sem.at[0]),
        pltpu.make_async_copy(right, out.at[:, width:], sem.at[1]),
    ]
    for copy in copies:
        copy.start()
    for copy in copies:
        copy.wait()


def place(pieces, sems):
    copies = [pltpu.make_async_copy(src, dst, sem) for (src, dst), sem in zip(pieces, sems)]
    for copy in copies:
        copy.start()
    return copies


def logits_kernel(n_img, n_cap, rows, width, *refs):
    img_s_parts, refs = refs[:n_img], refs[n_img:]
    img_t_parts, refs = refs[:n_img], refs[n_img:]
    cap_parts, refs = refs[:n_cap], refs[n_cap:]
    student_ref, teacher_ref, row_ref, col_ref, img_s, cap_s, img_t, cap_t, sems = refs

    def pieces(parts, out, columns):
        each = out.shape[0] // len(parts)
        return [(part.at[:, columns], out.at[k * each : (k + 1) * each]) for k, part in enumerate(parts)]

    front, back = slice(0, width), slice(width, width + cap_t.shape[1])
    everything = (
        pieces(cap_parts, cap_t, back)
        + pieces(img_t_parts, img_t, slice(None))
        + pieces(cap_parts, cap_s, front)
        + pieces(img_s_parts, img_s, slice(None))
    )
    copies = place(everything, [sems.at[k] for k in range(len(everything))])
    half = n_img + n_cap
    row_columns, col_lines = [], []
    for wait, left, right, out in (
        (copies[:half], img_t, cap_t, teacher_ref),
        (copies[half:], img_s, cap_s, student_ref),
    ):
        for copy in wait:
            copy.wait()
        gain = logit_gain / math.sqrt(left.shape[1])
        out[...] = gain * lax.dot_general(
            left[...], right[...], (((1,), (1,)), ((), ())), preferred_element_type=jnp.float32
        )
        matrix = out[...]
        peak = jnp.max(matrix, axis=1, keepdims=True)
        row_columns = [peak, jnp.sum(jnp.exp(matrix - peak), axis=1, keepdims=True)] + row_columns
        peak = jnp.max(matrix, axis=0, keepdims=True)
        col_lines = [peak, jnp.sum(jnp.exp(matrix - peak), axis=0, keepdims=True)] + col_lines
    store_slots(row_ref, lines_of(row_columns), rows)
    blank = jnp.zeros((4, col_lines[0].shape[1]), jnp.float32)
    store_slots(col_ref, jnp.concatenate(col_lines + [blank], axis=0), rows)


def tile_kernel(rows, student_ref, teacher_ref, row_ref, row_id_ref, col_ref, col_id_ref, cap_s, tile_ref, *outs):
    def finish(ref, id_ref):
        lines = load_slots(ref, rows)
        ids = load_slots(id_ref, rows)
        line = lax.broadcasted_iota(jnp.int32, lines.shape, 0)
        lse_s = lines[PEAK_S : PEAK_S + 1] + jnp.log(lines[TOTAL_S : TOTAL_S + 1])
        lse_t = lines[PEAK_T : PEAK_T + 1] + jnp.log(lines[TOTAL_T : TOTAL_T + 1])
        return jnp.where(line == 0, lse_s, jnp.where(line == 1, lse_t, ids))

    across = finish(col_ref, col_id_ref)
    down = columns_of(finish(row_ref, row_id_ref))
    total = student_ref.shape[0]
    step = 64 if total % 64 == 0 else total
    for r in range(0, total, step):
        at = slice(r, r + step)
        s, t = student_ref[at], teacher_ref[at]
        grad = 0.5 * (jnp.exp(s - down[at, 0:1]) + jnp.exp(s - across[0:1]))
        grad = grad - 0.25 * (jnp.exp(t - down[at, 1:2]) + jnp.exp(t - across[1:2]))
        grad = grad - jnp.where(down[at, INDEX : INDEX + 1] == across[INDEX : INDEX + 1], 0.5, 0.0)
        tile_ref[at] = grad.astype(jnp.bfloat16)
    spread(jnp.dot(tile_ref[...], cap_s[...], preferred_element_type=jnp.float32), outs)


def caption_kernel(tile_ref, img_s, *outs):
    part = lax.dot_general(
        tile_ref[...], img_s[...], (((0,), (0,)), ((), ())), preferred_element_type=jnp.float32
    )
    spread(part, outs)


def spread(part, outs):
    start = 0
    for out in outs:
        out[...] = part[start : start + out.shape[0]].astype(out.dtype)
        start += out.shape[0]


def merge_kernel(order, one, two, out):
    for s, o in enumerate(order):
        x, y = one[s], two[o]
        peak_s = jnp.maximum(x[PEAK_S : PEAK_S + 1], y[PEAK_S : PEAK_S + 1])
        peak_t = jnp.maximum(x[PEAK_T : PEAK_T + 1], y[PEAK_T : PEAK_T + 1])
        line = lax.broadcasted_iota(jnp.int32, x.shape, 0)
        peak = jnp.where(line <= TOTAL_S, peak_s, peak_t)
        x_peak = jnp.where(line <= TOTAL_S, x[PEAK_S : PEAK_S + 1], x[PEAK_T : PEAK_T + 1])
        y_peak = jnp.where(line <= TOTAL_S, y[PEAK_S : PEAK_S + 1], y[PEAK_T : PEAK_T + 1])
        total = x * jnp.exp(x_peak - peak) + y * jnp.exp(y_peak - peak)
        merged = jnp.where((line == PEAK_S) | (line == PEAK_T), peak, total)
        out[s] = jnp.where(line < INDEX, merged, 0.0)


VMEM, ANY = pltpu.VMEM, pl.ANY


def call(kernel, outs, args, flops=0, scratch=(), space=VMEM, out_space=VMEM):
    moved = sum(math.prod(a.shape) * a.dtype.itemsize for a in list(args) + list(outs))
    return pl.pallas_call(
        kernel,
        out_shape=outs,
        in_specs=[pl.BlockSpec(memory_space=space)] * len(args),
        out_specs=[pl.BlockSpec(memory_space=out_space)] * len(outs),
        scratch_shapes=scratch,
        compiler_params=pltpu.CompilerParams(vmem_limit_bytes=16 * 2**20),
        cost_estimate=pl.CostEstimate(flops=flops, bytes_accessed=moved, transcendentals=0),
    )(*args)


def pool_step(stats, axes, d, bit):
    stride = math.prod(lax.axis_size(a) for a in axes[d + 1 :]) * bit
    order = [s ^ stride for s in range(stats.shape[0])]
    other = swap(stats, axes[d], bit)
    return call(
        functools.partial(merge_kernel, order), [jax.ShapeDtypeStruct(stats.shape, stats.dtype)], [stats, other]
    )[0]


def owners(axes):
    result = {}
    for d, axis in enumerate(axes):
        index = lax.axis_index(axis) ^ jnp.arange(lax.axis_size(axis), dtype=jnp.int32)
        result[axis] = index.reshape([-1 if e == d else 1 for e in range(len(axes))])
    return result


def identity_block(axes, order, rows):
    place = {a: lax.axis_index(a) for a in order}
    place.update(owners(axes))
    owner = 0
    for axis in order:
        owner = owner * lax.axis_size(axis) + place[axis]
    index = owner.reshape(-1, 1, 1) * rows + jnp.arange(LANES, dtype=jnp.int32)[None, None, :]
    line = jnp.arange(8, dtype=jnp.int32)[None, :, None]
    return jnp.where(line == INDEX, index, 0).astype(jnp.float32)


def after(value, other):
    return lax.optimization_barrier((value, other))[0]


def local(image_student, caption_student, image_teacher, caption_teacher):
    ilo, chi, core, ihi, clo = (lax.axis_size(a) for a in ROW_AXES + COL_AXES)
    rows, width = image_student.shape
    depth = image_teacher.shape[1]
    assert rows <= LANES and core == 2
    n_img, n_cap = ilo * chi, core * ihi * clo
    total, columns = n_img * rows, n_cap * rows
    f32, bf16 = jnp.float32, jnp.bfloat16
    shape = jax.ShapeDtypeStruct

    def gather_images(own):
        far = [own] + [swap(own, "chi", m) for m in range(1, chi)]
        return far + [swap(part, "ilo", m) for m in range(1, ilo) for part in far]

    def gather_captions(own):
        far = [own] + [swap(own, "clo", m) for m in range(1, clo)]
        far = far + [swap(part, "ihi", m) for m in range(1, ihi) for part in far]
        return far + [swap(part, "core", 1) for part in far]

    def shards(parts):
        return parts if rows % 16 == 0 else [jnp.concatenate(parts, axis=0)]

    if rows % 16 == 0:
        caption = call(
            pack_kernel,
            [shape((rows, width + depth), bf16)],
            [caption_student, caption_teacher],
            scratch=[pltpu.SemaphoreType.DMA((2,))],
            space=ANY,
            out_space=ANY,
        )[0]
    else:
        caption = jnp.concatenate([caption_student, caption_teacher], axis=1)
    img_t, img_s = shards(gather_images(image_teacher)), shards(gather_images(image_student))
    cap = shards(gather_captions(caption))

    student, teacher, row_stats, col_stats, images, captions = call(
        functools.partial(logits_kernel, len(img_s), len(cap), rows, width),
        [
            shape((total, columns), f32),
            shape((total, columns), f32),
            shape((n_img, 8, LANES), f32),
            shape((n_cap, 8, LANES), f32),
            shape((total, width), bf16),
            shape((columns, width), bf16),
        ],
        img_s + img_t + cap,
        2 * total * columns * (width + depth),
        scratch=[
            pltpu.VMEM((total, depth), bf16),
            pltpu.VMEM((columns, depth), bf16),
            pltpu.SemaphoreType.DMA((2 * (len(img_s) + len(cap)),)),
        ],
        space=ANY,
    )
    for d, axis in enumerate(ROW_AXES):
        for bit in bits(axis):
            row_stats = pool_step(row_stats, ROW_AXES, d, bit)
    for d, axis in enumerate(COL_AXES):
        for bit in bits(axis):
            col_stats = pool_step(col_stats, COL_AXES, d, bit)
    row_ids = identity_block(ROW_AXES, ("ihi", "ilo", "core", "chi", "clo"), rows)
    col_ids = identity_block(COL_AXES, ("chi", "clo", "ihi", "ilo", "core"), rows)

    def outs(count, near, far):
        piece = count // (near * far)
        own = [shape((piece, width), f32)] * far
        return own + [shape((piece, width), bf16)] * ((near - 1) * far)

    tile, *image_parts = call(
        functools.partial(tile_kernel, rows),
        [shape((total, columns), bf16)] + outs(total, ilo, chi),
        [student, teacher, row_stats, row_ids, col_stats, col_ids, captions],
        2 * total * columns * width,
    )
    held, sent = call(
        caption_kernel,
        [shape((columns // 2, width), f32), shape((columns // 2, width), bf16)],
        [tile, images],
        2 * total * columns * width,
    )

    def collect(held, sent, near, far):
        count = lax.axis_size(far)
        held = list(held)
        arrived = None
        for f in reversed(range(count)):
            for m in range(1, lax.axis_size(near)):
                term = sent[m - 1][f]
                if f == 0 and arrived is not None:
                    term = after(term, arrived)
                arrived = swap(term, near, m)
                held[f] = held[f] + arrived.astype(f32)
        result = held[0]
        for f in range(1, count):
            result = result + swap(held[f].astype(bf16), far, f).astype(f32)
        return result

    image_sent = [image_parts[m * chi : (m + 1) * chi] for m in range(1, ilo)]
    image_grad = collect(image_parts[:chi], image_sent, "ilo", "chi")
    pair = (held + swap(sent, "core", 1).astype(f32)).reshape(ihi, clo, rows, width)
    caption_grad = collect(pair[0], pair[1:].astype(bf16), "ihi", "clo")
    return (image_grad, caption_grad)


def split(count):
    low = 1 << ((count.bit_length() - 1) // 2)
    return count // low, low


def solution(mesh):
    ihi, ilo = split(mesh.shape["img"] // 2)
    chi, clo = split(mesh.shape["cap"])
    fine = Mesh(mesh.devices.reshape(ihi, ilo, 2, chi, clo), ("ihi", "ilo", "core", "chi", "clo"))
    by_image = P(("ihi", "ilo", "core", "chi", "clo"), None)
    by_caption = P(("chi", "clo", "ihi", "ilo", "core"), None)
    return jax.shard_map(
        local,
        mesh=fine,
        in_specs=(by_image, by_caption, by_image, by_caption),
        out_specs=(by_image, by_caption),
        check_vma=False,
    )
```

```python
import functools
import math

import jax
import jax.numpy as jnp
from jax import lax
from jax.experimental import pallas as pl
from jax.experimental.pallas import tpu as pltpu
from jax.sharding import Mesh, PartitionSpec as P

logit_gain = 3.0
ROW_AXES = ("ilo", "chi")
COL_AXES = ("core", "ihi", "clo")
ROW_STEPS = ("ilo", "chi")
COL_STEPS = ("ihi", "clo", "core")
ROW_ORDER = ("ihi", "ilo", "core", "chi", "clo")
COL_ORDER = ("chi", "clo", "ihi", "ilo", "core")
LANES = 128
PEAK_S, TOTAL_S, PEAK_T, TOTAL_T, INDEX = range(5)


def swap(value, axis, mask):
    size = lax.axis_size(axis)
    return lax.ppermute(value, axis, [(j, j ^ mask) for j in range(size)])


def bits(axis):
    size = lax.axis_size(axis)
    return [1 << b for b in range(size.bit_length() - 1)]


def lines_of(columns):
    count = columns[0].shape[0]
    lane = lax.broadcasted_iota(jnp.int32, (count, LANES), 1)
    wide = jnp.zeros((count, LANES), jnp.float32)
    for k, column in enumerate(columns):
        wide = jnp.where(lane == k, column, wide)
    spare = -count % LANES
    if spare:
        wide = jnp.concatenate([wide, jnp.zeros((spare, LANES), jnp.float32)], axis=0)
    return wide.T[:8, :count]


def columns_of(lines):
    count = lines.shape[1]
    spare = -count % LANES
    if spare:
        lines = jnp.concatenate([lines, jnp.zeros((8, spare), jnp.float32)], axis=1)
    tall = jnp.concatenate([lines, jnp.zeros((LANES - 8, count + spare), jnp.float32)], axis=0)
    return tall.T[:count]


def load_slots(blocks, rows):
    return jnp.concatenate([block[:, :rows] for block in blocks], axis=1)


def owners(axes, order):
    sizes = [lax.axis_size(a) for a in axes]
    result = []
    for s in range(math.prod(sizes)):
        place = {a: lax.axis_index(a) for a in order}
        for axis, size in zip(reversed(axes), reversed(sizes)):
            place[axis] = place[axis] ^ (s % size)
            s //= size
        owner = 0
        for axis in order:
            owner = owner * lax.axis_size(axis) + place[axis]
        result.append(owner)
    return result


def joined(refs, columns=slice(None)):
    values = [ref[:, columns] for ref in refs]
    return values[0] if len(values) == 1 else jnp.concatenate(values, axis=0)


def copy_all(pairs, sems):
    copies = [pltpu.make_async_copy(src, dst, sems.at[k]) for k, (src, dst) in enumerate(pairs)]
    for copy in copies:
        copy.start()
    for copy in copies:
        copy.wait()


def pack_kernel(image_s, image_t, caption_s, caption_t, image, caption, sems):
    width = image_s.shape[1]
    copy_all(
        [
            (image_s, image.at[:, :width]),
            (image_t, image.at[:, width:]),
            (caption_s, caption.at[:, :width]),
            (caption_t, caption.at[:, width:]),
        ],
        sems,
    )


def assemble_kernel(*refs):
    refs[-1][...] = joined(refs[:-1])


def logits(left, right, out):
    gain = logit_gain / math.sqrt(left.shape[1])
    out[...] = gain * lax.dot_general(left, right, (((1,), (1,)), ((), ())), preferred_element_type=jnp.float32)
    matrix = out[...]
    peak = jnp.max(matrix, axis=1, keepdims=True)
    columns = [peak, jnp.sum(jnp.exp(matrix - peak), axis=1, keepdims=True)]
    peak = jnp.max(matrix, axis=0, keepdims=True)
    return columns, [peak, jnp.sum(jnp.exp(matrix - peak), axis=0, keepdims=True)]


def logits_kernel(n_img, rows, width, *refs):
    img_parts, cap_parts = refs[:n_img], refs[n_img:-5]
    student_ref, teacher_ref, row_ref, col_ref, images = refs[-5:]
    columns, lines = [], []
    for part, out in ((slice(0, width), student_ref), (slice(width, None), teacher_ref)):
        left = joined(img_parts, part)
        if out is student_ref:
            images[...] = left
        more = logits(left, joined(cap_parts, part), out)
        columns, lines = columns + more[0], lines + more[1]
    lines.append(jnp.zeros((4, lines[0].shape[1]), jnp.float32))
    row = lax.broadcasted_iota(jnp.int32, (8, LANES), 0)
    lane = lax.broadcasted_iota(jnp.int32, (8, LANES), 1)
    for ref, values, axes, order in (
        (row_ref, lines_of(columns), ROW_AXES, ROW_ORDER),
        (col_ref, jnp.concatenate(lines, axis=0), COL_AXES, COL_ORDER),
    ):
        for s, owner in enumerate(owners(axes, order)):
            ref[s] = jnp.zeros((8, LANES), jnp.float32)
            ref[s, :, :rows] = values[:, s * rows : (s + 1) * rows]
            index = (owner * rows + lane).astype(jnp.float32)
            ref[s] = jnp.where(row == INDEX, index, ref[s])


def merged(x, y):
    line = lax.broadcasted_iota(jnp.int32, x.shape, 0)
    student = line <= TOTAL_S
    x_peak = jnp.where(student, x[PEAK_S : PEAK_S + 1], x[PEAK_T : PEAK_T + 1])
    y_peak = jnp.where(student, y[PEAK_S : PEAK_S + 1], y[PEAK_T : PEAK_T + 1])
    peak = jnp.maximum(x_peak, y_peak)
    total = x * jnp.exp(x_peak - peak) + y * jnp.exp(y_peak - peak)
    both = jnp.where((line == PEAK_S) | (line == PEAK_T), peak, total)
    return jnp.where(line < INDEX, both, x)


def merged_blocks(mine, other, distance):
    return [merged(mine[s], other[s ^ distance]) for s in range(mine.shape[0])]


def merge_kernel(distances, *refs):
    n = len(distances)
    for k, distance in enumerate(distances):
        for s, block in enumerate(merged_blocks(refs[2 * k], refs[2 * k + 1], distance)):
            refs[2 * n + k][s] = block


def tile_kernel(distances, rows, student_ref, teacher_ref, *refs):
    refs = list(refs)
    blocks = []
    for distance in distances:
        mine = refs.pop(0)
        if distance is None:
            blocks.append([mine[s] for s in range(mine.shape[0])])
        else:
            blocks.append(merged_blocks(mine, refs.pop(0), distance))
    tile_ref, send_ref = refs
    total, count = teacher_ref.shape

    def finish(blocks):
        lines = load_slots(blocks, rows)
        line = lax.broadcasted_iota(jnp.int32, lines.shape, 0)
        lse_s = lines[PEAK_S : PEAK_S + 1] + jnp.log(lines[TOTAL_S : TOTAL_S + 1])
        lse_t = lines[PEAK_T : PEAK_T + 1] + jnp.log(lines[TOTAL_T : TOTAL_T + 1])
        return jnp.where(line == 0, lse_s, jnp.where(line == 1, lse_t, lines))

    down, across = columns_of(finish(blocks[0])), finish(blocks[1])
    step = 64 if total % 64 == 0 else total
    for r in range(0, total, step):
        at = slice(r, r + step)
        s, t = student_ref[at], teacher_ref[at]
        grad = 0.5 * (jnp.exp(s - down[at, 0:1]) + jnp.exp(s - across[0:1]))
        grad = grad - 0.25 * (jnp.exp(t - down[at, 1:2]) + jnp.exp(t - across[1:2]))
        grad = grad - jnp.where(down[at, INDEX : INDEX + 1] == across[INDEX : INDEX + 1], 0.5, 0.0)
        tile_ref[at] = grad.astype(jnp.bfloat16)
    send_ref[...] = tile_ref[:, count // 2 :]


def spread(part, outs):
    start = 0
    for out in outs:
        out[...] = part[start : start + out.shape[0]].astype(out.dtype)
        start += out.shape[0]


def image_kernel(width, tile_ref, *refs):
    parts = [ref for ref in refs if ref.dtype == jnp.bfloat16 and ref.shape[1] > width]
    right = joined(parts, slice(0, width))
    spread(jnp.dot(tile_ref[...], right, preferred_element_type=jnp.float32), refs[len(parts) :])


def caption_kernel(tile_ref, tile_other, images, images_other, *outs):
    half = tile_other.shape[1]
    part = 0.0
    for tile, rows in ((tile_ref[:, :half], images[...]), (tile_other[...], images_other[...])):
        part = part + lax.dot_general(tile, rows, (((0,), (0,)), ((), ())), preferred_element_type=jnp.float32)
    spread(part, outs)


def sum_kernel(counts, *refs):
    refs = list(refs)
    terms = [[refs.pop(0) for _ in range(count)] for count in counts]
    outs, held, sems = refs[: len(counts)], refs[len(counts) : -1], refs[-1]
    copies = []
    for k, (group, out, here) in enumerate(zip(terms, outs, held)):
        total = group[0][...]
        for term in group[1:]:
            total = total + term[...].astype(jnp.float32)
        here[...] = total
        copies.append(pltpu.make_async_copy(here, out, sems.at[k]))
        copies[-1].start()
    for copy in copies:
        copy.wait()


VMEM, HBM = pltpu.VMEM, pltpu.HBM


def call(kernel, outs, args, flops=0, scratch=(), in_hbm=0, out_space=VMEM):
    moved = sum(math.prod(a.shape) * a.dtype.itemsize for a in list(args) + list(outs))
    spaces = [HBM] * in_hbm + [VMEM] * (len(args) - in_hbm)
    return pl.pallas_call(
        kernel,
        out_shape=[out_space(out.shape, out.dtype) for out in outs],
        in_specs=[pl.BlockSpec(memory_space=space) for space in spaces],
        out_specs=[pl.BlockSpec(memory_space=out_space)] * len(outs),
        scratch_shapes=scratch,
        compiler_params=pltpu.CompilerParams(vmem_limit_bytes=16 * 2**20),
        cost_estimate=pl.CostEstimate(flops=flops, bytes_accessed=moved, transcendentals=0),
    )(*(pltpu.with_memory_space_constraint(arg, space) for arg, space in zip(args, spaces)))


def steps_of(names, axes):
    result = []
    for name in names:
        stride = math.prod(lax.axis_size(a) for a in axes[axes.index(name) + 1 :])
        result += [(name, bit, stride * bit) for bit in bits(name)]
    return result


def after(value, *others):
    return lax.optimization_barrier((value, others))[0]


def local(image_student, caption_student, image_teacher, caption_teacher):
    ilo, chi, core, ihi, clo = (lax.axis_size(a) for a in ROW_AXES + COL_AXES)
    rows, width = image_student.shape
    depth = image_teacher.shape[1]
    assert rows <= LANES and core == 2 and chi > 1 and clo > 1
    n_img, n_cap = ilo * chi, core * ihi * clo
    total, columns = n_img * rows, n_cap * rows
    f32, bf16 = jnp.float32, jnp.bfloat16
    shape = jax.ShapeDtypeStruct
    dma = pltpu.SemaphoreType.DMA

    aligned = rows % 16 == 0
    if aligned:
        image, caption = call(
            pack_kernel,
            [shape((rows, width + depth), bf16)] * 2,
            [image_student, image_teacher, caption_student, caption_teacher],
            scratch=[dma((4,))],
            in_hbm=4,
        )
    else:
        image = jnp.concatenate([image_student, image_teacher], axis=1)
        caption = jnp.concatenate([caption_student, caption_teacher], axis=1)

    def assemble(parts):
        if not aligned:
            return jnp.concatenate(parts, axis=0)
        return call(assemble_kernel, [shape((len(parts) * rows, width + depth), bf16)], parts)[0]

    def gather(own, far_axis, near_axis):
        near = {m: swap(own, near_axis, m) for m in range(1, lax.axis_size(near_axis))}
        far = [swap(own, far_axis, m) for m in range(1, lax.axis_size(far_axis))]
        return [own] + far + [p for m in near for p in [near[m]] + [swap(part, near_axis, m) for part in far]]

    img, cap = gather(image, "chi", "ilo"), gather(caption, "clo", "ihi")
    cap = [assemble([after(cap[0], *img[1 : chi + 1])] + cap[1:-1]), cap[-1]]
    cap = cap + [swap(part, "core", 1) for part in cap]
    if not aligned:
        img, cap = [assemble(img)], [assemble(cap)]

    row_shape, col_shape = shape((n_img, 8, LANES), f32), shape((n_cap, 8, LANES), f32)
    student, teacher, row_stats, col_stats, images = call(
        functools.partial(logits_kernel, len(img), rows, width),
        [shape((total, columns), f32)] * 2 + [row_shape, col_shape, shape((total, width), bf16)],
        img + cap,
        2 * total * columns * (width + depth),
    )

    stats = [row_stats, col_stats]
    steps = [steps_of(ROW_STEPS, ROW_AXES), steps_of(COL_STEPS, COL_AXES)]
    count = max(map(len, steps))
    for k in range(count):
        active = [d for d in range(2) if k < len(steps[d])]
        arrived = {d: swap(stats[d], steps[d][k][0], steps[d][k][1]) for d in active}
        if k == count - 1:
            break
        results = call(
            functools.partial(merge_kernel, [steps[d][k][2] for d in active]),
            [shape(stats[d].shape, f32) for d in active],
            [block for d in active for block in (stats[d], arrived[d])],
        )
        for d, result in zip(active, results):
            stats[d] = result

    images_other = swap(after(images, stats[1]), "core", 1)
    tile, tile_send = call(
        functools.partial(tile_kernel, [steps[d][k][2] if d in active else None for d in range(2)], rows),
        [shape((total, columns), bf16), shape((total, columns // 2), bf16)],
        [student, teacher] + [b for d in range(2) for b in ([stats[d], arrived[d]] if d in active else [stats[d]])],
        10 * total * columns,
    )
    tile_other = swap(tile_send, "core", 1)

    def outs_of(count, near, far):
        piece = count // (near * far)
        return [shape((piece, width), f32)] * far + [shape((piece, width), bf16)] * ((near - 1) * far)

    image_parts = call(
        functools.partial(image_kernel, width),
        outs_of(total, ilo, chi),
        [tile] + cap,
        2 * total * columns * width,
    )
    caption_parts = call(
        caption_kernel,
        outs_of(columns // 2, ihi, clo),
        [tile, tile_other, images, images_other],
        2 * total * columns * width,
    )

    def hop(parts, near, far, f, *gate):
        size = lax.axis_size(far)
        sent = [(m, parts[m * size + f]) for m in range(1, lax.axis_size(near))]
        return [parts[f]] + [swap(after(term, *gate) if gate else term, near, m) for m, term in sent]

    def rounded(terms):
        total = terms[0]
        for term in terms[1:]:
            total = total + term.astype(f32)
        return total.astype(bf16)

    image_far = [rounded(hop(image_parts, "ilo", "chi", f)) for f in range(1, chi)]
    caption_far = [rounded(hop(caption_parts, "ihi", "clo", f)) for f in range(1, clo)]
    image_terms = hop(image_parts, "ilo", "chi", 0, image_far[0], caption_far[0])
    caption_terms = hop(caption_parts, "ihi", "clo", 0, image_far[0], caption_far[0])
    image_terms += [swap(image_far[f - 1], "chi", f) for f in range(1, chi)]
    caption_terms += [swap(caption_far[f - 1], "clo", f) for f in range(1, clo)]
    out = shape((rows, width), f32)
    return tuple(
        call(
            functools.partial(sum_kernel, (len(image_terms), len(caption_terms))),
            [out, out],
            image_terms + caption_terms,
            scratch=[pltpu.VMEM((rows, width), f32)] * 2 + [dma((2,))],
            out_space=HBM,
        )
    )


def split(count):
    low = 1 << ((count.bit_length() - 1) // 2)
    return count // low, low


def solution(mesh):
    ihi, ilo = split(mesh.shape["img"] // 2)
    chi, clo = split(mesh.shape["cap"])
    fine = Mesh(mesh.devices.reshape(ihi, ilo, 2, chi, clo), ("ihi", "ilo", "core", "chi", "clo"))
    by_image = P(("ihi", "ilo", "core", "chi", "clo"), None)
    by_caption = P(("chi", "clo", "ihi", "ilo", "core"), None)
    return jax.shard_map(
        local,
        mesh=fine,
        in_specs=(by_image, by_caption, by_image, by_caption),
        out_specs=(by_image, by_caption),
        check_vma=False,
    )
```

```python
import functools
import math

import jax
import jax.numpy as jnp
from jax import lax
from jax.experimental import pallas as pl
from jax.experimental.pallas import tpu as pltpu
from jax.sharding import Mesh, PartitionSpec as P

logit_gain = 3.0
ROW_AXES = ("ilo", "chi")
COL_AXES = ("core", "ihi", "clo")
ROW_STAGES = (("ilo",), ("chi",))
COL_STAGES = (("ihi", "clo"), ("core",))
ROW_ORDER = ("ihi", "ilo", "core", "chi", "clo")
COL_ORDER = ("chi", "clo", "ihi", "ilo", "core")
LANES = 128
PEAK_S, TOTAL_S, PEAK_T, TOTAL_T, INDEX = range(5)


def swap(value, axis, mask):
    size = lax.axis_size(axis)
    return lax.ppermute(value, axis, [(j, j ^ mask) for j in range(size)])


def partners(names, axes):
    sizes = [lax.axis_size(a) for a in names]
    strides = [math.prod(lax.axis_size(a) for a in axes[axes.index(name) + 1 :]) for name in names]
    result = []
    for mask in range(1, math.prod(sizes)):
        distance, rest = 0, mask
        for size, stride in zip(reversed(sizes), reversed(strides)):
            distance += rest % size * stride
            rest //= size
        result.append((mask, distance))
    return result


def lines_of(columns):
    count = columns[0].shape[0]
    lane = lax.broadcasted_iota(jnp.int32, (count, LANES), 1)
    wide = jnp.zeros((count, LANES), jnp.float32)
    for k, column in enumerate(columns):
        wide = jnp.where(lane == k, column, wide)
    spare = -count % LANES
    if spare:
        wide = jnp.concatenate([wide, jnp.zeros((spare, LANES), jnp.float32)], axis=0)
    return wide.T[:8, :count]


def columns_of(lines):
    count = lines.shape[1]
    spare = -count % LANES
    if spare:
        lines = jnp.concatenate([lines, jnp.zeros((8, spare), jnp.float32)], axis=1)
    tall = jnp.concatenate([lines, jnp.zeros((LANES - 8, count + spare), jnp.float32)], axis=0)
    return tall.T[:count]


def load_slots(blocks, rows):
    return jnp.concatenate([block[:, :rows] for block in blocks], axis=1)


def owners(axes, order):
    sizes = [lax.axis_size(a) for a in axes]
    result = []
    for s in range(math.prod(sizes)):
        place = {a: lax.axis_index(a) for a in order}
        for axis, size in zip(reversed(axes), reversed(sizes)):
            place[axis] = place[axis] ^ (s % size)
            s //= size
        owner = 0
        for axis in order:
            owner = owner * lax.axis_size(axis) + place[axis]
        result.append(owner)
    return result


def joined(refs, columns=slice(None)):
    values = [ref[:, columns] for ref in refs]
    return values[0] if len(values) == 1 else jnp.concatenate(values, axis=0)


def copy_all(pairs, sems):
    copies = [pltpu.make_async_copy(src, dst, sems.at[k]) for k, (src, dst) in enumerate(pairs)]
    for copy in copies:
        copy.start()
    for copy in copies:
        copy.wait()


def pack_kernel(image_s, image_t, caption_s, caption_t, image, caption, sems):
    width = image_s.shape[1]
    copy_all(
        [
            (image_s, image.at[:, :width]),
            (image_t, image.at[:, width:]),
            (caption_s, caption.at[:, :width]),
            (caption_t, caption.at[:, width:]),
        ],
        sems,
    )


def duplicate_kernel(image, caption, image_out, caption_out):
    image_out[...] = image[...]
    caption_out[...] = caption[...]


def assemble_kernel(*refs):
    refs[-1][...] = joined(refs[:-1])


def logits(left, right, out):
    gain = logit_gain / math.sqrt(left.shape[1])
    out[...] = gain * lax.dot_general(left, right, (((1,), (1,)), ((), ())), preferred_element_type=jnp.float32)
    matrix = out[...]
    peak = jnp.max(matrix, axis=1, keepdims=True)
    columns = [peak, jnp.sum(jnp.exp(matrix - peak), axis=1, keepdims=True)]
    peak = jnp.max(matrix, axis=0, keepdims=True)
    return columns, [peak, jnp.sum(jnp.exp(matrix - peak), axis=0, keepdims=True)]


def logits_kernel(n_img, rows, width, *refs):
    img_parts, cap_parts = refs[:n_img], refs[n_img:-5]
    student_ref, teacher_ref, row_ref, col_ref, images = refs[-5:]
    columns, lines = [], []
    for part, out in ((slice(0, width), student_ref), (slice(width, None), teacher_ref)):
        left = joined(img_parts, part)
        if out is student_ref:
            images[...] = left
        more = logits(left, joined(cap_parts, part), out)
        columns, lines = columns + more[0], lines + more[1]
    lines.append(jnp.zeros((4, lines[0].shape[1]), jnp.float32))
    row = lax.broadcasted_iota(jnp.int32, (8, LANES), 0)
    lane = lax.broadcasted_iota(jnp.int32, (8, LANES), 1)
    for ref, values, axes, order in (
        (row_ref, lines_of(columns), ROW_AXES, ROW_ORDER),
        (col_ref, jnp.concatenate(lines, axis=0), COL_AXES, COL_ORDER),
    ):
        for s, owner in enumerate(owners(axes, order)):
            ref[s] = jnp.zeros((8, LANES), jnp.float32)
            ref[s, :, :rows] = values[:, s * rows : (s + 1) * rows]
            index = (owner * rows + lane).astype(jnp.float32)
            ref[s] = jnp.where(row == INDEX, index, ref[s])


def merged(x, y):
    line = lax.broadcasted_iota(jnp.int32, x.shape, 0)
    student = line <= TOTAL_S
    x_peak = jnp.where(student, x[PEAK_S : PEAK_S + 1], x[PEAK_T : PEAK_T + 1])
    y_peak = jnp.where(student, y[PEAK_S : PEAK_S + 1], y[PEAK_T : PEAK_T + 1])
    peak = jnp.maximum(x_peak, y_peak)
    total = x * jnp.exp(x_peak - peak) + y * jnp.exp(y_peak - peak)
    both = jnp.where((line == PEAK_S) | (line == PEAK_T), peak, total)
    return jnp.where(line < INDEX, both, x)


def merged_blocks(mine, others, distances):
    blocks = [mine[s] for s in range(mine.shape[0])]
    for other, distance in zip(others, distances):
        blocks = [merged(block, other[s ^ distance]) for s, block in enumerate(blocks)]
    return blocks


def take(refs, plan):
    result = []
    for distances in plan:
        mine, others = refs[0], refs[1 : 1 + len(distances)]
        del refs[: 1 + len(distances)]
        result.append(merged_blocks(mine, others, distances))
    return result


def merge_kernel(plan, *refs):
    refs = list(refs)
    results = take(refs, plan)
    for out, blocks in zip(refs, results):
        for s, block in enumerate(blocks):
            out[s] = block


def tile_kernel(plan, rows, student_ref, teacher_ref, *refs):
    refs = list(refs)
    blocks = take(refs, plan)
    tile_ref, send_ref = refs
    total, count = teacher_ref.shape

    def finish(blocks):
        lines = load_slots(blocks, rows)
        line = lax.broadcasted_iota(jnp.int32, lines.shape, 0)
        lse_s = lines[PEAK_S : PEAK_S + 1] + jnp.log(lines[TOTAL_S : TOTAL_S + 1])
        lse_t = lines[PEAK_T : PEAK_T + 1] + jnp.log(lines[TOTAL_T : TOTAL_T + 1])
        return jnp.where(line == 0, lse_s, jnp.where(line == 1, lse_t, lines))

    down, across = columns_of(finish(blocks[0])), finish(blocks[1])
    step = 64 if total % 64 == 0 else total
    for r in range(0, total, step):
        at = slice(r, r + step)
        s, t = student_ref[at], teacher_ref[at]
        grad = 0.5 * (jnp.exp(s - down[at, 0:1]) + jnp.exp(s - across[0:1]))
        grad = grad - 0.25 * (jnp.exp(t - down[at, 1:2]) + jnp.exp(t - across[1:2]))
        grad = grad - jnp.where(down[at, INDEX : INDEX + 1] == across[INDEX : INDEX + 1], 0.5, 0.0)
        tile_ref[at] = grad.astype(jnp.bfloat16)
    send_ref[...] = tile_ref[:, count // 2 :]


def spread(part, outs):
    start = 0
    for out in outs:
        out[...] = part[start : start + out.shape[0]].astype(out.dtype)
        start += out.shape[0]


def image_kernel(width, tile_ref, *refs):
    parts = [ref for ref in refs if ref.dtype == jnp.bfloat16 and ref.shape[1] > width]
    right = joined(parts, slice(0, width))
    spread(jnp.dot(tile_ref[...], right, preferred_element_type=jnp.float32), refs[len(parts) :])


def caption_kernel(tile_ref, tile_other, images, images_other, *outs):
    half = tile_other.shape[1]
    part = 0.0
    for tile, rows in ((tile_ref[:, :half], images[...]), (tile_other[...], images_other[...])):
        part = part + lax.dot_general(tile, rows, (((0,), (0,)), ((), ())), preferred_element_type=jnp.float32)
    spread(part, outs)


def sum_kernel(counts, *refs):
    refs = list(refs)
    terms = [[refs.pop(0) for _ in range(count)] for count in counts]
    outs, held, sems = refs[: len(counts)], refs[len(counts) : -1], refs[-1]
    copies = []
    for k, (group, out, here) in enumerate(zip(terms, outs, held)):
        total = group[0][...]
        for term in group[1:]:
            total = total + term[...].astype(jnp.float32)
        here[...] = total
        copies.append(pltpu.make_async_copy(here, out, sems.at[k]))
        copies[-1].start()
    for copy in copies:
        copy.wait()


VMEM, HBM = pltpu.VMEM, pltpu.HBM


def call(kernel, outs, args, flops=0, scratch=(), in_hbm=0, out_space=VMEM):
    moved = sum(math.prod(a.shape) * a.dtype.itemsize for a in list(args) + list(outs))
    spaces = [HBM] * in_hbm + [VMEM] * (len(args) - in_hbm)
    return pl.pallas_call(
        kernel,
        out_shape=[out_space(out.shape, out.dtype) for out in outs],
        in_specs=[pl.BlockSpec(memory_space=space) for space in spaces],
        out_specs=[pl.BlockSpec(memory_space=out_space)] * len(outs),
        scratch_shapes=scratch,
        compiler_params=pltpu.CompilerParams(vmem_limit_bytes=16 * 2**20),
        cost_estimate=pl.CostEstimate(flops=flops, bytes_accessed=moved, transcendentals=0),
    )(*(pltpu.with_memory_space_constraint(arg, space) for arg, space in zip(args, spaces)))


def after(value, *others):
    return lax.optimization_barrier((value, others))[0]


def local(image_student, caption_student, image_teacher, caption_teacher):
    ilo, chi, core, ihi, clo = (lax.axis_size(a) for a in ROW_AXES + COL_AXES)
    rows, width = image_student.shape
    depth = image_teacher.shape[1]
    assert rows <= LANES and core == 2 and chi > 1 and clo > 1
    n_img, n_cap = ilo * chi, core * ihi * clo
    total, columns = n_img * rows, n_cap * rows
    f32, bf16 = jnp.float32, jnp.bfloat16
    shape = jax.ShapeDtypeStruct
    dma = pltpu.SemaphoreType.DMA

    aligned = rows % 16 == 0
    if aligned:
        image, caption = call(
            pack_kernel,
            [shape((rows, width + depth), bf16)] * 2,
            [image_student, image_teacher, caption_student, caption_teacher],
            scratch=[dma((4,))],
            in_hbm=4,
        )
    else:
        image = jnp.concatenate([image_student, image_teacher], axis=1)
        caption = jnp.concatenate([caption_student, caption_teacher], axis=1)

    def assemble(parts):
        if not aligned:
            return jnp.concatenate(parts, axis=0)
        return call(assemble_kernel, [shape((len(parts) * rows, width + depth), bf16)], parts)[0]

    if aligned:
        image_near, caption_near = call(
            duplicate_kernel, [shape((rows, width + depth), bf16)] * 2, [image, caption]
        )
    else:
        image_near, caption_near = image, caption

    def gather(own, own_near, far_axis, near_axis):
        far = [swap(own, far_axis, m) for m in range(1, lax.axis_size(far_axis))]
        parts = [own] + far
        for m in range(1, lax.axis_size(near_axis)):
            parts += [swap(part, near_axis, m) for part in [own_near] + far]
        return parts

    img, cap = gather(image, image_near, "chi", "ilo"), gather(caption, caption_near, "clo", "ihi")
    cap = [assemble([after(cap[0], *img[1 : chi + 1])] + cap[1:-1]), cap[-1]]
    cap = cap + [swap(part, "core", 1) for part in cap]
    if not aligned:
        img, cap = [assemble(img)], [assemble(cap)]

    row_shape, col_shape = shape((n_img, 8, LANES), f32), shape((n_cap, 8, LANES), f32)
    student, teacher, row_stats, col_stats, images = call(
        functools.partial(logits_kernel, len(img), rows, width),
        [shape((total, columns), f32)] * 2 + [row_shape, col_shape, shape((total, width), bf16)],
        img + cap,
        2 * total * columns * (width + depth),
    )

    images_other = swap(images, "core", 1)
    stats = [row_stats, col_stats]
    for row_names, col_names in zip(ROW_STAGES, COL_STAGES):
        plan, blocks = [], []
        for block, names, axes in zip(stats, (row_names, col_names), (ROW_AXES, COL_AXES)):
            others = partners(names, axes)
            plan.append([distance for _, distance in others])
            blocks += [block] + [swap(block, names, mask) for mask, _ in others]
        if row_names != ROW_STAGES[-1]:
            blocks[0] = after(blocks[0], images_other)
            stats = call(functools.partial(merge_kernel, plan), [row_shape, col_shape], blocks)

    tile, tile_send = call(
        functools.partial(tile_kernel, plan, rows),
        [shape((total, columns), bf16), shape((total, columns // 2), bf16)],
        [student, teacher] + blocks,
        10 * total * columns,
    )
    tile_other = swap(tile_send, "core", 1)

    def outs_of(count, near, far):
        piece = count // (near * far)
        return [shape((piece, width), f32)] * far + [shape((piece, width), bf16)] * ((near - 1) * far)

    image_parts = call(
        functools.partial(image_kernel, width),
        outs_of(total, ilo, chi),
        [tile] + cap,
        2 * total * columns * width,
    )
    caption_parts = call(
        caption_kernel,
        outs_of(columns // 2, ihi, clo),
        [tile, tile_other, images, images_other],
        2 * total * columns * width,
    )

    def hop(parts, near, far, f, *gate):
        size = lax.axis_size(far)
        sent = [(m, parts[m * size + f]) for m in range(1, lax.axis_size(near))]
        return [parts[f]] + [swap(after(term, *gate) if gate else term, near, m) for m, term in sent]

    def rounded(terms):
        total = terms[0]
        for term in terms[1:]:
            total = total + term.astype(f32)
        return total.astype(bf16)

    image_far = [rounded(hop(image_parts, "ilo", "chi", f)) for f in range(1, chi)]
    caption_far = [rounded(hop(caption_parts, "ihi", "clo", f)) for f in range(1, clo)]
    image_terms = hop(image_parts, "ilo", "chi", 0, image_far[0], caption_far[0])
    caption_terms = hop(caption_parts, "ihi", "clo", 0, image_far[0], caption_far[0])
    image_terms += [swap(image_far[f - 1], "chi", f) for f in range(1, chi)]
    caption_terms += [swap(caption_far[f - 1], "clo", f) for f in range(1, clo)]
    out = shape((rows, width), f32)
    return tuple(
        call(
            functools.partial(sum_kernel, (len(image_terms), len(caption_terms))),
            [out, out],
            image_terms + caption_terms,
            scratch=[pltpu.VMEM((rows, width), f32)] * 2 + [dma((2,))],
            out_space=HBM,
        )
    )


def split(count):
    low = 1 << ((count.bit_length() - 1) // 2)
    return count // low, low


def solution(mesh):
    ihi, ilo = split(mesh.shape["img"] // 2)
    chi, clo = split(mesh.shape["cap"])
    fine = Mesh(mesh.devices.reshape(ihi, ilo, 2, chi, clo), ("ihi", "ilo", "core", "chi", "clo"))
    by_image = P(("ihi", "ilo", "core", "chi", "clo"), None)
    by_caption = P(("chi", "clo", "ihi", "ilo", "core"), None)
    return jax.shard_map(
        local,
        mesh=fine,
        in_specs=(by_image, by_caption, by_image, by_caption),
        out_specs=(by_image, by_caption),
        check_vma=False,
    )
```

```python
import functools
import math

import jax
import jax.numpy as jnp
from jax import lax
from jax.experimental import pallas as pl
from jax.experimental.pallas import tpu as pltpu
from jax.sharding import Mesh, PartitionSpec as P

logit_gain = 3.0
ROW_AXES = ("ilo", "chi")
COL_AXES = ("core", "ihi", "clo")
ROW_STAGES = (("ilo",), ("chi",))
COL_STAGES = (("ihi", "clo"), ("core",))
ROW_ORDER = ("ihi", "ilo", "core", "chi", "clo")
COL_ORDER = ("chi", "clo", "ihi", "ilo", "core")
LANES = 128
PEAK_S, TOTAL_S, PEAK_T, TOTAL_T, INDEX = range(5)


def swap(value, axis, mask):
    size = lax.axis_size(axis)
    return lax.ppermute(value, axis, [(j, j ^ mask) for j in range(size)])


def partners(names, axes):
    sizes = [lax.axis_size(a) for a in names]
    strides = [math.prod(lax.axis_size(a) for a in axes[axes.index(name) + 1 :]) for name in names]
    result = []
    for mask in range(1, math.prod(sizes)):
        distance, rest = 0, mask
        for size, stride in zip(reversed(sizes), reversed(strides)):
            distance += rest % size * stride
            rest //= size
        result.append((mask, distance))
    return result


def lines_of(columns):
    count = columns[0].shape[0]
    lane = lax.broadcasted_iota(jnp.int32, (count, LANES), 1)
    wide = jnp.zeros((count, LANES), jnp.float32)
    for k, column in enumerate(columns):
        wide = jnp.where(lane == k, column, wide)
    spare = -count % LANES
    if spare:
        wide = jnp.concatenate([wide, jnp.zeros((spare, LANES), jnp.float32)], axis=0)
    return wide.T[:8, :count]


def columns_of(lines):
    count = lines.shape[1]
    spare = -count % LANES
    if spare:
        lines = jnp.concatenate([lines, jnp.zeros((8, spare), jnp.float32)], axis=1)
    tall = jnp.concatenate([lines, jnp.zeros((LANES - 8, count + spare), jnp.float32)], axis=0)
    return tall.T[:count]


def load_slots(blocks, rows):
    return jnp.concatenate([block[:, :rows] for block in blocks], axis=1)


def owners(axes, order):
    sizes = [lax.axis_size(a) for a in axes]
    result = []
    for s in range(math.prod(sizes)):
        place = {a: lax.axis_index(a) for a in order}
        for axis, size in zip(reversed(axes), reversed(sizes)):
            place[axis] = place[axis] ^ (s % size)
            s //= size
        owner = 0
        for axis in order:
            owner = owner * lax.axis_size(axis) + place[axis]
        result.append(owner)
    return result


def joined(refs, columns=slice(None)):
    values = [ref[:, columns] for ref in refs]
    return values[0] if len(values) == 1 else jnp.concatenate(values, axis=0)


def copy_all(pairs, sems):
    copies = [pltpu.make_async_copy(src, dst, sems.at[k]) for k, (src, dst) in enumerate(pairs)]
    for copy in copies:
        copy.start()
    for copy in copies:
        copy.wait()


def pack_kernel(image_s, image_t, caption_s, caption_t, image, caption, sems):
    width = image_s.shape[1]
    copy_all(
        [
            (image_s, image.at[:, :width]),
            (image_t, image.at[:, width:]),
            (caption_s, caption.at[:, :width]),
            (caption_t, caption.at[:, width:]),
        ],
        sems,
    )


def duplicate_kernel(*refs):
    count = len(refs) // 2
    for value, out in zip(refs[:count], refs[count:]):
        out[...] = value[...]


def assemble_kernel(*refs):
    refs[-1][...] = joined(refs[:-1])


def logits(left, right, out):
    gain = logit_gain / math.sqrt(left.shape[1])
    out[...] = gain * lax.dot_general(left, right, (((1,), (1,)), ((), ())), preferred_element_type=jnp.float32)
    matrix = out[...]
    peak = jnp.max(matrix, axis=1, keepdims=True)
    columns = [peak, jnp.sum(jnp.exp(matrix - peak), axis=1, keepdims=True)]
    peak = jnp.max(matrix, axis=0, keepdims=True)
    return columns, [peak, jnp.sum(jnp.exp(matrix - peak), axis=0, keepdims=True)]


def logits_kernel(n_img, rows, width, *refs):
    img_parts, cap_parts = refs[:n_img], refs[n_img:-5]
    student_ref, teacher_ref, row_ref, col_ref, images = refs[-5:]
    columns, lines = [], []
    for part, out in ((slice(0, width), student_ref), (slice(width, None), teacher_ref)):
        left = joined(img_parts, part)
        if out is student_ref:
            images[...] = left
        more = logits(left, joined(cap_parts, part), out)
        columns, lines = columns + more[0], lines + more[1]
    lines.append(jnp.zeros((4, lines[0].shape[1]), jnp.float32))
    row = lax.broadcasted_iota(jnp.int32, (8, LANES), 0)
    lane = lax.broadcasted_iota(jnp.int32, (8, LANES), 1)
    for ref, values, axes, order in (
        (row_ref, lines_of(columns), ROW_AXES, ROW_ORDER),
        (col_ref, jnp.concatenate(lines, axis=0), COL_AXES, COL_ORDER),
    ):
        for s, owner in enumerate(owners(axes, order)):
            ref[s] = jnp.zeros((8, LANES), jnp.float32)
            ref[s, :, :rows] = values[:, s * rows : (s + 1) * rows]
            index = (owner * rows + lane).astype(jnp.float32)
            ref[s] = jnp.where(row == INDEX, index, ref[s])


def merged(x, y):
    line = lax.broadcasted_iota(jnp.int32, x.shape, 0)
    student = line <= TOTAL_S
    x_peak = jnp.where(student, x[PEAK_S : PEAK_S + 1], x[PEAK_T : PEAK_T + 1])
    y_peak = jnp.where(student, y[PEAK_S : PEAK_S + 1], y[PEAK_T : PEAK_T + 1])
    peak = jnp.maximum(x_peak, y_peak)
    total = x * jnp.exp(x_peak - peak) + y * jnp.exp(y_peak - peak)
    both = jnp.where((line == PEAK_S) | (line == PEAK_T), peak, total)
    return jnp.where(line < INDEX, both, x)


def merged_blocks(mine, others, distances):
    blocks = [mine[s] for s in range(mine.shape[0])]
    for other, distance in zip(others, distances):
        blocks = [merged(block, other[s ^ distance]) for s, block in enumerate(blocks)]
    return blocks


def take(refs, plan):
    result = []
    for distances in plan:
        mine, others = refs[0], refs[1 : 1 + len(distances)]
        del refs[: 1 + len(distances)]
        result.append(merged_blocks(mine, others, distances))
    return result


def merge_kernel(plan, *refs):
    refs = list(refs)
    results = take(refs, plan)
    for out, blocks in zip(refs, results):
        for s, block in enumerate(blocks):
            out[s] = block


def tile_kernel(plan, n_cap, rows, width, student_ref, teacher_ref, *refs):
    refs = list(refs)
    blocks = take(refs, plan)
    captions = [refs.pop(0) for _ in range(n_cap)]
    tile_ref, send_ref, first_ref = refs
    total, count = teacher_ref.shape

    def finish(blocks):
        lines = load_slots(blocks, rows)
        line = lax.broadcasted_iota(jnp.int32, lines.shape, 0)
        lse_s = lines[PEAK_S : PEAK_S + 1] + jnp.log(lines[TOTAL_S : TOTAL_S + 1])
        lse_t = lines[PEAK_T : PEAK_T + 1] + jnp.log(lines[TOTAL_T : TOTAL_T + 1])
        return jnp.where(line == 0, lse_s, jnp.where(line == 1, lse_t, lines))

    down, across = columns_of(finish(blocks[0])), finish(blocks[1])
    step = 64 if total % 64 == 0 else total
    for r in range(0, total, step):
        at = slice(r, r + step)
        s, t = student_ref[at], teacher_ref[at]
        grad = 0.5 * (jnp.exp(s - down[at, 0:1]) + jnp.exp(s - across[0:1]))
        grad = grad - 0.25 * (jnp.exp(t - down[at, 1:2]) + jnp.exp(t - across[1:2]))
        grad = grad - jnp.where(down[at, INDEX : INDEX + 1] == across[INDEX : INDEX + 1], 0.5, 0.0)
        tile_ref[at] = grad.astype(jnp.bfloat16)
    send_ref[...] = tile_ref[:, count // 2 :]
    right = joined(captions, slice(0, width))
    part = jnp.dot(tile_ref[total - first_ref.shape[0] :], right, preferred_element_type=jnp.float32)
    first_ref[...] = part.astype(jnp.bfloat16)


def spread(part, outs):
    start = 0
    for out in outs:
        out[...] = part[start : start + out.shape[0]].astype(out.dtype)
        start += out.shape[0]


def image_kernel(width, tile_ref, *refs):
    parts = [ref for ref in refs if ref.dtype == jnp.bfloat16 and ref.shape[1] > width]
    right = joined(parts, slice(0, width))
    outs = refs[len(parts) :]
    count = sum(out.shape[0] for out in outs)
    spread(jnp.dot(tile_ref[:count], right, preferred_element_type=jnp.float32), outs)


def caption_kernel(tile_ref, tile_other, images, images_other, *outs):
    half = tile_other.shape[1]
    part = 0.0
    for tile, rows in ((tile_ref[:, :half], images[...]), (tile_other[...], images_other[...])):
        part = part + lax.dot_general(tile, rows, (((0,), (0,)), ((), ())), preferred_element_type=jnp.float32)
    spread(part, outs)


def sum_kernel(counts, *refs):
    refs = list(refs)
    terms = [[refs.pop(0) for _ in range(count)] for count in counts]
    outs, held, sems = refs[: len(counts)], refs[len(counts) : -1], refs[-1]
    copies = []
    for k, (group, out, here) in enumerate(zip(terms, outs, held)):
        total = group[0][...]
        for term in group[1:]:
            total = total + term[...].astype(jnp.float32)
        here[...] = total
        copies.append(pltpu.make_async_copy(here, out, sems.at[k]))
        copies[-1].start()
    for copy in copies:
        copy.wait()


VMEM, HBM = pltpu.VMEM, pltpu.HBM


def call(kernel, outs, args, flops=0, scratch=(), in_hbm=0, out_space=VMEM):
    moved = sum(math.prod(a.shape) * a.dtype.itemsize for a in list(args) + list(outs))
    spaces = [HBM] * in_hbm + [VMEM] * (len(args) - in_hbm)
    return pl.pallas_call(
        kernel,
        out_shape=[out_space(out.shape, out.dtype) for out in outs],
        in_specs=[pl.BlockSpec(memory_space=space) for space in spaces],
        out_specs=[pl.BlockSpec(memory_space=out_space)] * len(outs),
        scratch_shapes=scratch,
        compiler_params=pltpu.CompilerParams(vmem_limit_bytes=16 * 2**20),
        cost_estimate=pl.CostEstimate(flops=flops, bytes_accessed=moved, transcendentals=0),
    )(*(pltpu.with_memory_space_constraint(arg, space) for arg, space in zip(args, spaces)))


def after(value, *others):
    return lax.optimization_barrier((value, others))[0]


def local(image_student, caption_student, image_teacher, caption_teacher):
    ilo, chi, core, ihi, clo = (lax.axis_size(a) for a in ROW_AXES + COL_AXES)
    rows, width = image_student.shape
    depth = image_teacher.shape[1]
    assert rows <= LANES and core == 2 and chi > 1 and clo > 1
    n_img, n_cap = ilo * chi, core * ihi * clo
    total, columns = n_img * rows, n_cap * rows
    f32, bf16 = jnp.float32, jnp.bfloat16
    shape = jax.ShapeDtypeStruct
    dma = pltpu.SemaphoreType.DMA

    aligned = rows % 16 == 0
    if aligned:
        image, caption = call(
            pack_kernel,
            [shape((rows, width + depth), bf16)] * 2,
            [image_student, image_teacher, caption_student, caption_teacher],
            scratch=[dma((4,))],
            in_hbm=4,
        )
    else:
        image = jnp.concatenate([image_student, image_teacher], axis=1)
        caption = jnp.concatenate([caption_student, caption_teacher], axis=1)

    def assemble(parts):
        if not aligned:
            return jnp.concatenate(parts, axis=0)
        return call(assemble_kernel, [shape((len(parts) * rows, width + depth), bf16)], parts)[0]

    if aligned:
        image_near, caption_near = call(
            duplicate_kernel, [shape((rows, width + depth), bf16)] * 2, [image, caption]
        )
    else:
        image_near, caption_near = image, caption

    def gather(own, own_near, far_axis, near_axis):
        far = [swap(own, far_axis, m) for m in range(1, lax.axis_size(far_axis))]
        parts = [own] + far
        for m in range(1, lax.axis_size(near_axis)):
            parts += [swap(part, near_axis, m) for part in [own_near] + far]
        return parts

    img, cap = gather(image, image_near, "chi", "ilo"), gather(caption, caption_near, "clo", "ihi")
    cap = [assemble([after(cap[0], *img[1 : chi + 1])] + cap[1:-1]), cap[-1]]
    cap = cap + [swap(part, "core", 1) for part in cap]
    if not aligned:
        img, cap = [assemble(img)], [assemble(cap)]

    row_shape, col_shape = shape((n_img, 8, LANES), f32), shape((n_cap, 8, LANES), f32)
    student, teacher, row_stats, col_stats, images = call(
        functools.partial(logits_kernel, len(img), rows, width),
        [shape((total, columns), f32)] * 2 + [row_shape, col_shape, shape((total, width), bf16)],
        img + cap,
        2 * total * columns * (width + depth),
    )

    images_other = swap(images, "core", 1)
    stats = [row_stats, col_stats]
    for row_names, col_names in zip(ROW_STAGES, COL_STAGES):
        plan, blocks = [], []
        for block, names, axes in zip(stats, (row_names, col_names), (ROW_AXES, COL_AXES)):
            others = partners(names, axes)
            plan.append([distance for _, distance in others])
            blocks += [block] + [swap(block, names, mask) for mask, _ in others]
        if row_names != ROW_STAGES[-1]:
            blocks[0] = after(blocks[0], images_other)
            stats = call(functools.partial(merge_kernel, plan), [row_shape, col_shape], blocks)

    tile, tile_send, image_first = call(
        functools.partial(tile_kernel, plan, len(cap), rows, width),
        [shape((total, columns), bf16), shape((total, columns // 2), bf16), shape((rows, width), bf16)],
        [student, teacher] + blocks + cap,
        2 * rows * columns * width,
    )
    tile_other = swap(tile_send, "core", 1)

    def outs_of(count, near, far):
        piece = count // (near * far)
        return [shape((piece, width), f32)] * far + [shape((piece, width), bf16)] * ((near - 1) * far)

    image_parts = call(
        functools.partial(image_kernel, width),
        outs_of(total, ilo, chi)[:-1],
        [tile] + cap,
        2 * total * columns * width,
    )
    image_parts = list(image_parts) + [image_first]
    caption_parts = call(
        caption_kernel,
        outs_of(columns // 2, ihi, clo),
        [tile, tile_other, images, images_other],
        2 * total * columns * width,
    )

    def hop(parts, near, far, f):
        size = lax.axis_size(far)
        return [parts[f]] + [swap(parts[m * size + f], near, m) for m in range(1, lax.axis_size(near))]

    def rounded(terms):
        total = terms[0]
        for term in terms[1:]:
            total = total + term.astype(f32)
        return total.astype(bf16)

    image_far = [rounded(hop(image_parts, "ilo", "chi", f)) for f in range(1, chi)]
    caption_far = [rounded(hop(caption_parts, "ihi", "clo", f)) for f in range(1, clo)]
    seconds = [parts[m * far] for parts, near, far in ((image_parts, ilo, chi), (caption_parts, ihi, clo)) for m in range(1, near)]
    image_terms = [image_parts[0]] + [swap(part, "ilo", m) for m, part in enumerate(seconds[: ilo - 1], 1)]
    caption_terms = [caption_parts[0]] + [swap(part, "ihi", m) for m, part in enumerate(seconds[ilo - 1 :], 1)]
    image_terms += [swap(image_far[f - 1], "chi", f) for f in range(1, chi)]
    caption_terms += [swap(caption_far[f - 1], "clo", f) for f in range(1, clo)]
    out = shape((rows, width), f32)
    caption_grad, image_grad = call(
        functools.partial(sum_kernel, (len(caption_terms), len(image_terms))),
        [out, out],
        caption_terms + image_terms,
        scratch=[pltpu.VMEM((rows, width), f32)] * 2 + [dma((2,))],
        out_space=HBM,
    )
    return (image_grad, caption_grad)


def split(count):
    low = 1 << ((count.bit_length() - 1) // 2)
    return count // low, low


def solution(mesh):
    ihi, ilo = split(mesh.shape["img"] // 2)
    chi, clo = split(mesh.shape["cap"])
    fine = Mesh(mesh.devices.reshape(ihi, ilo, 2, chi, clo), ("ihi", "ilo", "core", "chi", "clo"))
    by_image = P(("ihi", "ilo", "core", "chi", "clo"), None)
    by_caption = P(("chi", "clo", "ihi", "ilo", "core"), None)
    return jax.shard_map(
        local,
        mesh=fine,
        in_specs=(by_image, by_caption, by_image, by_caption),
        out_specs=(by_image, by_caption),
        check_vma=False,
    )
```

```python
import functools
import math

import jax
import jax.numpy as jnp
from jax import lax
from jax.experimental import pallas as pl
from jax.experimental.pallas import tpu as pltpu
from jax.sharding import Mesh, PartitionSpec as P

logit_gain = 3.0
ROW_AXES = ("ilo", "chi")
COL_AXES = ("core", "clo", "ihi")
ROW_STAGES = (("ilo",), ("chi",))
COL_STAGES = (("ihi", "clo"), ("core",))
ROW_ORDER = ("ihi", "ilo", "core", "chi", "clo")
COL_ORDER = ("chi", "clo", "ihi", "ilo", "core")
LANES = 128
PEAK_S, TOTAL_S, PEAK_T, TOTAL_T, INDEX = range(5)


def swap(value, axis, mask):
    size = lax.axis_size(axis)
    return lax.ppermute(value, axis, [(j, j ^ mask) for j in range(size)])


def partners(names, axes):
    sizes = [lax.axis_size(a) for a in names]
    strides = [math.prod(lax.axis_size(a) for a in axes[axes.index(name) + 1 :]) for name in names]
    result = []
    for mask in range(1, math.prod(sizes)):
        distance, rest = 0, mask
        for size, stride in zip(reversed(sizes), reversed(strides)):
            distance += rest % size * stride
            rest //= size
        result.append((mask, distance))
    return result


def lines_of(columns):
    count = columns[0].shape[0]
    lane = lax.broadcasted_iota(jnp.int32, (count, LANES), 1)
    wide = jnp.zeros((count, LANES), jnp.float32)
    for k, column in enumerate(columns):
        wide = jnp.where(lane == k, column, wide)
    spare = -count % LANES
    if spare:
        wide = jnp.concatenate([wide, jnp.zeros((spare, LANES), jnp.float32)], axis=0)
    return wide.T[:8, :count]


def columns_of(lines):
    count = lines.shape[1]
    spare = -count % LANES
    if spare:
        lines = jnp.concatenate([lines, jnp.zeros((8, spare), jnp.float32)], axis=1)
    tall = jnp.concatenate([lines, jnp.zeros((LANES - 8, count + spare), jnp.float32)], axis=0)
    return tall.T[:count]


def load_slots(blocks, rows):
    return jnp.concatenate([block[:, :rows] for block in blocks], axis=1)


def owners(axes, order):
    sizes = [lax.axis_size(a) for a in axes]
    result = []
    for s in range(math.prod(sizes)):
        place = {a: lax.axis_index(a) for a in order}
        for axis, size in zip(reversed(axes), reversed(sizes)):
            place[axis] = place[axis] ^ (s % size)
            s //= size
        owner = 0
        for axis in order:
            owner = owner * lax.axis_size(axis) + place[axis]
        result.append(owner)
    return result


def joined(refs, columns=slice(None)):
    values = [ref[:, columns] for ref in refs]
    return values[0] if len(values) == 1 else jnp.concatenate(values, axis=0)


def copy_all(pairs, sems):
    copies = [pltpu.make_async_copy(src, dst, sems.at[k]) for k, (src, dst) in enumerate(pairs)]
    for copy in copies:
        copy.start()
    for copy in copies:
        copy.wait()


def pack_kernel(image_s, image_t, caption_s, caption_t, image, caption, sems):
    width = image_s.shape[1]
    copy_all(
        [
            (image_s, image.at[:, :width]),
            (image_t, image.at[:, width:]),
            (caption_s, caption.at[:, :width]),
            (caption_t, caption.at[:, width:]),
        ],
        sems,
    )


def duplicate_kernel(*refs):
    count = len(refs) // 2
    for value, out in zip(refs[:count], refs[count:]):
        out[...] = value[...]


def assemble_kernel(*refs):
    refs[-1][...] = joined(refs[:-1])


def logits(left, right, out):
    gain = logit_gain / math.sqrt(left.shape[1])
    out[...] = gain * lax.dot_general(left, right, (((1,), (1,)), ((), ())), preferred_element_type=jnp.float32)
    matrix = out[...]
    peak = jnp.max(matrix, axis=1, keepdims=True)
    columns = [peak, jnp.sum(jnp.exp(matrix - peak), axis=1, keepdims=True)]
    peak = jnp.max(matrix, axis=0, keepdims=True)
    return columns, [peak, jnp.sum(jnp.exp(matrix - peak), axis=0, keepdims=True)]


def logits_kernel(n_img, rows, width, *refs):
    img_parts, cap_parts = refs[:n_img], refs[n_img:-5]
    student_ref, teacher_ref, row_ref, col_ref, images = refs[-5:]
    columns, lines = [], []
    for part, out in ((slice(0, width), student_ref), (slice(width, None), teacher_ref)):
        left = joined(img_parts, part)
        if out is student_ref:
            images[...] = left
        more = logits(left, joined(cap_parts, part), out)
        columns, lines = columns + more[0], lines + more[1]
    lines.append(jnp.zeros((4, lines[0].shape[1]), jnp.float32))
    row = lax.broadcasted_iota(jnp.int32, (8, LANES), 0)
    lane = lax.broadcasted_iota(jnp.int32, (8, LANES), 1)
    for ref, values, axes, order in (
        (row_ref, lines_of(columns), ROW_AXES, ROW_ORDER),
        (col_ref, jnp.concatenate(lines, axis=0), COL_AXES, COL_ORDER),
    ):
        for s, owner in enumerate(owners(axes, order)):
            ref[s] = jnp.zeros((8, LANES), jnp.float32)
            ref[s, :, :rows] = values[:, s * rows : (s + 1) * rows]
            index = (owner * rows + lane).astype(jnp.float32)
            ref[s] = jnp.where(row == INDEX, index, ref[s])


def merged(x, y):
    line = lax.broadcasted_iota(jnp.int32, x.shape, 0)
    student = line <= TOTAL_S
    x_peak = jnp.where(student, x[PEAK_S : PEAK_S + 1], x[PEAK_T : PEAK_T + 1])
    y_peak = jnp.where(student, y[PEAK_S : PEAK_S + 1], y[PEAK_T : PEAK_T + 1])
    peak = jnp.maximum(x_peak, y_peak)
    total = x * jnp.exp(x_peak - peak) + y * jnp.exp(y_peak - peak)
    both = jnp.where((line == PEAK_S) | (line == PEAK_T), peak, total)
    return jnp.where(line < INDEX, both, x)


def merged_blocks(mine, others, distances):
    blocks = [mine[s] for s in range(mine.shape[0])]
    for other, distance in zip(others, distances):
        blocks = [merged(block, other[s ^ distance]) for s, block in enumerate(blocks)]
    return blocks


def take(refs, plan):
    result = []
    for distances in plan:
        mine, others = refs[0], refs[1 : 1 + len(distances)]
        del refs[: 1 + len(distances)]
        result.append(merged_blocks(mine, others, distances))
    return result


def merge_kernel(plan, *refs):
    refs = list(refs)
    results = take(refs, plan)
    for out, blocks in zip(refs, results):
        for s, block in enumerate(blocks):
            out[s] = block


def tile_kernel(plan, n_cap, rows, width, student_ref, teacher_ref, *refs):
    refs = list(refs)
    blocks = take(refs, plan)
    captions = [refs.pop(0) for _ in range(n_cap)]
    tile_ref, send_ref, *outs = refs
    total, count = teacher_ref.shape

    def finish(blocks):
        lines = load_slots(blocks, rows)
        line = lax.broadcasted_iota(jnp.int32, lines.shape, 0)
        lse_s = lines[PEAK_S : PEAK_S + 1] + jnp.log(lines[TOTAL_S : TOTAL_S + 1])
        lse_t = lines[PEAK_T : PEAK_T + 1] + jnp.log(lines[TOTAL_T : TOTAL_T + 1])
        return jnp.where(line == 0, lse_s, jnp.where(line == 1, lse_t, lines))

    down, across = columns_of(finish(blocks[0])), finish(blocks[1])
    step = 64 if total % 64 == 0 else total
    for r in range(0, total, step):
        at = slice(r, r + step)
        s, t = student_ref[at], teacher_ref[at]
        grad = 0.5 * (jnp.exp(s - down[at, 0:1]) + jnp.exp(s - across[0:1]))
        grad = grad - 0.25 * (jnp.exp(t - down[at, 1:2]) + jnp.exp(t - across[1:2]))
        grad = grad - jnp.where(down[at, INDEX : INDEX + 1] == across[INDEX : INDEX + 1], 0.5, 0.0)
        tile_ref[at] = grad.astype(jnp.bfloat16)
    send_ref[...] = tile_ref[:, count // 2 :]
    right = joined(captions, slice(0, width))
    each = len(outs) * rows // lax.axis_size("ilo")
    step = each + rows
    for k in range(lax.axis_size("ilo")):
        part = jnp.dot(tile_ref[k * step + rows : (k + 1) * step], right, preferred_element_type=jnp.float32)
        spread(part, outs[k * each // rows : (k + 1) * each // rows])


def spread(part, outs):
    start = 0
    for out in outs:
        out[...] = part[start : start + out.shape[0]].astype(out.dtype)
        start += out.shape[0]


def image_kernel(width, step, tile_ref, *refs):
    parts = [ref for ref in refs if ref.dtype == jnp.bfloat16 and ref.shape[1] > width]
    right = joined(parts, slice(0, width))
    for k, out in enumerate(refs[len(parts) :]):
        start = k * step
        spread(jnp.dot(tile_ref[start : start + out.shape[0]], right, preferred_element_type=jnp.float32), [out])


def caption_kernel(tile_ref, tile_other, images, images_other, *outs):
    half = tile_other.shape[1]
    part = 0.0
    for tile, rows in ((tile_ref[:, :half], images[...]), (tile_other[...], images_other[...])):
        part = part + lax.dot_general(tile, rows, (((0,), (0,)), ((), ())), preferred_element_type=jnp.float32)
    spread(part, outs)


def sum_kernel(counts, *refs):
    refs = list(refs)
    terms = [[refs.pop(0) for _ in range(count)] for count in counts]
    outs, held, sems = refs[: len(counts)], refs[len(counts) : -1], refs[-1]
    copies = []
    for k, (group, out, here) in enumerate(zip(terms, outs, held)):
        total = group[0][...]
        for term in group[1:]:
            total = total + term[...].astype(jnp.float32)
        here[...] = total
        copies.append(pltpu.make_async_copy(here, out, sems.at[k]))
        copies[-1].start()
    for copy in copies:
        copy.wait()


VMEM, HBM = pltpu.VMEM, pltpu.HBM


def call(kernel, outs, args, flops=0, scratch=(), in_hbm=0, out_space=VMEM):
    moved = sum(math.prod(a.shape) * a.dtype.itemsize for a in list(args) + list(outs))
    spaces = [HBM] * in_hbm + [VMEM] * (len(args) - in_hbm)
    return pl.pallas_call(
        kernel,
        out_shape=[out_space(out.shape, out.dtype) for out in outs],
        in_specs=[pl.BlockSpec(memory_space=space) for space in spaces],
        out_specs=[pl.BlockSpec(memory_space=out_space)] * len(outs),
        scratch_shapes=scratch,
        compiler_params=pltpu.CompilerParams(vmem_limit_bytes=16 * 2**20),
        cost_estimate=pl.CostEstimate(flops=flops, bytes_accessed=moved, transcendentals=0),
    )(*(pltpu.with_memory_space_constraint(arg, space) for arg, space in zip(args, spaces)))


def after(value, *others):
    return lax.optimization_barrier((value, others))[0]


def local(image_student, caption_student, image_teacher, caption_teacher):
    ilo, chi, core, clo, ihi = (lax.axis_size(a) for a in ROW_AXES + COL_AXES)
    rows, width = image_student.shape
    depth = image_teacher.shape[1]
    assert rows <= LANES and core == 2 and chi > 1 and clo > 1
    n_img, n_cap = ilo * chi, core * ihi * clo
    total, columns = n_img * rows, n_cap * rows
    f32, bf16 = jnp.float32, jnp.bfloat16
    shape = jax.ShapeDtypeStruct
    dma = pltpu.SemaphoreType.DMA

    aligned = rows % 16 == 0
    if aligned:
        image, caption = call(
            pack_kernel,
            [shape((rows, width + depth), bf16)] * 2,
            [image_student, image_teacher, caption_student, caption_teacher],
            scratch=[dma((4,))],
            in_hbm=4,
        )
    else:
        image = jnp.concatenate([image_student, image_teacher], axis=1)
        caption = jnp.concatenate([caption_student, caption_teacher], axis=1)

    def assemble(parts):
        if not aligned:
            return jnp.concatenate(parts, axis=0)
        return call(assemble_kernel, [shape((len(parts) * rows, width + depth), bf16)], parts)[0]

    if aligned:
        image_near, caption_near = call(
            duplicate_kernel, [shape((rows, width + depth), bf16)] * 2, [image, caption]
        )
    else:
        image_near, caption_near = image, caption

    def gather(own, own_near, far_axis, near_axis):
        parts = {(0, c): swap(own, far_axis, c) if c else own for c in range(lax.axis_size(far_axis))}
        for h in range(1, lax.axis_size(near_axis)):
            parts.update({(h, c): swap(parts[0, c] if c else own_near, near_axis, h) for c in range(lax.axis_size(far_axis))})
        return parts

    img, cap = gather(image, image_near, "chi", "ilo"), gather(caption, caption_near, "clo", "ihi")
    early = [cap[h, 0] for h in range(ihi)]
    early = assemble([after(early[0], img[1, 0], img[0, 1])] + early[1:])
    late = [cap[h, c] for c in range(1, clo) for h in range(ihi)]
    late = assemble([after(late[0], img[1, 1])] + late[1:])
    img = [img[h, c] for h in range(ilo) for c in range(chi)]
    cap = [early, late, swap(early, "core", 1), swap(late, "core", 1)]
    if not aligned:
        img, cap = [assemble(img)], [assemble(cap)]

    row_shape, col_shape = shape((n_img, 8, LANES), f32), shape((n_cap, 8, LANES), f32)
    student, teacher, row_stats, col_stats, images = call(
        functools.partial(logits_kernel, len(img), rows, width),
        [shape((total, columns), f32)] * 2 + [row_shape, col_shape, shape((total, width), bf16)],
        img + cap,
        2 * total * columns * (width + depth),
    )

    images_other = swap(images, "core", 1)
    stats = [row_stats, col_stats]
    for row_names, col_names in zip(ROW_STAGES, COL_STAGES):
        plan, blocks = [], []
        for block, names, axes in zip(stats, (row_names, col_names), (ROW_AXES, COL_AXES)):
            others = partners(names, axes)
            plan.append([distance for _, distance in others])
            blocks += [block] + [swap(block, names, mask) for mask, _ in others]
        if row_names != ROW_STAGES[-1]:
            blocks[0] = after(blocks[0], images_other)
            stats = call(functools.partial(merge_kernel, plan), [row_shape, col_shape], blocks)

    far_blocks = [(h, c) for h in range(ilo) for c in range(1, chi)]
    near_blocks = [(h, 0) for h in range(ilo)]

    def pieces(blocks):
        return [shape((rows, width), bf16 if h else f32) for h, _ in blocks]

    tile, tile_send, *image_parts = call(
        functools.partial(tile_kernel, plan, len(cap), rows, width),
        [shape((total, columns), bf16), shape((total, columns // 2), bf16)] + pieces(far_blocks),
        [student, teacher] + blocks + cap,
        2 * total * columns * width // 2,
    )
    image_parts = dict(zip(far_blocks, image_parts))
    tile_other = swap(tile_send, "core", 1)

    caption_blocks = [(h, c) for c in range(clo) for h in range(ihi)]
    caption_parts = call(
        caption_kernel,
        pieces(caption_blocks),
        [tile, tile_other, images, images_other],
        2 * total * columns * width,
    )
    caption_parts = dict(zip(caption_blocks, caption_parts))

    def hop(parts, near, f):
        return [parts[0, f]] + [swap(parts[h, f], near, h) for h in range(1, lax.axis_size(near))]

    def rounded(terms):
        total = terms[0]
        for term in terms[1:]:
            total = total + term.astype(f32)
        return total.astype(bf16)

    image_far = [rounded(hop(image_parts, "ilo", f)) for f in range(1, chi)]
    caption_far = [rounded(hop(caption_parts, "ihi", f)) for f in range(1, clo)]
    rest = call(
        functools.partial(image_kernel, width, chi * rows),
        pieces(near_blocks),
        [after(tile, image_far[0])] + cap,
        2 * total * columns * width // chi,
    )
    image_parts.update(zip(near_blocks, rest))
    image_terms, caption_terms = hop(image_parts, "ilo", 0), hop(caption_parts, "ihi", 0)
    image_terms += [swap(image_far[f - 1], "chi", f) for f in range(1, chi)]
    caption_terms += [swap(caption_far[f - 1], "clo", f) for f in range(1, clo)]
    out = shape((rows, width), f32)
    caption_grad, image_grad = call(
        functools.partial(sum_kernel, (len(caption_terms), len(image_terms))),
        [out, out],
        caption_terms + image_terms,
        scratch=[pltpu.VMEM((rows, width), f32)] * 2 + [dma((2,))],
        out_space=HBM,
    )
    return (image_grad, caption_grad)


def split(count):
    low = 1 << ((count.bit_length() - 1) // 2)
    return count // low, low


def solution(mesh):
    ihi, ilo = split(mesh.shape["img"] // 2)
    chi, clo = split(mesh.shape["cap"])
    fine = Mesh(mesh.devices.reshape(ihi, ilo, 2, chi, clo), ("ihi", "ilo", "core", "chi", "clo"))
    by_image = P(("ihi", "ilo", "core", "chi", "clo"), None)
    by_caption = P(("chi", "clo", "ihi", "ilo", "core"), None)
    return jax.shard_map(
        local,
        mesh=fine,
        in_specs=(by_image, by_caption, by_image, by_caption),
        out_specs=(by_image, by_caption),
        check_vma=False,
    )
```

```python
import functools
import math

import jax
import jax.numpy as jnp
from jax import lax
from jax.experimental import pallas as pl
from jax.experimental.pallas import tpu as pltpu
from jax.sharding import Mesh, PartitionSpec as P

logit_gain = 3.0
ROW_AXES = ("ilo", "chi")
COL_AXES = ("core", "clo", "ihi")
ROW_STAGES = (("ilo",), ("chi",))
COL_STAGES = (("ihi", "clo"), ("core",))
ROW_ORDER = ("ihi", "ilo", "core", "chi", "clo")
COL_ORDER = ("chi", "clo", "ihi", "ilo", "core")
LANES = 128
PEAK_S, TOTAL_S, PEAK_T, TOTAL_T, INDEX = range(5)


def swap(value, axis, mask):
    size = lax.axis_size(axis)
    return lax.ppermute(value, axis, [(j, j ^ mask) for j in range(size)])


def partners(names, axes):
    sizes = [lax.axis_size(a) for a in names]
    strides = [math.prod(lax.axis_size(a) for a in axes[axes.index(name) + 1 :]) for name in names]
    result = []
    for mask in range(1, math.prod(sizes)):
        distance, rest = 0, mask
        for size, stride in zip(reversed(sizes), reversed(strides)):
            distance += rest % size * stride
            rest //= size
        result.append((mask, distance))
    return result


def lines_of(columns):
    count = columns[0].shape[0]
    lane = lax.broadcasted_iota(jnp.int32, (count, LANES), 1)
    wide = jnp.zeros((count, LANES), jnp.float32)
    for k, column in enumerate(columns):
        wide = jnp.where(lane == k, column, wide)
    spare = -count % LANES
    if spare:
        wide = jnp.concatenate([wide, jnp.zeros((spare, LANES), jnp.float32)], axis=0)
    return wide.T[:8, :count]


def columns_of(lines):
    count = lines.shape[1]
    spare = -count % LANES
    if spare:
        lines = jnp.concatenate([lines, jnp.zeros((8, spare), jnp.float32)], axis=1)
    tall = jnp.concatenate([lines, jnp.zeros((LANES - 8, count + spare), jnp.float32)], axis=0)
    return tall.T[:count]


def load_slots(blocks, rows):
    return jnp.concatenate([block[:, :rows] for block in blocks], axis=1)


def owners(axes, order):
    sizes = [lax.axis_size(a) for a in axes]
    result = []
    for s in range(math.prod(sizes)):
        place = {a: lax.axis_index(a) for a in order}
        for axis, size in zip(reversed(axes), reversed(sizes)):
            place[axis] = place[axis] ^ (s % size)
            s //= size
        owner = 0
        for axis in order:
            owner = owner * lax.axis_size(axis) + place[axis]
        result.append(owner)
    return result


def joined(refs, columns=slice(None)):
    values = [ref[:, columns] for ref in refs]
    return values[0] if len(values) == 1 else jnp.concatenate(values, axis=0)


def copy_all(pairs, sems):
    copies = [pltpu.make_async_copy(src, dst, sems.at[k]) for k, (src, dst) in enumerate(pairs)]
    for copy in copies:
        copy.start()
    for copy in copies:
        copy.wait()


def pack_kernel(image_s, image_t, caption_s, caption_t, image, caption, sems):
    width = image_s.shape[1]
    copy_all(
        [
            (image_s, image.at[:, :width]),
            (image_t, image.at[:, width:]),
            (caption_s, caption.at[:, :width]),
            (caption_t, caption.at[:, width:]),
        ],
        sems,
    )


def duplicate_kernel(*refs):
    count = len(refs) // 2
    for value, out in zip(refs[:count], refs[count:]):
        out[...] = value[...]


def assemble_kernel(*refs):
    refs[-1][...] = joined(refs[:-1])


def window(refs, start, stop, columns):
    values, first = [], 0
    for ref in refs:
        low, high = max(start - first, 0), min(stop - first, ref.shape[0])
        if low < high:
            values.append(ref[low:high, columns])
        first += ref.shape[0]
    return values[0] if len(values) == 1 else jnp.concatenate(values, axis=0)


def logits(left, right, out):
    gain = logit_gain / math.sqrt(left.shape[1])
    out[...] = gain * lax.dot_general(left, right, (((1,), (1,)), ((), ())), preferred_element_type=jnp.float32)
    matrix = out[...]
    peak = jnp.max(matrix, axis=1, keepdims=True)
    columns = [peak, jnp.sum(jnp.exp(matrix - peak), axis=1, keepdims=True)]
    peak = jnp.max(matrix, axis=0, keepdims=True)
    return columns, [peak, jnp.sum(jnp.exp(matrix - peak), axis=0, keepdims=True)]


def stacked(lines):
    count = lines[0].shape[1]
    row = lax.broadcasted_iota(jnp.int32, (8, count), 0)
    result = jnp.zeros((8, count), jnp.float32)
    for k, line in enumerate(lines):
        result = jnp.where(row == k, line, result)
    return result


def head_kernel(n_img, width, *refs):
    img_parts, cap_parts = refs[:n_img], refs[n_img:-4]
    student_ref, teacher_ref, wide_ref, lines_ref = refs[-4:]
    count = student_ref.shape[1]
    columns, lines = [], []
    for part, out in ((slice(0, width), student_ref), (slice(width, None), teacher_ref)):
        left = joined(img_parts, part)
        more = logits(left, window(cap_parts, 0, count, part), out)
        columns, lines = columns + more[0], lines + more[1]
    lane = lax.broadcasted_iota(jnp.int32, wide_ref.shape, 1)
    wide = jnp.zeros(wide_ref.shape, jnp.float32)
    for k, column in enumerate(columns):
        wide = jnp.where(lane == k, column, wide)
    wide_ref[...] = wide
    lines_ref[...] = stacked(lines)


def tail_kernel(n_img, start, rows, width, wide_ref, lines_ref, *refs):
    img_parts, cap_parts = refs[:n_img], refs[n_img:-5]
    student_ref, teacher_ref, row_ref, col_ref, images = refs[-5:]
    stop = start + student_ref.shape[1]
    columns, lines = [], []
    for part, out in ((slice(0, width), student_ref), (slice(width, None), teacher_ref)):
        left = joined(img_parts, part)
        if out is student_ref:
            images[...] = left
        (peak, total), more = logits(left, window(cap_parts, start, stop, part), out)
        k = len(columns)
        before_peak, before = wide_ref[:, k : k + 1], wide_ref[:, k + 1 : k + 2]
        both = jnp.maximum(peak, before_peak)
        columns += [both, before * jnp.exp(before_peak - both) + total * jnp.exp(peak - both)]
        lines += more
    lines = jnp.concatenate([lines_ref[...], stacked(lines)], axis=1)
    row = lax.broadcasted_iota(jnp.int32, (8, LANES), 0)
    lane = lax.broadcasted_iota(jnp.int32, (8, LANES), 1)
    for ref, values, axes, order in (
        (row_ref, lines_of(columns), ROW_AXES, ROW_ORDER),
        (col_ref, lines, COL_AXES, COL_ORDER),
    ):
        for s, owner in enumerate(owners(axes, order)):
            ref[s] = jnp.zeros((8, LANES), jnp.float32)
            ref[s, :, :rows] = values[:, s * rows : (s + 1) * rows]
            index = (owner * rows + lane).astype(jnp.float32)
            ref[s] = jnp.where(row == INDEX, index, ref[s])


def merged(x, y):
    line = lax.broadcasted_iota(jnp.int32, x.shape, 0)
    student = line <= TOTAL_S
    x_peak = jnp.where(student, x[PEAK_S : PEAK_S + 1], x[PEAK_T : PEAK_T + 1])
    y_peak = jnp.where(student, y[PEAK_S : PEAK_S + 1], y[PEAK_T : PEAK_T + 1])
    peak = jnp.maximum(x_peak, y_peak)
    total = x * jnp.exp(x_peak - peak) + y * jnp.exp(y_peak - peak)
    both = jnp.where((line == PEAK_S) | (line == PEAK_T), peak, total)
    return jnp.where(line < INDEX, both, x)


def merged_blocks(mine, others, distances):
    blocks = [mine[s] for s in range(mine.shape[0])]
    for other, distance in zip(others, distances):
        blocks = [merged(block, other[s ^ distance]) for s, block in enumerate(blocks)]
    return blocks


def take(refs, plan):
    result = []
    for distances in plan:
        mine, others = refs[0], refs[1 : 1 + len(distances)]
        del refs[: 1 + len(distances)]
        result.append(merged_blocks(mine, others, distances))
    return result


def merge_kernel(plan, *refs):
    refs = list(refs)
    results = take(refs, plan)
    for out, blocks in zip(refs, results):
        for s, block in enumerate(blocks):
            out[s] = block


def tile_kernel(plan, n_cap, rows, width, *refs):
    refs = list(refs)
    student_refs, teacher_refs = (refs.pop(0), refs.pop(0)), (refs.pop(0), refs.pop(0))
    blocks = take(refs, plan)
    captions = [refs.pop(0) for _ in range(n_cap)]
    tile_ref, send_ref, *outs = refs
    total, count = tile_ref.shape

    def finish(blocks):
        lines = load_slots(blocks, rows)
        line = lax.broadcasted_iota(jnp.int32, lines.shape, 0)
        lse_s = lines[PEAK_S : PEAK_S + 1] + jnp.log(lines[TOTAL_S : TOTAL_S + 1])
        lse_t = lines[PEAK_T : PEAK_T + 1] + jnp.log(lines[TOTAL_T : TOTAL_T + 1])
        return jnp.where(line == 0, lse_s, jnp.where(line == 1, lse_t, lines))

    down, across = columns_of(finish(blocks[0])), finish(blocks[1])
    step = 64 if total % 64 == 0 else total
    for r in range(0, total, step):
        at = slice(r, r + step)
        s, t = (jnp.concatenate([ref[at] for ref in pair], axis=1) for pair in (student_refs, teacher_refs))
        grad = 0.5 * (jnp.exp(s - down[at, 0:1]) + jnp.exp(s - across[0:1]))
        grad = grad - 0.25 * (jnp.exp(t - down[at, 1:2]) + jnp.exp(t - across[1:2]))
        grad = grad - jnp.where(down[at, INDEX : INDEX + 1] == across[INDEX : INDEX + 1], 0.5, 0.0)
        tile_ref[at] = grad.astype(jnp.bfloat16)
    send_ref[...] = tile_ref[:, count // 2 :]
    right = joined(captions, slice(0, width))
    each = len(outs) * rows // lax.axis_size("ilo")
    step = each + rows
    for k in range(lax.axis_size("ilo")):
        part = jnp.dot(tile_ref[k * step + rows : (k + 1) * step], right, preferred_element_type=jnp.float32)
        spread(part, outs[k * each // rows : (k + 1) * each // rows])


def spread(part, outs):
    start = 0
    for out in outs:
        out[...] = part[start : start + out.shape[0]].astype(out.dtype)
        start += out.shape[0]


def image_kernel(width, step, tile_ref, *refs):
    parts = [ref for ref in refs if ref.dtype == jnp.bfloat16 and ref.shape[1] > width]
    right = joined(parts, slice(0, width))
    for k, out in enumerate(refs[len(parts) :]):
        start = k * step
        spread(jnp.dot(tile_ref[start : start + out.shape[0]], right, preferred_element_type=jnp.float32), [out])


def caption_kernel(tile_ref, tile_other, images, images_other, *outs):
    half = tile_other.shape[1]
    part = 0.0
    for tile, rows in ((tile_ref[:, :half], images[...]), (tile_other[...], images_other[...])):
        part = part + lax.dot_general(tile, rows, (((0,), (0,)), ((), ())), preferred_element_type=jnp.float32)
    spread(part, outs)


def sum_kernel(counts, *refs):
    refs = list(refs)
    terms = [[refs.pop(0) for _ in range(count)] for count in counts]
    outs, held, sems = refs[: len(counts)], refs[len(counts) : -1], refs[-1]
    copies = []
    for k, (group, out, here) in enumerate(zip(terms, outs, held)):
        total = group[0][...]
        for term in group[1:]:
            total = total + term[...].astype(jnp.float32)
        here[...] = total
        copies.append(pltpu.make_async_copy(here, out, sems.at[k]))
        copies[-1].start()
    for copy in copies:
        copy.wait()


VMEM, HBM = pltpu.VMEM, pltpu.HBM


def call(kernel, outs, args, flops=0, scratch=(), in_hbm=0, out_space=VMEM):
    moved = sum(math.prod(a.shape) * a.dtype.itemsize for a in list(args) + list(outs))
    spaces = [HBM] * in_hbm + [VMEM] * (len(args) - in_hbm)
    return pl.pallas_call(
        kernel,
        out_shape=[out_space(out.shape, out.dtype) for out in outs],
        in_specs=[pl.BlockSpec(memory_space=space) for space in spaces],
        out_specs=[pl.BlockSpec(memory_space=out_space)] * len(outs),
        scratch_shapes=scratch,
        compiler_params=pltpu.CompilerParams(vmem_limit_bytes=16 * 2**20),
        cost_estimate=pl.CostEstimate(flops=flops, bytes_accessed=moved, transcendentals=0),
    )(*(pltpu.with_memory_space_constraint(arg, space) for arg, space in zip(args, spaces)))


def after(value, *others):
    return lax.optimization_barrier((value, others))[0]


def local(image_student, caption_student, image_teacher, caption_teacher):
    ilo, chi, core, clo, ihi = (lax.axis_size(a) for a in ROW_AXES + COL_AXES)
    rows, width = image_student.shape
    depth = image_teacher.shape[1]
    assert rows <= LANES and core == 2 and chi > 1 and clo > 1
    n_img, n_cap = ilo * chi, core * ihi * clo
    total, columns = n_img * rows, n_cap * rows
    f32, bf16 = jnp.float32, jnp.bfloat16
    shape = jax.ShapeDtypeStruct
    dma = pltpu.SemaphoreType.DMA

    aligned = rows % 16 == 0
    if aligned:
        image, caption = call(
            pack_kernel,
            [shape((rows, width + depth), bf16)] * 2,
            [image_student, image_teacher, caption_student, caption_teacher],
            scratch=[dma((4,))],
            in_hbm=4,
        )
    else:
        image = jnp.concatenate([image_student, image_teacher], axis=1)
        caption = jnp.concatenate([caption_student, caption_teacher], axis=1)

    def assemble(parts):
        if not aligned:
            return jnp.concatenate(parts, axis=0)
        return call(assemble_kernel, [shape((len(parts) * rows, width + depth), bf16)], parts)[0]

    if aligned:
        image_near, caption_near = call(
            duplicate_kernel, [shape((rows, width + depth), bf16)] * 2, [image, caption]
        )
    else:
        image_near, caption_near = image, caption

    def gather(own, own_near, far_axis, near_axis):
        parts = {(0, c): swap(own, far_axis, c) if c else own for c in range(lax.axis_size(far_axis))}
        for h in range(1, lax.axis_size(near_axis)):
            parts.update({(h, c): swap(parts[0, c] if c else own_near, near_axis, h) for c in range(lax.axis_size(far_axis))})
        return parts

    img, cap = gather(image, image_near, "chi", "ilo"), gather(caption, caption_near, "clo", "ihi")
    early = [cap[h, 0] for h in range(ihi)]
    early = assemble([after(early[0], img[1, 0], img[0, 1])] + early[1:])
    late = [cap[h, c] for c in range(1, clo) for h in range(ihi)]
    late = assemble([after(late[0], img[1, 1])] + late[1:])
    img = [img[h, c] for h in range(ilo) for c in range(chi)]
    cap = [early, late, swap(early, "core", 1), swap(late, "core", 1)]
    if not aligned:
        img, cap = [assemble(img)], [assemble(cap)]

    row_shape, col_shape = shape((n_img, 8, LANES), f32), shape((n_cap, 8, LANES), f32)
    head = (columns - (cap[-1].shape[0] if aligned else rows)) // LANES * LANES
    ready = cap[:-1] if aligned else cap
    skipped = [part for k, part in enumerate(cap) if sum(p.shape[0] for p in cap[: k + 1]) <= head]
    needed = cap[len(skipped) :]
    start = head - sum(part.shape[0] for part in skipped)
    student, teacher, wide, lines = call(
        functools.partial(head_kernel, len(img), width),
        [shape((total, head), f32)] * 2 + [shape((total, LANES), f32), shape((8, head), f32)],
        img + ready,
        2 * total * head * (width + depth),
    )
    student_tail, teacher_tail, row_stats, col_stats, images = call(
        functools.partial(tail_kernel, len(img), start, rows, width),
        [shape((total, columns - head), f32)] * 2 + [row_shape, col_shape, shape((total, width), bf16)],
        [wide, lines] + img + needed,
        2 * total * (columns - head) * (width + depth),
    )

    images_other = swap(images, "core", 1)
    stats = [row_stats, col_stats]
    for row_names, col_names in zip(ROW_STAGES, COL_STAGES):
        plan, blocks = [], []
        for block, names, axes in zip(stats, (row_names, col_names), (ROW_AXES, COL_AXES)):
            others = partners(names, axes)
            plan.append([distance for _, distance in others])
            blocks += [block] + [swap(block, names, mask) for mask, _ in others]
        if row_names != ROW_STAGES[-1]:
            blocks[0] = after(blocks[0], images_other)
            stats = call(functools.partial(merge_kernel, plan), [row_shape, col_shape], blocks)

    far_blocks = [(h, c) for h in range(ilo) for c in range(1, chi)]
    near_blocks = [(h, 0) for h in range(ilo)]

    def pieces(blocks):
        return [shape((rows, width), bf16 if h else f32) for h, _ in blocks]

    tile, tile_send, *image_parts = call(
        functools.partial(tile_kernel, plan, len(cap), rows, width),
        [shape((total, columns), bf16), shape((total, columns // 2), bf16)] + pieces(far_blocks),
        [student, student_tail, teacher, teacher_tail] + blocks + cap,
        2 * total * columns * width // 2,
    )
    image_parts = dict(zip(far_blocks, image_parts))
    tile_other = swap(tile_send, "core", 1)

    caption_blocks = [(h, c) for c in range(clo) for h in range(ihi)]
    caption_parts = call(
        caption_kernel,
        pieces(caption_blocks),
        [tile, tile_other, images, images_other],
        2 * total * columns * width,
    )
    caption_parts = dict(zip(caption_blocks, caption_parts))

    def hop(parts, near, f):
        return [parts[0, f]] + [swap(parts[h, f], near, h) for h in range(1, lax.axis_size(near))]

    def rounded(terms):
        total = terms[0]
        for term in terms[1:]:
            total = total + term.astype(f32)
        return total.astype(bf16)

    image_far = [rounded(hop(image_parts, "ilo", f)) for f in range(1, chi)]
    caption_far = [rounded(hop(caption_parts, "ihi", f)) for f in range(1, clo)]
    rest = call(
        functools.partial(image_kernel, width, chi * rows),
        pieces(near_blocks),
        [after(tile, image_far[0])] + cap,
        2 * total * columns * width // chi,
    )
    image_parts.update(zip(near_blocks, rest))
    image_terms, caption_terms = hop(image_parts, "ilo", 0), hop(caption_parts, "ihi", 0)
    image_terms += [swap(image_far[f - 1], "chi", f) for f in range(1, chi)]
    caption_terms += [swap(caption_far[f - 1], "clo", f) for f in range(1, clo)]
    out = shape((rows, width), f32)
    caption_grad, image_grad = call(
        functools.partial(sum_kernel, (len(caption_terms), len(image_terms))),
        [out, out],
        caption_terms + image_terms,
        scratch=[pltpu.VMEM((rows, width), f32)] * 2 + [dma((2,))],
        out_space=HBM,
    )
    return (image_grad, caption_grad)


def split(count):
    low = 1 << ((count.bit_length() - 1) // 2)
    return count // low, low


def solution(mesh):
    ihi, ilo = split(mesh.shape["img"] // 2)
    chi, clo = split(mesh.shape["cap"])
    fine = Mesh(mesh.devices.reshape(ihi, ilo, 2, chi, clo), ("ihi", "ilo", "core", "chi", "clo"))
    by_image = P(("ihi", "ilo", "core", "chi", "clo"), None)
    by_caption = P(("chi", "clo", "ihi", "ilo", "core"), None)
    return jax.shard_map(
        local,
        mesh=fine,
        in_specs=(by_image, by_caption, by_image, by_caption),
        out_specs=(by_image, by_caption),
        check_vma=False,
    )
```

```python
import functools
import math

import jax
import jax.numpy as jnp
from jax import lax
from jax.experimental import pallas as pl
from jax.experimental.pallas import tpu as pltpu
from jax.sharding import Mesh, PartitionSpec as P

logit_gain = 3.0
ROW_AXES = ("ilo", "chi")
COL_AXES = ("core", "clo", "ihi")
ROW_STAGES = (("ilo",), ("chi",))
COL_STAGES = (("ihi", "clo"), ("core",))
ROW_ORDER = ("ihi", "ilo", "core", "chi", "clo")
COL_ORDER = ("chi", "clo", "ihi", "ilo", "core")
LANES = 128
PEAK_S, TOTAL_S, PEAK_T, TOTAL_T, INDEX = range(5)


def swap(value, axis, mask):
    size = lax.axis_size(axis)
    return lax.ppermute(value, axis, [(j, j ^ mask) for j in range(size)])


def partners(names, axes):
    sizes = [lax.axis_size(a) for a in names]
    strides = [math.prod(lax.axis_size(a) for a in axes[axes.index(name) + 1 :]) for name in names]
    result = []
    for mask in range(1, math.prod(sizes)):
        distance, rest = 0, mask
        for size, stride in zip(reversed(sizes), reversed(strides)):
            distance += rest % size * stride
            rest //= size
        result.append((mask, distance))
    return result


def lines_of(columns):
    count = columns[0].shape[0]
    lane = lax.broadcasted_iota(jnp.int32, (count, LANES), 1)
    wide = jnp.zeros((count, LANES), jnp.float32)
    for k, column in enumerate(columns):
        wide = jnp.where(lane == k, column, wide)
    spare = -count % LANES
    if spare:
        wide = jnp.concatenate([wide, jnp.zeros((spare, LANES), jnp.float32)], axis=0)
    return wide.T[:8, :count]


def columns_of(lines):
    count = lines.shape[1]
    spare = -count % LANES
    if spare:
        lines = jnp.concatenate([lines, jnp.zeros((8, spare), jnp.float32)], axis=1)
    tall = jnp.concatenate([lines, jnp.zeros((LANES - 8, count + spare), jnp.float32)], axis=0)
    return tall.T[:count]


def store_slots(ref, lines, rows):
    ref[...] = jnp.zeros_like(ref)
    for s in range(ref.shape[0]):
        ref[s, :, :rows] = lines[:, s * rows : (s + 1) * rows]


def load_slots(blocks, rows):
    return jnp.concatenate([block[:, :rows] for block in blocks], axis=1)


def owners(axes, order):
    sizes = [lax.axis_size(a) for a in axes]
    result = []
    for s in range(math.prod(sizes)):
        place = {a: lax.axis_index(a) for a in order}
        for axis, size in zip(reversed(axes), reversed(sizes)):
            place[axis] = place[axis] ^ (s % size)
            s //= size
        owner = 0
        for axis in order:
            owner = owner * lax.axis_size(axis) + place[axis]
        result.append(owner)
    return result


def joined(refs, columns=slice(None)):
    values = [ref[:, columns] for ref in refs]
    return values[0] if len(values) == 1 else jnp.concatenate(values, axis=0)


def copy_all(pairs, sems):
    copies = [pltpu.make_async_copy(src, dst, sems.at[k]) for k, (src, dst) in enumerate(pairs)]
    for copy in copies:
        copy.start()
    for copy in copies:
        copy.wait()


def pack_kernel(image_s, image_t, caption_s, caption_t, image, caption, sems):
    width = image_s.shape[1]
    copy_all(
        [
            (image_s, image.at[:, :width]),
            (image_t, image.at[:, width:]),
            (caption_s, caption.at[:, :width]),
            (caption_t, caption.at[:, width:]),
        ],
        sems,
    )


def duplicate_kernel(*refs):
    count = len(refs) // 2
    for value, out in zip(refs[:count], refs[count:]):
        out[...] = value[...]


def assemble_kernel(*refs):
    refs[-1][...] = joined(refs[:-1])


def window(refs, start, stop, columns):
    values, first = [], 0
    for ref in refs:
        low, high = max(start - first, 0), min(stop - first, ref.shape[0])
        if low < high:
            values.append(ref[low:high, columns])
        first += ref.shape[0]
    return values[0] if len(values) == 1 else jnp.concatenate(values, axis=0)


def logits(left, right, out):
    gain = logit_gain / math.sqrt(left.shape[1])
    out[...] = gain * lax.dot_general(left, right, (((1,), (1,)), ((), ())), preferred_element_type=jnp.float32)
    matrix = out[...]
    peak = jnp.max(matrix, axis=1, keepdims=True)
    columns = [peak, jnp.sum(jnp.exp(matrix - peak), axis=1, keepdims=True)]
    peak = jnp.max(matrix, axis=0, keepdims=True)
    return columns, [peak, jnp.sum(jnp.exp(matrix - peak), axis=0, keepdims=True)]


def stacked(lines):
    count = lines[0].shape[1]
    row = lax.broadcasted_iota(jnp.int32, (8, count), 0)
    result = jnp.zeros((8, count), jnp.float32)
    for k, line in enumerate(lines):
        result = jnp.where(row == k, line, result)
    return result


def head_kernel(n_img, rows, width, *refs):
    img_parts, cap_parts = refs[:n_img], refs[n_img:-4]
    student_ref, teacher_ref, row_ref, lines_ref = refs[-4:]
    count = student_ref.shape[1]
    columns, lines = [], []
    for part, out in ((slice(0, width), student_ref), (slice(width, None), teacher_ref)):
        more = logits(joined(img_parts, part), window(cap_parts, 0, count, part), out)
        columns, lines = columns + more[0], lines + more[1]
    store_slots(row_ref, lines_of(columns), rows)
    lines_ref[...] = stacked(lines)


def tail_kernel(n_img, start, rows, width, head_ref, lines_ref, *refs):
    img_parts, cap_parts = refs[:n_img], refs[n_img:-5]
    student_ref, teacher_ref, row_ref, col_ref, images = refs[-5:]
    stop = start + student_ref.shape[1]
    columns, lines = [], []
    for part, out in ((slice(0, width), student_ref), (slice(width, None), teacher_ref)):
        left = joined(img_parts, part)
        if out is student_ref:
            images[...] = left
        more = logits(left, window(cap_parts, start, stop, part), out)
        columns, lines = columns + more[0], lines + more[1]
    store_slots(row_ref, lines_of(columns), rows)
    store_slots(col_ref, jnp.concatenate([lines_ref[...], stacked(lines)], axis=1), rows)
    row = lax.broadcasted_iota(jnp.int32, (8, LANES), 0)
    lane = lax.broadcasted_iota(jnp.int32, (8, LANES), 1)
    for ref, axes, order in ((row_ref, ROW_AXES, ROW_ORDER), (col_ref, COL_AXES, COL_ORDER)):
        for s, owner in enumerate(owners(axes, order)):
            block = merged(head_ref[s], ref[s]) if ref is row_ref else ref[s]
            ref[s] = jnp.where(row == INDEX, (owner * rows + lane).astype(jnp.float32), block)


def merged(x, y):
    line = lax.broadcasted_iota(jnp.int32, x.shape, 0)
    student = line <= TOTAL_S
    x_peak = jnp.where(student, x[PEAK_S : PEAK_S + 1], x[PEAK_T : PEAK_T + 1])
    y_peak = jnp.where(student, y[PEAK_S : PEAK_S + 1], y[PEAK_T : PEAK_T + 1])
    peak = jnp.maximum(x_peak, y_peak)
    total = x * jnp.exp(x_peak - peak) + y * jnp.exp(y_peak - peak)
    both = jnp.where((line == PEAK_S) | (line == PEAK_T), peak, total)
    return jnp.where(line < INDEX, both, x)


def merged_blocks(mine, others, distances):
    blocks = [mine[s] for s in range(mine.shape[0])]
    for other, distance in zip(others, distances):
        blocks = [merged(block, other[s ^ distance]) for s, block in enumerate(blocks)]
    return blocks


def take(refs, plan):
    result = []
    for distances in plan:
        mine, others = refs[0], refs[1 : 1 + len(distances)]
        del refs[: 1 + len(distances)]
        result.append(merged_blocks(mine, others, distances))
    return result


def merge_kernel(plan, *refs):
    refs = list(refs)
    results = take(refs, plan)
    for out, blocks in zip(refs, results):
        for s, block in enumerate(blocks):
            out[s] = block


def tile_kernel(plan, n_cap, rows, width, *refs):
    refs = list(refs)
    student_refs, teacher_refs = (refs.pop(0), refs.pop(0)), (refs.pop(0), refs.pop(0))
    blocks = take(refs, plan)
    captions = [refs.pop(0) for _ in range(n_cap)]
    tile_ref, send_ref, first_ref = refs
    total, count = tile_ref.shape

    def finish(blocks):
        lines = load_slots(blocks, rows)
        line = lax.broadcasted_iota(jnp.int32, lines.shape, 0)
        lse_s = lines[PEAK_S : PEAK_S + 1] + jnp.log(lines[TOTAL_S : TOTAL_S + 1])
        lse_t = lines[PEAK_T : PEAK_T + 1] + jnp.log(lines[TOTAL_T : TOTAL_T + 1])
        return jnp.where(line == 0, lse_s, jnp.where(line == 1, lse_t, lines))

    down, across = columns_of(finish(blocks[0])), finish(blocks[1])
    step = 64 if total % 64 == 0 else total
    for r in range(0, total, step):
        at = slice(r, r + step)
        s, t = (jnp.concatenate([ref[at] for ref in pair], axis=1) for pair in (student_refs, teacher_refs))
        grad = 0.5 * (jnp.exp(s - down[at, 0:1]) + jnp.exp(s - across[0:1]))
        grad = grad - 0.25 * (jnp.exp(t - down[at, 1:2]) + jnp.exp(t - across[1:2]))
        grad = grad - jnp.where(down[at, INDEX : INDEX + 1] == across[INDEX : INDEX + 1], 0.5, 0.0)
        tile_ref[at] = grad.astype(jnp.bfloat16)
    send_ref[...] = tile_ref[:, count // 2 :]
    right = joined(captions, slice(0, width))
    part = jnp.dot(tile_ref[total - first_ref.shape[0] :], right, preferred_element_type=jnp.float32)
    first_ref[...] = part.astype(jnp.bfloat16)


def spread(part, outs):
    start = 0
    for out in outs:
        out[...] = part[start : start + out.shape[0]].astype(out.dtype)
        start += out.shape[0]


def image_kernel(width, tile_ref, *refs):
    parts = [ref for ref in refs if ref.dtype == jnp.bfloat16 and ref.shape[1] > width]
    right = joined(parts, slice(0, width))
    outs = refs[len(parts) :]
    count = sum(out.shape[0] for out in outs)
    spread(jnp.dot(tile_ref[:count], right, preferred_element_type=jnp.float32), outs)


def caption_kernel(tile_ref, tile_other, images, images_other, *outs):
    half = tile_other.shape[1]
    part = 0.0
    for tile, rows in ((tile_ref[:, :half], images[...]), (tile_other[...], images_other[...])):
        part = part + lax.dot_general(tile, rows, (((0,), (0,)), ((), ())), preferred_element_type=jnp.float32)
    spread(part, outs)


def sum_kernel(counts, *refs):
    refs = list(refs)
    terms = [[refs.pop(0) for _ in range(count)] for count in counts]
    outs, held, sems = refs[: len(counts)], refs[len(counts) : -1], refs[-1]
    copies = []
    for k, (group, out, here) in enumerate(zip(terms, outs, held)):
        total = group[0][...]
        for term in group[1:]:
            total = total + term[...].astype(jnp.float32)
        here[...] = total
        copies.append(pltpu.make_async_copy(here, out, sems.at[k]))
        copies[-1].start()
    for copy in copies:
        copy.wait()


VMEM, HBM = pltpu.VMEM, pltpu.HBM


def call(kernel, outs, args, flops=0, scratch=(), in_hbm=0, out_space=VMEM):
    moved = sum(math.prod(a.shape) * a.dtype.itemsize for a in list(args) + list(outs))
    spaces = [HBM] * in_hbm + [VMEM] * (len(args) - in_hbm)
    return pl.pallas_call(
        kernel,
        out_shape=[out_space(out.shape, out.dtype) for out in outs],
        in_specs=[pl.BlockSpec(memory_space=space) for space in spaces],
        out_specs=[pl.BlockSpec(memory_space=out_space)] * len(outs),
        scratch_shapes=scratch,
        compiler_params=pltpu.CompilerParams(vmem_limit_bytes=16 * 2**20),
        cost_estimate=pl.CostEstimate(flops=flops, bytes_accessed=moved, transcendentals=0),
    )(*(pltpu.with_memory_space_constraint(arg, space) for arg, space in zip(args, spaces)))


def after(value, *others):
    return lax.optimization_barrier((value, others))[0]


def local(image_student, caption_student, image_teacher, caption_teacher):
    ilo, chi, core, clo, ihi = (lax.axis_size(a) for a in ROW_AXES + COL_AXES)
    rows, width = image_student.shape
    depth = image_teacher.shape[1]
    assert rows <= LANES and core == 2 and chi > 1 and clo > 1
    n_img, n_cap = ilo * chi, core * ihi * clo
    total, columns = n_img * rows, n_cap * rows
    f32, bf16 = jnp.float32, jnp.bfloat16
    shape = jax.ShapeDtypeStruct
    dma = pltpu.SemaphoreType.DMA

    aligned = rows % 16 == 0
    if aligned:
        image, caption = call(
            pack_kernel,
            [shape((rows, width + depth), bf16)] * 2,
            [image_student, image_teacher, caption_student, caption_teacher],
            scratch=[dma((4,))],
            in_hbm=4,
        )
    else:
        image = jnp.concatenate([image_student, image_teacher], axis=1)
        caption = jnp.concatenate([caption_student, caption_teacher], axis=1)

    def assemble(parts):
        if not aligned:
            return jnp.concatenate(parts, axis=0)
        return call(assemble_kernel, [shape((len(parts) * rows, width + depth), bf16)], parts)[0]

    if aligned:
        image_near, caption_near = call(
            duplicate_kernel, [shape((rows, width + depth), bf16)] * 2, [image, caption]
        )
    else:
        image_near, caption_near = image, caption

    def gather(own, own_near, far_axis, near_axis):
        parts = {(0, c): swap(own, far_axis, c) if c else own for c in range(lax.axis_size(far_axis))}
        for h in range(1, lax.axis_size(near_axis)):
            parts.update({(h, c): swap(parts[0, c] if c else own_near, near_axis, h) for c in range(lax.axis_size(far_axis))})
        return parts

    img, cap = gather(image, image_near, "chi", "ilo"), gather(caption, caption_near, "clo", "ihi")
    early = [cap[h, 0] for h in range(ihi)]
    early = assemble([after(early[0], img[1, 0], img[0, 1])] + early[1:])
    late = [cap[h, c] for c in range(1, clo) for h in range(ihi)]
    late = assemble([after(late[0], img[1, 1])] + late[1:])
    img = [img[h, c] for h in range(ilo) for c in range(chi)]
    cap = [early, late, swap(early, "core", 1), swap(late, "core", 1)]
    if not aligned:
        img, cap = [assemble(img)], [assemble(cap)]

    row_shape, col_shape = shape((n_img, 8, LANES), f32), shape((n_cap, 8, LANES), f32)
    head = (columns - (cap[-1].shape[0] if aligned else rows)) // LANES * LANES
    ready = cap[:-1] if aligned else cap
    skipped = [part for k, part in enumerate(cap) if sum(p.shape[0] for p in cap[: k + 1]) <= head]
    needed = cap[len(skipped) :]
    start = head - sum(part.shape[0] for part in skipped)
    student, teacher, row_head, lines = call(
        functools.partial(head_kernel, len(img), rows, width),
        [shape((total, head), f32)] * 2 + [row_shape, shape((8, head), f32)],
        img + ready,
        2 * total * head * (width + depth),
    )
    student_tail, teacher_tail, row_stats, col_stats, images = call(
        functools.partial(tail_kernel, len(img), start, rows, width),
        [shape((total, columns - head), f32)] * 2 + [row_shape, col_shape, shape((total, width), bf16)],
        [row_head, lines] + img + needed,
        2 * total * (columns - head) * (width + depth),
    )

    images_other = swap(images, "core", 1)
    stats = [row_stats, col_stats]
    for row_names, col_names in zip(ROW_STAGES, COL_STAGES):
        plan, blocks = [], []
        for block, names, axes in zip(stats, (row_names, col_names), (ROW_AXES, COL_AXES)):
            others = partners(names, axes)
            plan.append([distance for _, distance in others])
            blocks += [block] + [swap(block, names, mask) for mask, _ in others]
        if row_names != ROW_STAGES[-1]:
            blocks[0] = after(blocks[0], images_other)
            stats = call(functools.partial(merge_kernel, plan), [row_shape, col_shape], blocks)

    image_blocks = [(h, c) for h in range(ilo) for c in range(chi)]
    caption_blocks = [(h, c) for c in range(clo) for h in range(ihi)]

    def pieces(blocks):
        return [shape((rows, width), bf16 if h else f32) for h, _ in blocks]

    tile, tile_send, image_first = call(
        functools.partial(tile_kernel, plan, len(cap), rows, width),
        [shape((total, columns), bf16), shape((total, columns // 2), bf16), shape((rows, width), bf16)],
        [student, student_tail, teacher, teacher_tail] + blocks + cap,
        2 * rows * columns * width,
    )
    tile_other = swap(tile_send, "core", 1)

    image_parts = call(
        functools.partial(image_kernel, width),
        pieces(image_blocks)[:-1],
        [tile] + cap,
        2 * total * columns * width,
    )
    image_parts = dict(zip(image_blocks, list(image_parts) + [image_first]))
    caption_parts = call(
        caption_kernel,
        pieces(caption_blocks),
        [tile, tile_other, images, images_other],
        2 * total * columns * width,
    )
    caption_parts = dict(zip(caption_blocks, caption_parts))

    def hop(parts, near, f):
        return [parts[0, f]] + [swap(parts[h, f], near, h) for h in range(1, lax.axis_size(near))]

    def rounded(terms):
        total = terms[0]
        for term in terms[1:]:
            total = total + term.astype(f32)
        return total.astype(bf16)

    image_far = [rounded(hop(image_parts, "ilo", f)) for f in range(1, chi)]
    caption_far = [rounded(hop(caption_parts, "ihi", f)) for f in range(1, clo)]
    image_terms, caption_terms = hop(image_parts, "ilo", 0), hop(caption_parts, "ihi", 0)
    image_terms += [swap(image_far[f - 1], "chi", f) for f in range(1, chi)]
    caption_terms += [swap(caption_far[f - 1], "clo", f) for f in range(1, clo)]
    out = shape((rows, width), f32)
    caption_grad, image_grad = call(
        functools.partial(sum_kernel, (len(caption_terms), len(image_terms))),
        [out, out],
        caption_terms + image_terms,
        scratch=[pltpu.VMEM((rows, width), f32)] * 2 + [dma((2,))],
        out_space=HBM,
    )
    return (image_grad, caption_grad)


def split(count):
    low = 1 << ((count.bit_length() - 1) // 2)
    return count // low, low


def solution(mesh):
    ihi, ilo = split(mesh.shape["img"] // 2)
    chi, clo = split(mesh.shape["cap"])
    fine = Mesh(mesh.devices.reshape(ihi, ilo, 2, chi, clo), ("ihi", "ilo", "core", "chi", "clo"))
    by_image = P(("ihi", "ilo", "core", "chi", "clo"), None)
    by_caption = P(("chi", "clo", "ihi", "ilo", "core"), None)
    return jax.shard_map(
        local,
        mesh=fine,
        in_specs=(by_image, by_caption, by_image, by_caption),
        out_specs=(by_image, by_caption),
        check_vma=False,
    )
```

```python
import functools
import math

import jax
import jax.numpy as jnp
from jax import lax
from jax.experimental import pallas as pl
from jax.experimental.pallas import tpu as pltpu
from jax.sharding import Mesh, PartitionSpec as P

logit_gain = 3.0
ROW_AXES = ("ilo", "chi")
COL_AXES = ("core", "clo", "ihi")
ROW_STAGES = (("chi",), ("ilo",), ())
COL_STAGES = (("ihi",), ("clo",), ("core",))
ROW_ORDER = ("ihi", "ilo", "core", "chi", "clo")
COL_ORDER = ("chi", "clo", "ihi", "ilo", "core")
LANES = 128
PEAK_S, TOTAL_S, PEAK_T, TOTAL_T, INDEX = range(5)


def swap(value, axis, mask):
    size = lax.axis_size(axis)
    return lax.ppermute(value, axis, [(j, j ^ mask) for j in range(size)])


def partners(names, axes):
    sizes = [lax.axis_size(a) for a in names]
    strides = [math.prod(lax.axis_size(a) for a in axes[axes.index(name) + 1 :]) for name in names]
    result = []
    for mask in range(1, math.prod(sizes)):
        distance, rest = 0, mask
        for size, stride in zip(reversed(sizes), reversed(strides)):
            distance += rest % size * stride
            rest //= size
        result.append((mask, distance))
    return result


def lines_of(columns):
    count = columns[0].shape[0]
    lane = lax.broadcasted_iota(jnp.int32, (count, LANES), 1)
    wide = jnp.zeros((count, LANES), jnp.float32)
    for k, column in enumerate(columns):
        wide = jnp.where(lane == k, column, wide)
    spare = -count % LANES
    if spare:
        wide = jnp.concatenate([wide, jnp.zeros((spare, LANES), jnp.float32)], axis=0)
    return wide.T[:8, :count]


def columns_of(lines):
    count = lines.shape[1]
    spare = -count % LANES
    if spare:
        lines = jnp.concatenate([lines, jnp.zeros((8, spare), jnp.float32)], axis=1)
    tall = jnp.concatenate([lines, jnp.zeros((LANES - 8, count + spare), jnp.float32)], axis=0)
    return tall.T[:count]


def store_slots(ref, lines, rows):
    ref[...] = jnp.zeros_like(ref)
    for s in range(ref.shape[0]):
        ref[s, :, :rows] = lines[:, s * rows : (s + 1) * rows]


def load_slots(blocks, rows):
    return jnp.concatenate([block[:, :rows] for block in blocks], axis=1)


def owners(axes, order):
    sizes = [lax.axis_size(a) for a in axes]
    result = []
    for s in range(math.prod(sizes)):
        place = {a: lax.axis_index(a) for a in order}
        for axis, size in zip(reversed(axes), reversed(sizes)):
            place[axis] = place[axis] ^ (s % size)
            s //= size
        owner = 0
        for axis in order:
            owner = owner * lax.axis_size(axis) + place[axis]
        result.append(owner)
    return result


def joined(refs, columns=slice(None)):
    values = [ref[:, columns] for ref in refs]
    return values[0] if len(values) == 1 else jnp.concatenate(values, axis=0)


def copy_all(pairs, sems):
    copies = [pltpu.make_async_copy(src, dst, sems.at[k]) for k, (src, dst) in enumerate(pairs)]
    for copy in copies:
        copy.start()
    for copy in copies:
        copy.wait()


def pack_kernel(image_s, image_t, caption_s, caption_t, image, caption, sems):
    width = image_s.shape[1]
    copy_all(
        [
            (image_s, image.at[:, :width]),
            (image_t, image.at[:, width:]),
            (caption_s, caption.at[:, :width]),
            (caption_t, caption.at[:, width:]),
        ],
        sems,
    )


def duplicate_kernel(*refs):
    count = len(refs) // 2
    for value, out in zip(refs[:count], refs[count:]):
        out[...] = value[...]


def assemble_kernel(*refs):
    refs[-1][...] = joined(refs[:-1])


def window(refs, start, stop, columns):
    values, first = [], 0
    for ref in refs:
        low, high = max(start - first, 0), min(stop - first, ref.shape[0])
        if low < high:
            values.append(ref[low:high, columns])
        first += ref.shape[0]
    return values[0] if len(values) == 1 else jnp.concatenate(values, axis=0)


def logits(left, right, out):
    gain = logit_gain / math.sqrt(left.shape[1])
    out[...] = gain * lax.dot_general(left, right, (((1,), (1,)), ((), ())), preferred_element_type=jnp.float32)
    matrix = out[...]
    peak = jnp.max(matrix, axis=1, keepdims=True)
    columns = [peak, jnp.sum(jnp.exp(matrix - peak), axis=1, keepdims=True)]
    peak = jnp.max(matrix, axis=0, keepdims=True)
    return columns, [peak, jnp.sum(jnp.exp(matrix - peak), axis=0, keepdims=True)]


def stacked(lines):
    count = lines[0].shape[1]
    row = lax.broadcasted_iota(jnp.int32, (8, count), 0)
    result = jnp.zeros((8, count), jnp.float32)
    for k, line in enumerate(lines):
        result = jnp.where(row == k, line, result)
    return result


def head_kernel(n_img, rows, width, *refs):
    img_parts, cap_parts = refs[:n_img], refs[n_img:-4]
    student_ref, teacher_ref, row_ref, lines_ref = refs[-4:]
    count = student_ref.shape[1]
    columns, lines = [], []
    for part, out in ((slice(0, width), student_ref), (slice(width, None), teacher_ref)):
        more = logits(joined(img_parts, part), window(cap_parts, 0, count, part), out)
        columns, lines = columns + more[0], lines + more[1]
    store_slots(row_ref, lines_of(columns), rows)
    lines_ref[...] = stacked(lines)


def tail_kernel(n_img, start, rows, width, head_ref, lines_ref, *refs):
    img_parts, cap_parts = refs[:n_img], refs[n_img:-5]
    student_ref, teacher_ref, row_ref, col_ref, images = refs[-5:]
    stop = start + student_ref.shape[1]
    columns, lines = [], []
    for part, out in ((slice(0, width), student_ref), (slice(width, None), teacher_ref)):
        left = joined(img_parts, part)
        if out is student_ref:
            images[...] = left
        more = logits(left, window(cap_parts, start, stop, part), out)
        columns, lines = columns + more[0], lines + more[1]
    store_slots(row_ref, lines_of(columns), rows)
    store_slots(col_ref, jnp.concatenate([lines_ref[...], stacked(lines)], axis=1), rows)
    row = lax.broadcasted_iota(jnp.int32, (8, LANES), 0)
    lane = lax.broadcasted_iota(jnp.int32, (8, LANES), 1)
    for ref, axes, order in ((row_ref, ROW_AXES, ROW_ORDER), (col_ref, COL_AXES, COL_ORDER)):
        for s, owner in enumerate(owners(axes, order)):
            block = merged(head_ref[s], ref[s]) if ref is row_ref else ref[s]
            ref[s] = jnp.where(row == INDEX, (owner * rows + lane).astype(jnp.float32), block)


def merged(x, y):
    line = lax.broadcasted_iota(jnp.int32, x.shape, 0)
    student = line <= TOTAL_S
    x_peak = jnp.where(student, x[PEAK_S : PEAK_S + 1], x[PEAK_T : PEAK_T + 1])
    y_peak = jnp.where(student, y[PEAK_S : PEAK_S + 1], y[PEAK_T : PEAK_T + 1])
    peak = jnp.maximum(x_peak, y_peak)
    total = x * jnp.exp(x_peak - peak) + y * jnp.exp(y_peak - peak)
    both = jnp.where((line == PEAK_S) | (line == PEAK_T), peak, total)
    return jnp.where(line < INDEX, both, x)


def merged_blocks(mine, others, distances):
    blocks = [mine[s] for s in range(mine.shape[0])]
    for other, distance in zip(others, distances):
        blocks = [merged(block, other[s ^ distance]) for s, block in enumerate(blocks)]
    return blocks


def take(refs, plan):
    result = []
    for distances in plan:
        mine, others = refs[0], refs[1 : 1 + len(distances)]
        del refs[: 1 + len(distances)]
        result.append(merged_blocks(mine, others, distances))
    return result


def merge_kernel(plan, *refs):
    refs = list(refs)
    results = take(refs, plan)
    for out, blocks in zip(refs, results):
        for s, block in enumerate(blocks):
            out[s] = block


def tile_kernel(plan, n_cap, rows, width, *refs):
    refs = list(refs)
    student_refs, teacher_refs = (refs.pop(0), refs.pop(0)), (refs.pop(0), refs.pop(0))
    blocks = take(refs, plan)
    captions = [refs.pop(0) for _ in range(n_cap)]
    tile_ref, send_ref, first_ref = refs
    total, count = tile_ref.shape

    def finish(blocks):
        lines = load_slots(blocks, rows)
        line = lax.broadcasted_iota(jnp.int32, lines.shape, 0)
        lse_s = lines[PEAK_S : PEAK_S + 1] + jnp.log(lines[TOTAL_S : TOTAL_S + 1])
        lse_t = lines[PEAK_T : PEAK_T + 1] + jnp.log(lines[TOTAL_T : TOTAL_T + 1])
        return jnp.where(line == 0, lse_s, jnp.where(line == 1, lse_t, lines))

    down, across = columns_of(finish(blocks[0])), finish(blocks[1])
    step = 64 if total % 64 == 0 else total
    for r in range(0, total, step):
        at = slice(r, r + step)
        s, t = (jnp.concatenate([ref[at] for ref in pair], axis=1) for pair in (student_refs, teacher_refs))
        grad = 0.5 * (jnp.exp(s - down[at, 0:1]) + jnp.exp(s - across[0:1]))
        grad = grad - 0.25 * (jnp.exp(t - down[at, 1:2]) + jnp.exp(t - across[1:2]))
        grad = grad - jnp.where(down[at, INDEX : INDEX + 1] == across[INDEX : INDEX + 1], 0.5, 0.0)
        tile_ref[at] = grad.astype(jnp.bfloat16)
    send_ref[...] = tile_ref[:, count // 2 :]
    right = joined(captions, slice(0, width))
    part = jnp.dot(tile_ref[total - first_ref.shape[0] :], right, preferred_element_type=jnp.float32)
    first_ref[...] = part.astype(jnp.bfloat16)


def spread(part, outs):
    start = 0
    for out in outs:
        out[...] = part[start : start + out.shape[0]].astype(out.dtype)
        start += out.shape[0]


def image_kernel(width, tile_ref, *refs):
    parts = [ref for ref in refs if ref.dtype == jnp.bfloat16 and ref.shape[1] > width]
    right = joined(parts, slice(0, width))
    outs = refs[len(parts) :]
    count = sum(out.shape[0] for out in outs)
    spread(jnp.dot(tile_ref[:count], right, preferred_element_type=jnp.float32), outs)


def caption_kernel(tile_ref, tile_other, images, images_other, *outs):
    half = tile_other.shape[1]
    part = 0.0
    for tile, rows in ((tile_ref[:, :half], images[...]), (tile_other[...], images_other[...])):
        part = part + lax.dot_general(tile, rows, (((0,), (0,)), ((), ())), preferred_element_type=jnp.float32)
    spread(part, outs)


def sum_kernel(counts, *refs):
    refs = list(refs)
    terms = [[refs.pop(0) for _ in range(count)] for count in counts]
    outs, held, sems = refs[: len(counts)], refs[len(counts) : -1], refs[-1]
    copies = []
    for k, (group, out, here) in enumerate(zip(terms, outs, held)):
        total = group[0][...]
        for term in group[1:]:
            total = total + term[...].astype(jnp.float32)
        here[...] = total
        copies.append(pltpu.make_async_copy(here, out, sems.at[k]))
        copies[-1].start()
    for copy in copies:
        copy.wait()


VMEM, HBM = pltpu.VMEM, pltpu.HBM


def call(kernel, outs, args, flops=0, scratch=(), in_hbm=0, out_space=VMEM):
    moved = sum(math.prod(a.shape) * a.dtype.itemsize for a in list(args) + list(outs))
    spaces = [HBM] * in_hbm + [VMEM] * (len(args) - in_hbm)
    return pl.pallas_call(
        kernel,
        out_shape=[out_space(out.shape, out.dtype) for out in outs],
        in_specs=[pl.BlockSpec(memory_space=space) for space in spaces],
        out_specs=[pl.BlockSpec(memory_space=out_space)] * len(outs),
        scratch_shapes=scratch,
        compiler_params=pltpu.CompilerParams(vmem_limit_bytes=16 * 2**20),
        cost_estimate=pl.CostEstimate(flops=flops, bytes_accessed=moved, transcendentals=0),
    )(*(pltpu.with_memory_space_constraint(arg, space) for arg, space in zip(args, spaces)))


def after(value, *others):
    return lax.optimization_barrier((value, others))[0]


def local(image_student, caption_student, image_teacher, caption_teacher):
    ilo, chi, core, clo, ihi = (lax.axis_size(a) for a in ROW_AXES + COL_AXES)
    rows, width = image_student.shape
    depth = image_teacher.shape[1]
    assert rows <= LANES and core == 2 and chi > 1 and clo > 1
    n_img, n_cap = ilo * chi, core * ihi * clo
    total, columns = n_img * rows, n_cap * rows
    f32, bf16 = jnp.float32, jnp.bfloat16
    shape = jax.ShapeDtypeStruct
    dma = pltpu.SemaphoreType.DMA

    aligned = rows % 16 == 0
    if aligned:
        image, caption = call(
            pack_kernel,
            [shape((rows, width + depth), bf16)] * 2,
            [image_student, image_teacher, caption_student, caption_teacher],
            scratch=[dma((4,))],
            in_hbm=4,
        )
    else:
        image = jnp.concatenate([image_student, image_teacher], axis=1)
        caption = jnp.concatenate([caption_student, caption_teacher], axis=1)

    def assemble(parts):
        if not aligned:
            return jnp.concatenate(parts, axis=0)
        return call(assemble_kernel, [shape((len(parts) * rows, width + depth), bf16)], parts)[0]

    if aligned:
        image_near, caption_near = call(
            duplicate_kernel, [shape((rows, width + depth), bf16)] * 2, [image, caption]
        )
    else:
        image_near, caption_near = image, caption

    def gather(own, own_near, far_axis, near_axis):
        parts = {(0, c): swap(own, far_axis, c) if c else own for c in range(lax.axis_size(far_axis))}
        for h in range(1, lax.axis_size(near_axis)):
            parts.update({(h, c): swap(parts[0, c] if c else own_near, near_axis, h) for c in range(lax.axis_size(far_axis))})
        return parts

    img, cap = gather(image, image_near, "chi", "ilo"), gather(caption, caption_near, "clo", "ihi")
    early = [cap[h, 0] for h in range(ihi)]
    early = assemble([after(early[0], img[1, 0], img[0, 1])] + early[1:])
    late = [cap[h, c] for c in range(1, clo) for h in range(ihi)]
    late = assemble([after(late[0], img[1, 1])] + late[1:])
    img = [img[h, c] for h in range(ilo) for c in range(chi)]
    cap = [early, late, swap(early, "core", 1), swap(late, "core", 1)]
    if not aligned:
        img, cap = [assemble(img)], [assemble(cap)]

    row_shape, col_shape = shape((n_img, 8, LANES), f32), shape((n_cap, 8, LANES), f32)
    head = (columns - (cap[-1].shape[0] if aligned else rows)) // LANES * LANES
    ready = cap[:-1] if aligned else cap
    skipped = [part for k, part in enumerate(cap) if sum(p.shape[0] for p in cap[: k + 1]) <= head]
    needed = cap[len(skipped) :]
    start = head - sum(part.shape[0] for part in skipped)
    student, teacher, row_head, lines = call(
        functools.partial(head_kernel, len(img), rows, width),
        [shape((total, head), f32)] * 2 + [row_shape, shape((8, head), f32)],
        img + ready,
        2 * total * head * (width + depth),
    )
    student_tail, teacher_tail, row_stats, col_stats, images = call(
        functools.partial(tail_kernel, len(img), start, rows, width),
        [shape((total, columns - head), f32)] * 2 + [row_shape, col_shape, shape((total, width), bf16)],
        [row_head, lines] + img + needed,
        2 * total * (columns - head) * (width + depth),
    )

    images_other = swap(images, "core", 1)
    stats = [row_stats, col_stats]
    for row_names, col_names in zip(ROW_STAGES, COL_STAGES):
        plan, blocks = [], []
        for block, names, axes in zip(stats, (row_names, col_names), (ROW_AXES, COL_AXES)):
            others = partners(names, axes)
            plan.append([distance for _, distance in others])
            blocks += [block] + [swap(block, names, mask) for mask, _ in others]
        if col_names == COL_STAGES[0]:
            blocks[0] = after(blocks[0], images_other)
        if col_names != COL_STAGES[-1]:
            stats = call(functools.partial(merge_kernel, plan), [row_shape, col_shape], blocks)

    image_blocks = [(h, c) for h in range(ilo) for c in range(chi)]
    caption_blocks = [(h, c) for c in range(clo) for h in range(ihi)]

    def pieces(blocks):
        return [shape((rows, width), bf16 if h else f32) for h, _ in blocks]

    tile, tile_send, image_first = call(
        functools.partial(tile_kernel, plan, len(cap), rows, width),
        [shape((total, columns), bf16), shape((total, columns // 2), bf16), shape((rows, width), bf16)],
        [student, student_tail, teacher, teacher_tail] + blocks + cap,
        2 * rows * columns * width,
    )
    tile_other = swap(tile_send, "core", 1)

    image_parts = call(
        functools.partial(image_kernel, width),
        pieces(image_blocks)[:-1],
        [tile] + cap,
        2 * total * columns * width,
    )
    image_parts = dict(zip(image_blocks, list(image_parts) + [image_first]))
    caption_parts = call(
        caption_kernel,
        pieces(caption_blocks),
        [tile, tile_other, images, images_other],
        2 * total * columns * width,
    )
    caption_parts = dict(zip(caption_blocks, caption_parts))

    def hop(parts, near, f):
        return [parts[0, f]] + [swap(parts[h, f], near, h) for h in range(1, lax.axis_size(near))]

    def rounded(terms):
        total = terms[0]
        for term in terms[1:]:
            total = total + term.astype(f32)
        return total.astype(bf16)

    image_far = [rounded(hop(image_parts, "ilo", f)) for f in range(1, chi)]
    caption_far = [rounded(hop(caption_parts, "ihi", f)) for f in range(1, clo)]
    image_terms, caption_terms = hop(image_parts, "ilo", 0), hop(caption_parts, "ihi", 0)
    image_terms += [swap(image_far[f - 1], "chi", f) for f in range(1, chi)]
    caption_terms += [swap(caption_far[f - 1], "clo", f) for f in range(1, clo)]
    out = shape((rows, width), f32)
    caption_grad, image_grad = call(
        functools.partial(sum_kernel, (len(caption_terms), len(image_terms))),
        [out, out],
        caption_terms + image_terms,
        scratch=[pltpu.VMEM((rows, width), f32)] * 2 + [dma((2,))],
        out_space=HBM,
    )
    return (image_grad, caption_grad)


def split(count):
    low = 1 << ((count.bit_length() - 1) // 2)
    return count // low, low


def solution(mesh):
    ihi, ilo = split(mesh.shape["img"] // 2)
    chi, clo = split(mesh.shape["cap"])
    fine = Mesh(mesh.devices.reshape(ihi, ilo, 2, chi, clo), ("ihi", "ilo", "core", "chi", "clo"))
    by_image = P(("ihi", "ilo", "core", "chi", "clo"), None)
    by_caption = P(("chi", "clo", "ihi", "ilo", "core"), None)
    return jax.shard_map(
        local,
        mesh=fine,
        in_specs=(by_image, by_caption, by_image, by_caption),
        out_specs=(by_image, by_caption),
        check_vma=False,
    )
```

```python
import functools
import math

import jax
import jax.numpy as jnp
from jax import lax
from jax.experimental import pallas as pl
from jax.experimental.pallas import tpu as pltpu
from jax.sharding import Mesh, PartitionSpec as P

logit_gain = 3.0
ROW_AXES = ("ilo", "chi")
COL_AXES = ("core", "clo", "ihi")
ROW_STAGES = (("chi",), ("ilo",))
COL_STAGES = (("ihi", "clo"), ("core",))
ROW_ORDER = ("ihi", "ilo", "core", "chi", "clo")
COL_ORDER = ("chi", "clo", "ihi", "ilo", "core")
LANES = 128
PEAK_S, TOTAL_S, PEAK_T, TOTAL_T, INDEX = range(5)


def swap(value, axis, mask):
    size = lax.axis_size(axis)
    return lax.ppermute(value, axis, [(j, j ^ mask) for j in range(size)])


def partners(names, axes):
    sizes = [lax.axis_size(a) for a in names]
    strides = [math.prod(lax.axis_size(a) for a in axes[axes.index(name) + 1 :]) for name in names]
    result = []
    for mask in range(1, math.prod(sizes)):
        distance, rest = 0, mask
        for size, stride in zip(reversed(sizes), reversed(strides)):
            distance += rest % size * stride
            rest //= size
        result.append((mask, distance))
    return result


def lines_of(columns):
    count = columns[0].shape[0]
    lane = lax.broadcasted_iota(jnp.int32, (count, LANES), 1)
    wide = jnp.zeros((count, LANES), jnp.float32)
    for k, column in enumerate(columns):
        wide = jnp.where(lane == k, column, wide)
    spare = -count % LANES
    if spare:
        wide = jnp.concatenate([wide, jnp.zeros((spare, LANES), jnp.float32)], axis=0)
    return wide.T[:8, :count]


def columns_of(lines):
    count = lines.shape[1]
    spare = -count % LANES
    if spare:
        lines = jnp.concatenate([lines, jnp.zeros((8, spare), jnp.float32)], axis=1)
    tall = jnp.concatenate([lines, jnp.zeros((LANES - 8, count + spare), jnp.float32)], axis=0)
    return tall.T[:count]


def store_slots(ref, lines, rows):
    ref[...] = jnp.zeros_like(ref)
    for s in range(ref.shape[0]):
        ref[s, :, :rows] = lines[:, s * rows : (s + 1) * rows]


def load_slots(blocks, rows):
    return jnp.concatenate([block[:, :rows] for block in blocks], axis=1)


def owners(axes, order):
    sizes = [lax.axis_size(a) for a in axes]
    result = []
    for s in range(math.prod(sizes)):
        place = {a: lax.axis_index(a) for a in order}
        for axis, size in zip(reversed(axes), reversed(sizes)):
            place[axis] = place[axis] ^ (s % size)
            s //= size
        owner = 0
        for axis in order:
            owner = owner * lax.axis_size(axis) + place[axis]
        result.append(owner)
    return result


def joined(refs, columns=slice(None)):
    values = [ref[:, columns] for ref in refs]
    return values[0] if len(values) == 1 else jnp.concatenate(values, axis=0)


def copy_all(pairs, sems):
    copies = [pltpu.make_async_copy(src, dst, sems.at[k]) for k, (src, dst) in enumerate(pairs)]
    for copy in copies:
        copy.start()
    for copy in copies:
        copy.wait()


def pack_kernel(image_s, image_t, caption_s, caption_t, image, caption, sems):
    width = image_s.shape[1]
    copy_all(
        [
            (image_s, image.at[:, :width]),
            (image_t, image.at[:, width:]),
            (caption_s, caption.at[:, :width]),
            (caption_t, caption.at[:, width:]),
        ],
        sems,
    )


def duplicate_kernel(*refs):
    count = len(refs) // 2
    for value, out in zip(refs[:count], refs[count:]):
        out[...] = value[...]


def assemble_kernel(*refs):
    refs[-1][...] = joined(refs[:-1])


def window(refs, start, stop, columns):
    values, first = [], 0
    for ref in refs:
        low, high = max(start - first, 0), min(stop - first, ref.shape[0])
        if low < high:
            values.append(ref[low:high, columns])
        first += ref.shape[0]
    return values[0] if len(values) == 1 else jnp.concatenate(values, axis=0)


def logits(left, right, out):
    gain = logit_gain / math.sqrt(left.shape[1])
    out[...] = gain * lax.dot_general(left, right, (((1,), (1,)), ((), ())), preferred_element_type=jnp.float32)
    matrix = out[...]
    peak = jnp.max(matrix, axis=1, keepdims=True)
    columns = [peak, jnp.sum(jnp.exp(matrix - peak), axis=1, keepdims=True)]
    peak = jnp.max(matrix, axis=0, keepdims=True)
    return columns, [peak, jnp.sum(jnp.exp(matrix - peak), axis=0, keepdims=True)]


def stacked(lines):
    count = lines[0].shape[1]
    row = lax.broadcasted_iota(jnp.int32, (8, count), 0)
    result = jnp.zeros((8, count), jnp.float32)
    for k, line in enumerate(lines):
        result = jnp.where(row == k, line, result)
    return result


def head_kernel(n_img, rows, width, *refs):
    img_parts, cap_parts = refs[:n_img], refs[n_img:-4]
    student_ref, teacher_ref, row_ref, lines_ref = refs[-4:]
    count = student_ref.shape[1]
    columns, lines = [], []
    for part, out in ((slice(0, width), student_ref), (slice(width, None), teacher_ref)):
        more = logits(joined(img_parts, part), window(cap_parts, 0, count, part), out)
        columns, lines = columns + more[0], lines + more[1]
    store_slots(row_ref, lines_of(columns), rows)
    lines_ref[...] = stacked(lines)


def tail_kernel(n_img, start, rows, width, head_ref, lines_ref, *refs):
    img_parts, cap_parts = refs[:n_img], refs[n_img:-5]
    student_ref, teacher_ref, row_ref, col_ref, images = refs[-5:]
    stop = start + student_ref.shape[1]
    columns, lines = [], []
    for part, out in ((slice(0, width), student_ref), (slice(width, None), teacher_ref)):
        left = joined(img_parts, part)
        if out is student_ref:
            images[...] = left
        more = logits(left, window(cap_parts, start, stop, part), out)
        columns, lines = columns + more[0], lines + more[1]
    store_slots(row_ref, lines_of(columns), rows)
    store_slots(col_ref, jnp.concatenate([lines_ref[...], stacked(lines)], axis=1), rows)
    row = lax.broadcasted_iota(jnp.int32, (8, LANES), 0)
    lane = lax.broadcasted_iota(jnp.int32, (8, LANES), 1)
    for ref, axes, order in ((row_ref, ROW_AXES, ROW_ORDER), (col_ref, COL_AXES, COL_ORDER)):
        for s, owner in enumerate(owners(axes, order)):
            block = merged(head_ref[s], ref[s]) if ref is row_ref else ref[s]
            ref[s] = jnp.where(row == INDEX, (owner * rows + lane).astype(jnp.float32), block)


def merged(x, y):
    line = lax.broadcasted_iota(jnp.int32, x.shape, 0)
    student = line <= TOTAL_S
    x_peak = jnp.where(student, x[PEAK_S : PEAK_S + 1], x[PEAK_T : PEAK_T + 1])
    y_peak = jnp.where(student, y[PEAK_S : PEAK_S + 1], y[PEAK_T : PEAK_T + 1])
    peak = jnp.maximum(x_peak, y_peak)
    total = x * jnp.exp(x_peak - peak) + y * jnp.exp(y_peak - peak)
    both = jnp.where((line == PEAK_S) | (line == PEAK_T), peak, total)
    return jnp.where(line < INDEX, both, x)


def merged_blocks(mine, others, distances):
    blocks = [mine[s] for s in range(mine.shape[0])]
    for other, distance in zip(others, distances):
        blocks = [merged(block, other[s ^ distance]) for s, block in enumerate(blocks)]
    return blocks


def take(refs, plan):
    result = []
    for distances in plan:
        mine, others = refs[0], refs[1 : 1 + len(distances)]
        del refs[: 1 + len(distances)]
        result.append(merged_blocks(mine, others, distances))
    return result


def merge_kernel(plan, *refs):
    refs = list(refs)
    results = take(refs, plan)
    for out, blocks in zip(refs, results):
        for s, block in enumerate(blocks):
            out[s] = block


def tile_kernel(plan, n_cap, rows, width, *refs):
    refs = list(refs)
    student_refs, teacher_refs = (refs.pop(0), refs.pop(0)), (refs.pop(0), refs.pop(0))
    blocks = take(refs, plan)
    captions = [refs.pop(0) for _ in range(n_cap)]
    tile_ref, send_ref, first_ref = refs
    total, count = tile_ref.shape

    def finish(blocks):
        lines = load_slots(blocks, rows)
        line = lax.broadcasted_iota(jnp.int32, lines.shape, 0)
        lse_s = lines[PEAK_S : PEAK_S + 1] + jnp.log(lines[TOTAL_S : TOTAL_S + 1])
        lse_t = lines[PEAK_T : PEAK_T + 1] + jnp.log(lines[TOTAL_T : TOTAL_T + 1])
        return jnp.where(line == 0, lse_s, jnp.where(line == 1, lse_t, lines))

    down, across = columns_of(finish(blocks[0])), finish(blocks[1])
    step = 64 if total % 64 == 0 else total
    for r in range(0, total, step):
        at = slice(r, r + step)
        s, t = (jnp.concatenate([ref[at] for ref in pair], axis=1) for pair in (student_refs, teacher_refs))
        grad = 0.5 * (jnp.exp(s - down[at, 0:1]) + jnp.exp(s - across[0:1]))
        grad = grad - 0.25 * (jnp.exp(t - down[at, 1:2]) + jnp.exp(t - across[1:2]))
        grad = grad - jnp.where(down[at, INDEX : INDEX + 1] == across[INDEX : INDEX + 1], 0.5, 0.0)
        tile_ref[at] = grad.astype(jnp.bfloat16)
    send_ref[...] = tile_ref[:, count // 2 :]
    right = joined(captions, slice(0, width))
    part = jnp.dot(tile_ref[total - first_ref.shape[0] :], right, preferred_element_type=jnp.float32)
    first_ref[...] = part.astype(jnp.bfloat16)


def spread(part, outs):
    start = 0
    for out in outs:
        out[...] = part[start : start + out.shape[0]].astype(out.dtype)
        start += out.shape[0]


def image_kernel(width, tile_ref, *refs):
    parts = [ref for ref in refs if ref.dtype == jnp.bfloat16 and ref.shape[1] > width]
    right = joined(parts, slice(0, width))
    outs = refs[len(parts) :]
    count = sum(out.shape[0] for out in outs)
    spread(jnp.dot(tile_ref[:count], right, preferred_element_type=jnp.float32), outs)


def caption_kernel(tile_ref, tile_other, images, images_other, *outs):
    half = tile_other.shape[1]
    part = 0.0
    for tile, rows in ((tile_ref[:, :half], images[...]), (tile_other[...], images_other[...])):
        part = part + lax.dot_general(tile, rows, (((0,), (0,)), ((), ())), preferred_element_type=jnp.float32)
    spread(part, outs)


def sum_kernel(*refs):
    *terms, out, held, sem = refs
    total = terms[0][...]
    for term in terms[1:]:
        total = total + term[...].astype(jnp.float32)
    held[...] = total
    copy = pltpu.make_async_copy(held, out, sem)
    copy.start()
    copy.wait()


VMEM, HBM = pltpu.VMEM, pltpu.HBM


def call(kernel, outs, args, flops=0, scratch=(), in_hbm=0, out_space=VMEM):
    moved = sum(math.prod(a.shape) * a.dtype.itemsize for a in list(args) + list(outs))
    spaces = [HBM] * in_hbm + [VMEM] * (len(args) - in_hbm)
    return pl.pallas_call(
        kernel,
        out_shape=[out_space(out.shape, out.dtype) for out in outs],
        in_specs=[pl.BlockSpec(memory_space=space) for space in spaces],
        out_specs=[pl.BlockSpec(memory_space=out_space)] * len(outs),
        scratch_shapes=scratch,
        compiler_params=pltpu.CompilerParams(vmem_limit_bytes=16 * 2**20),
        cost_estimate=pl.CostEstimate(flops=flops, bytes_accessed=moved, transcendentals=0),
    )(*(pltpu.with_memory_space_constraint(arg, space) for arg, space in zip(args, spaces)))


def after(value, *others):
    return lax.optimization_barrier((value, others))[0]


def local(image_student, caption_student, image_teacher, caption_teacher):
    ilo, chi, core, clo, ihi = (lax.axis_size(a) for a in ROW_AXES + COL_AXES)
    rows, width = image_student.shape
    depth = image_teacher.shape[1]
    assert rows <= LANES and core == 2 and chi > 1 and clo > 1
    n_img, n_cap = ilo * chi, core * ihi * clo
    total, columns = n_img * rows, n_cap * rows
    f32, bf16 = jnp.float32, jnp.bfloat16
    shape = jax.ShapeDtypeStruct
    dma = pltpu.SemaphoreType.DMA

    aligned = rows % 16 == 0
    if aligned:
        image, caption = call(
            pack_kernel,
            [shape((rows, width + depth), bf16)] * 2,
            [image_student, image_teacher, caption_student, caption_teacher],
            scratch=[dma((4,))],
            in_hbm=4,
        )
    else:
        image = jnp.concatenate([image_student, image_teacher], axis=1)
        caption = jnp.concatenate([caption_student, caption_teacher], axis=1)

    def assemble(parts):
        if not aligned:
            return jnp.concatenate(parts, axis=0)
        return call(assemble_kernel, [shape((len(parts) * rows, width + depth), bf16)], parts)[0]

    if aligned:
        image_near, caption_near = call(
            duplicate_kernel, [shape((rows, width + depth), bf16)] * 2, [image, caption]
        )
    else:
        image_near, caption_near = image, caption

    def gather(own, own_near, far_axis, near_axis):
        parts = {(0, c): swap(own, far_axis, c) if c else own for c in range(lax.axis_size(far_axis))}
        for h in range(1, lax.axis_size(near_axis)):
            parts.update({(h, c): swap(parts[0, c] if c else own_near, near_axis, h) for c in range(lax.axis_size(far_axis))})
        return parts

    img, cap = gather(image, image_near, "chi", "ilo"), gather(caption, caption_near, "clo", "ihi")
    early = [cap[h, 0] for h in range(ihi)]
    early = assemble([after(early[0], img[1, 0], img[0, 1])] + early[1:])
    late = [cap[h, c] for c in range(1, clo) for h in range(ihi)]
    late = assemble([after(late[0], img[1, 1])] + late[1:])
    img = [img[h, c] for h in range(ilo) for c in range(chi)]
    cap = [early, late, swap(early, "core", 1), swap(late, "core", 1)]
    if not aligned:
        img, cap = [assemble(img)], [assemble(cap)]

    row_shape, col_shape = shape((n_img, 8, LANES), f32), shape((n_cap, 8, LANES), f32)
    head = (columns - (cap[-1].shape[0] if aligned else rows)) // LANES * LANES
    ready = cap[:-1] if aligned else cap
    skipped = [part for k, part in enumerate(cap) if sum(p.shape[0] for p in cap[: k + 1]) <= head]
    needed = cap[len(skipped) :]
    start = head - sum(part.shape[0] for part in skipped)
    student, teacher, row_head, lines = call(
        functools.partial(head_kernel, len(img), rows, width),
        [shape((total, head), f32)] * 2 + [row_shape, shape((8, head), f32)],
        img + ready,
        2 * total * head * (width + depth),
    )
    student_tail, teacher_tail, row_stats, col_stats, images = call(
        functools.partial(tail_kernel, len(img), start, rows, width),
        [shape((total, columns - head), f32)] * 2 + [row_shape, col_shape, shape((total, width), bf16)],
        [row_head, lines] + img + needed,
        2 * total * (columns - head) * (width + depth),
    )

    images_other = swap(images, "core", 1)
    stats = [row_stats, col_stats]
    for row_names, col_names in zip(ROW_STAGES, COL_STAGES):
        plan, blocks = [], []
        for block, names, axes in zip(stats, (row_names, col_names), (ROW_AXES, COL_AXES)):
            others = partners(names, axes)
            plan.append([distance for _, distance in others])
            blocks += [block] + [swap(block, names, mask) for mask, _ in others]
        if row_names != ROW_STAGES[-1]:
            blocks[0] = after(blocks[0], images_other)
            stats = call(functools.partial(merge_kernel, plan), [row_shape, col_shape], blocks)

    image_blocks = [(h, c) for h in range(ilo) for c in range(chi)]
    caption_blocks = [(h, c) for c in range(clo) for h in range(ihi)]

    def pieces(blocks):
        return [shape((rows, width), bf16 if h else f32) for h, _ in blocks]

    tile, tile_send, image_first = call(
        functools.partial(tile_kernel, plan, len(cap), rows, width),
        [shape((total, columns), bf16), shape((total, columns // 2), bf16), shape((rows, width), bf16)],
        [student, student_tail, teacher, teacher_tail] + blocks + cap,
        2 * rows * columns * width,
    )
    tile_other = swap(tile_send, "core", 1)

    image_parts = call(
        functools.partial(image_kernel, width),
        pieces(image_blocks)[:-1],
        [tile] + cap,
        2 * total * columns * width,
    )
    image_parts = dict(zip(image_blocks, list(image_parts) + [image_first]))
    caption_parts = call(
        caption_kernel,
        pieces(caption_blocks),
        [tile, tile_other, images, images_other],
        2 * total * columns * width,
    )
    caption_parts = dict(zip(caption_blocks, caption_parts))

    def hop(parts, near, f):
        return [parts[0, f]] + [swap(parts[h, f], near, h) for h in range(1, lax.axis_size(near))]

    def rounded(terms):
        total = terms[0]
        for term in terms[1:]:
            total = total + term.astype(f32)
        return total.astype(bf16)

    image_far = [rounded(hop(image_parts, "ilo", f)) for f in range(1, chi)]
    caption_far = [rounded(hop(caption_parts, "ihi", f)) for f in range(1, clo)]
    image_terms, caption_terms = hop(image_parts, "ilo", 0), hop(caption_parts, "ihi", 0)
    image_terms += [swap(image_far[f - 1], "chi", f) for f in range(1, chi)]
    caption_terms += [swap(caption_far[f - 1], "clo", f) for f in range(1, clo)]

    def total_of(terms):
        return call(
            sum_kernel,
            [shape((rows, width), f32)],
            terms,
            scratch=[pltpu.VMEM((rows, width), f32), dma],
            out_space=HBM,
        )[0]

    return (total_of(image_terms), total_of(caption_terms))


def split(count):
    low = 1 << ((count.bit_length() - 1) // 2)
    return count // low, low


def solution(mesh):
    ihi, ilo = split(mesh.shape["img"] // 2)
    chi, clo = split(mesh.shape["cap"])
    fine = Mesh(mesh.devices.reshape(ihi, ilo, 2, chi, clo), ("ihi", "ilo", "core", "chi", "clo"))
    by_image = P(("ihi", "ilo", "core", "chi", "clo"), None)
    by_caption = P(("chi", "clo", "ihi", "ilo", "core"), None)
    return jax.shard_map(
        local,
        mesh=fine,
        in_specs=(by_image, by_caption, by_image, by_caption),
        out_specs=(by_image, by_caption),
        check_vma=False,
    )
```

```python
import functools
import math

import jax
import jax.numpy as jnp
from jax import lax
from jax.experimental import pallas as pl
from jax.experimental.pallas import tpu as pltpu
from jax.sharding import Mesh, PartitionSpec as P

logit_gain = 3.0
ROW_AXES = ("ilo", "chi")
COL_AXES = ("core", "clo", "ihi")
ROW_STAGES = (("ilo",), ("chi",))
COL_STAGES = (("ihi", "clo"), ("core",))
ROW_ORDER = ("ihi", "ilo", "core", "chi", "clo")
COL_ORDER = ("chi", "clo", "ihi", "ilo", "core")
LANES = 128
PEAK_S, TOTAL_S, PEAK_T, TOTAL_T, INDEX = range(5)


def swap(value, axis, mask):
    size = lax.axis_size(axis)
    return lax.ppermute(value, axis, [(j, j ^ mask) for j in range(size)])


def partners(names, axes):
    sizes = [lax.axis_size(a) for a in names]
    strides = [math.prod(lax.axis_size(a) for a in axes[axes.index(name) + 1 :]) for name in names]
    result = []
    for mask in range(1, math.prod(sizes)):
        distance, rest = 0, mask
        for size, stride in zip(reversed(sizes), reversed(strides)):
            distance += rest % size * stride
            rest //= size
        result.append((mask, distance))
    return result


def lines_of(columns):
    count = columns[0].shape[0]
    lane = lax.broadcasted_iota(jnp.int32, (count, LANES), 1)
    wide = jnp.zeros((count, LANES), jnp.float32)
    for k, column in enumerate(columns):
        wide = jnp.where(lane == k, column, wide)
    spare = -count % LANES
    if spare:
        wide = jnp.concatenate([wide, jnp.zeros((spare, LANES), jnp.float32)], axis=0)
    return wide.T[:8, :count]


def columns_of(lines):
    count = lines.shape[1]
    spare = -count % LANES
    if spare:
        lines = jnp.concatenate([lines, jnp.zeros((8, spare), jnp.float32)], axis=1)
    tall = jnp.concatenate([lines, jnp.zeros((LANES - 8, count + spare), jnp.float32)], axis=0)
    return tall.T[:count]


def store_slots(ref, lines, rows):
    ref[...] = jnp.zeros_like(ref)
    for s in range(ref.shape[0]):
        ref[s, :, :rows] = lines[:, s * rows : (s + 1) * rows]


def load_slots(blocks, rows):
    return jnp.concatenate([block[:, :rows] for block in blocks], axis=1)


def owners(axes, order):
    sizes = [lax.axis_size(a) for a in axes]
    result = []
    for s in range(math.prod(sizes)):
        place = {a: lax.axis_index(a) for a in order}
        for axis, size in zip(reversed(axes), reversed(sizes)):
            place[axis] = place[axis] ^ (s % size)
            s //= size
        owner = 0
        for axis in order:
            owner = owner * lax.axis_size(axis) + place[axis]
        result.append(owner)
    return result


def joined(refs, columns=slice(None)):
    values = [ref[:, columns] for ref in refs]
    return values[0] if len(values) == 1 else jnp.concatenate(values, axis=0)


def copy_all(pairs, sems):
    copies = [pltpu.make_async_copy(src, dst, sems.at[k]) for k, (src, dst) in enumerate(pairs)]
    for copy in copies:
        copy.start()
    for copy in copies:
        copy.wait()


def pack_kernel(image_s, image_t, caption_s, caption_t, image, caption, sems):
    width = image_s.shape[1]
    copy_all(
        [
            (image_s, image.at[:, :width]),
            (image_t, image.at[:, width:]),
            (caption_s, caption.at[:, :width]),
            (caption_t, caption.at[:, width:]),
        ],
        sems,
    )


def duplicate_kernel(*refs):
    count = len(refs) // 2
    for value, out in zip(refs[:count], refs[count:]):
        out[...] = value[...]


def assemble_kernel(*refs):
    refs[-1][...] = joined(refs[:-1])


def window(refs, start, stop, columns):
    values, first = [], 0
    for ref in refs:
        low, high = max(start - first, 0), min(stop - first, ref.shape[0])
        if low < high:
            values.append(ref[low:high, columns])
        first += ref.shape[0]
    return values[0] if len(values) == 1 else jnp.concatenate(values, axis=0)


def logits(left, right, out):
    gain = logit_gain / math.sqrt(left.shape[1])
    out[...] = gain * lax.dot_general(left, right, (((1,), (1,)), ((), ())), preferred_element_type=jnp.float32)
    matrix = out[...]
    peak = jnp.max(matrix, axis=1, keepdims=True)
    columns = [peak, jnp.sum(jnp.exp(matrix - peak), axis=1, keepdims=True)]
    peak = jnp.max(matrix, axis=0, keepdims=True)
    return columns, [peak, jnp.sum(jnp.exp(matrix - peak), axis=0, keepdims=True)]


def stacked(lines):
    count = lines[0].shape[1]
    row = lax.broadcasted_iota(jnp.int32, (8, count), 0)
    result = jnp.zeros((8, count), jnp.float32)
    for k, line in enumerate(lines):
        result = jnp.where(row == k, line, result)
    return result


def head_kernel(n_img, rows, width, *refs):
    img_parts, cap_parts = refs[:n_img], refs[n_img:-4]
    student_ref, teacher_ref, row_ref, lines_ref = refs[-4:]
    count = student_ref.shape[1]
    columns, lines = [], []
    for part, out in ((slice(0, width), student_ref), (slice(width, None), teacher_ref)):
        more = logits(joined(img_parts, part), window(cap_parts, 0, count, part), out)
        columns, lines = columns + more[0], lines + more[1]
    store_slots(row_ref, lines_of(columns), rows)
    lines_ref[...] = stacked(lines)


def tail_kernel(n_img, start, rows, width, head_ref, lines_ref, *refs):
    img_parts, cap_parts = refs[:n_img], refs[n_img:-5]
    student_ref, teacher_ref, row_ref, col_ref, images = refs[-5:]
    stop = start + student_ref.shape[1]
    columns, lines = [], []
    for part, out in ((slice(0, width), student_ref), (slice(width, None), teacher_ref)):
        left = joined(img_parts, part)
        if out is student_ref:
            images[...] = left
        more = logits(left, window(cap_parts, start, stop, part), out)
        columns, lines = columns + more[0], lines + more[1]
    store_slots(row_ref, lines_of(columns), rows)
    store_slots(col_ref, jnp.concatenate([lines_ref[...], stacked(lines)], axis=1), rows)
    row = lax.broadcasted_iota(jnp.int32, (8, LANES), 0)
    lane = lax.broadcasted_iota(jnp.int32, (8, LANES), 1)
    for ref, axes, order in ((row_ref, ROW_AXES, ROW_ORDER), (col_ref, COL_AXES, COL_ORDER)):
        for s, owner in enumerate(owners(axes, order)):
            block = merged(head_ref[s], ref[s]) if ref is row_ref else ref[s]
            ref[s] = jnp.where(row == INDEX, (owner * rows + lane).astype(jnp.float32), block)


def merged(x, y):
    line = lax.broadcasted_iota(jnp.int32, x.shape, 0)
    student = line <= TOTAL_S
    x_peak = jnp.where(student, x[PEAK_S : PEAK_S + 1], x[PEAK_T : PEAK_T + 1])
    y_peak = jnp.where(student, y[PEAK_S : PEAK_S + 1], y[PEAK_T : PEAK_T + 1])
    peak = jnp.maximum(x_peak, y_peak)
    total = x * jnp.exp(x_peak - peak) + y * jnp.exp(y_peak - peak)
    both = jnp.where((line == PEAK_S) | (line == PEAK_T), peak, total)
    return jnp.where(line < INDEX, both, x)


def merged_blocks(mine, others, distances):
    blocks = [mine[s] for s in range(mine.shape[0])]
    for other, distance in zip(others, distances):
        blocks = [merged(block, other[s ^ distance]) for s, block in enumerate(blocks)]
    return blocks


def take(refs, plan):
    result = []
    for distances in plan:
        mine, others = refs[0], refs[1 : 1 + len(distances)]
        del refs[: 1 + len(distances)]
        result.append(merged_blocks(mine, others, distances))
    return result


def merge_kernel(plan, *refs):
    refs = list(refs)
    results = take(refs, plan)
    for out, blocks in zip(refs, results):
        for s, block in enumerate(blocks):
            out[s] = block


def tile_kernel(plan, n_cap, rows, width, *refs):
    refs = list(refs)
    student_refs, teacher_refs = (refs.pop(0), refs.pop(0)), (refs.pop(0), refs.pop(0))
    blocks = take(refs, plan)
    captions = [refs.pop(0) for _ in range(n_cap)]
    tile_ref, send_ref, first_ref = refs
    total, count = tile_ref.shape

    def finish(blocks):
        lines = load_slots(blocks, rows)
        line = lax.broadcasted_iota(jnp.int32, lines.shape, 0)
        lse_s = lines[PEAK_S : PEAK_S + 1] + jnp.log(lines[TOTAL_S : TOTAL_S + 1])
        lse_t = lines[PEAK_T : PEAK_T + 1] + jnp.log(lines[TOTAL_T : TOTAL_T + 1])
        return jnp.where(line == 0, lse_s, jnp.where(line == 1, lse_t, lines))

    down, across = columns_of(finish(blocks[0])), finish(blocks[1])
    step = 64 if total % 64 == 0 else total
    for r in range(0, total, step):
        at = slice(r, r + step)
        s, t = (jnp.concatenate([ref[at] for ref in pair], axis=1) for pair in (student_refs, teacher_refs))
        grad = 0.5 * (jnp.exp(s - down[at, 0:1]) + jnp.exp(s - across[0:1]))
        grad = grad - 0.25 * (jnp.exp(t - down[at, 1:2]) + jnp.exp(t - across[1:2]))
        grad = grad - jnp.where(down[at, INDEX : INDEX + 1] == across[INDEX : INDEX + 1], 0.5, 0.0)
        tile_ref[at] = grad.astype(jnp.bfloat16)
    send_ref[...] = tile_ref[:, count // 2 :]
    right = joined(captions, slice(0, width))
    part = jnp.dot(tile_ref[total - first_ref.shape[0] :], right, preferred_element_type=jnp.float32)
    first_ref[...] = part.astype(jnp.bfloat16)


def spread(part, outs):
    start = 0
    for out in outs:
        out[...] = part[start : start + out.shape[0]].astype(out.dtype)
        start += out.shape[0]


def image_kernel(width, tile_ref, *refs):
    parts = [ref for ref in refs if ref.dtype == jnp.bfloat16 and ref.shape[1] > width]
    right = joined(parts, slice(0, width))
    outs = refs[len(parts) :]
    count = sum(out.shape[0] for out in outs)
    spread(jnp.dot(tile_ref[:count], right, preferred_element_type=jnp.float32), outs)


def caption_kernel(tile_ref, tile_other, images, images_other, *outs):
    half = tile_other.shape[1]
    part = 0.0
    for tile, rows in ((tile_ref[:, :half], images[...]), (tile_other[...], images_other[...])):
        part = part + lax.dot_general(tile, rows, (((0,), (0,)), ((), ())), preferred_element_type=jnp.float32)
    spread(part, outs)


def sum_kernel(counts, *refs):
    refs = list(refs)
    terms = [[refs.pop(0) for _ in range(count)] for count in counts]
    outs, held, sems = refs[: len(counts)], refs[len(counts) : -1], refs[-1]
    copies = []
    for k, (group, out, here) in enumerate(zip(terms, outs, held)):
        total = group[0][...]
        for term in group[1:]:
            total = total + term[...].astype(jnp.float32)
        here[...] = total
        copies.append(pltpu.make_async_copy(here, out, sems.at[k]))
        copies[-1].start()
    for copy in copies:
        copy.wait()


VMEM, HBM = pltpu.VMEM, pltpu.HBM


def call(kernel, outs, args, flops=0, scratch=(), in_hbm=0, out_space=VMEM):
    moved = sum(math.prod(a.shape) * a.dtype.itemsize for a in list(args) + list(outs))
    spaces = [HBM] * in_hbm + [VMEM] * (len(args) - in_hbm)
    return pl.pallas_call(
        kernel,
        out_shape=[out_space(out.shape, out.dtype) for out in outs],
        in_specs=[pl.BlockSpec(memory_space=space) for space in spaces],
        out_specs=[pl.BlockSpec(memory_space=out_space)] * len(outs),
        scratch_shapes=scratch,
        compiler_params=pltpu.CompilerParams(vmem_limit_bytes=16 * 2**20),
        cost_estimate=pl.CostEstimate(flops=flops, bytes_accessed=moved, transcendentals=0),
    )(*(pltpu.with_memory_space_constraint(arg, space) for arg, space in zip(args, spaces)))


def after(value, *others):
    return lax.optimization_barrier((value, others))[0]


def local(image_student, caption_student, image_teacher, caption_teacher):
    ilo, chi, core, clo, ihi = (lax.axis_size(a) for a in ROW_AXES + COL_AXES)
    rows, width = image_student.shape
    depth = image_teacher.shape[1]
    assert rows <= LANES and core == 2 and chi > 1 and clo > 1
    n_img, n_cap = ilo * chi, core * ihi * clo
    total, columns = n_img * rows, n_cap * rows
    f32, bf16 = jnp.float32, jnp.bfloat16
    shape = jax.ShapeDtypeStruct
    dma = pltpu.SemaphoreType.DMA

    aligned = rows % 16 == 0
    if aligned:
        image, caption = call(
            pack_kernel,
            [shape((rows, width + depth), bf16)] * 2,
            [image_student, image_teacher, caption_student, caption_teacher],
            scratch=[dma((4,))],
            in_hbm=4,
        )
    else:
        image = jnp.concatenate([image_student, image_teacher], axis=1)
        caption = jnp.concatenate([caption_student, caption_teacher], axis=1)

    def assemble(parts):
        if not aligned:
            return jnp.concatenate(parts, axis=0)
        return call(assemble_kernel, [shape((len(parts) * rows, width + depth), bf16)], parts)[0]

    if aligned:
        image_near, caption_near = call(
            duplicate_kernel, [shape((rows, width + depth), bf16)] * 2, [image, caption]
        )
    else:
        image_near, caption_near = image, caption

    def gather(own, own_near, far_axis, near_axis):
        parts = {(0, c): swap(own, far_axis, c) if c else own for c in range(lax.axis_size(far_axis))}
        for h in range(1, lax.axis_size(near_axis)):
            parts.update({(h, c): swap(parts[0, c] if c else own_near, near_axis, h) for c in range(lax.axis_size(far_axis))})
        return parts

    img, cap = gather(image, image_near, "chi", "ilo"), gather(caption, caption_near, "clo", "ihi")
    early = [cap[h, 0] for h in range(ihi)]
    early = assemble([after(early[0], img[1, 0], img[0, 1])] + early[1:])
    late = [cap[h, c] for c in range(1, clo) for h in range(ihi)]
    late = assemble([after(late[0], img[1, 1])] + late[1:])
    img = [img[h, c] for h in range(ilo) for c in range(chi)]
    cap = [early, late, swap(early, "core", 1), swap(late, "core", 1)]
    if not aligned:
        img, cap = [assemble(img)], [assemble(cap)]

    row_shape, col_shape = shape((n_img, 8, LANES), f32), shape((n_cap, 8, LANES), f32)
    head = (columns - (cap[-1].shape[0] if aligned else rows)) // LANES * LANES
    ready = cap[:-1] if aligned else cap
    skipped = [part for k, part in enumerate(cap) if sum(p.shape[0] for p in cap[: k + 1]) <= head]
    needed = cap[len(skipped) :]
    start = head - sum(part.shape[0] for part in skipped)
    student, teacher, row_head, lines = call(
        functools.partial(head_kernel, len(img), rows, width),
        [shape((total, head), f32)] * 2 + [row_shape, shape((8, head), f32)],
        img + ready,
        2 * total * head * (width + depth),
    )
    student_tail, teacher_tail, row_stats, col_stats, images = call(
        functools.partial(tail_kernel, len(img), start, rows, width),
        [shape((total, columns - head), f32)] * 2 + [row_shape, col_shape, shape((total, width), bf16)],
        [row_head, lines] + img + needed,
        2 * total * (columns - head) * (width + depth),
    )

    images_other = swap(images, "core", 1)
    stats = [row_stats, col_stats]
    for row_names, col_names in zip(ROW_STAGES, COL_STAGES):
        plan, blocks = [], []
        for block, names, axes in zip(stats, (row_names, col_names), (ROW_AXES, COL_AXES)):
            others = partners(names, axes)
            plan.append([distance for _, distance in others])
            blocks += [block] + [swap(block, names, mask) for mask, _ in others]
        if row_names != ROW_STAGES[-1]:
            blocks[0] = after(blocks[0], images_other)
            stats = call(functools.partial(merge_kernel, plan), [row_shape, col_shape], blocks)

    image_blocks = [(h, c) for h in range(ilo) for c in range(chi)]
    caption_blocks = [(h, c) for c in range(clo) for h in range(ihi)]

    def pieces(blocks):
        return [shape((rows, width), bf16 if h else f32) for h, _ in blocks]

    tile, tile_send, image_first = call(
        functools.partial(tile_kernel, plan, len(cap), rows, width),
        [shape((total, columns), bf16), shape((total, columns // 2), bf16), shape((rows, width), bf16)],
        [student, student_tail, teacher, teacher_tail] + blocks + cap,
        2 * rows * columns * width,
    )
    tile_other = swap(tile_send, "core", 1)

    image_parts = call(
        functools.partial(image_kernel, width),
        pieces(image_blocks)[:-1],
        [tile] + cap,
        2 * total * columns * width,
    )
    image_parts = dict(zip(image_blocks, list(image_parts) + [image_first]))
    caption_parts = call(
        caption_kernel,
        pieces(caption_blocks),
        [tile, tile_other, images, images_other],
        2 * total * columns * width,
    )
    caption_parts = dict(zip(caption_blocks, caption_parts))

    def hop(parts, near, f):
        return [parts[0, f]] + [swap(parts[h, f], near, h) for h in range(1, lax.axis_size(near))]

    def rounded(terms):
        total = terms[0]
        for term in terms[1:]:
            total = total + term.astype(f32)
        return total.astype(bf16)

    image_far = [rounded(hop(image_parts, "ilo", f)) for f in range(1, chi)]
    caption_far = [rounded(hop(caption_parts, "ihi", f)) for f in range(1, clo)]
    image_terms = [image_parts[0, 0]]
    image_terms += [swap(after(image_parts[h, 0], image_far[0]), "ilo", h) for h in range(1, ilo)]
    caption_terms = hop(caption_parts, "ihi", 0)
    image_terms += [swap(image_far[f - 1], "chi", f) for f in range(1, chi)]
    caption_terms += [swap(caption_far[f - 1], "clo", f) for f in range(1, clo)]
    out = shape((rows, width), f32)
    caption_grad, image_grad = call(
        functools.partial(sum_kernel, (len(caption_terms), len(image_terms))),
        [out, out],
        caption_terms + image_terms,
        scratch=[pltpu.VMEM((rows, width), f32)] * 2 + [dma((2,))],
        out_space=HBM,
    )
    return (image_grad, caption_grad)


def split(count):
    low = 1 << ((count.bit_length() - 1) // 2)
    return count // low, low


def solution(mesh):
    ihi, ilo = split(mesh.shape["img"] // 2)
    chi, clo = split(mesh.shape["cap"])
    fine = Mesh(mesh.devices.reshape(ihi, ilo, 2, chi, clo), ("ihi", "ilo", "core", "chi", "clo"))
    by_image = P(("ihi", "ilo", "core", "chi", "clo"), None)
    by_caption = P(("chi", "clo", "ihi", "ilo", "core"), None)
    return jax.shard_map(
        local,
        mesh=fine,
        in_specs=(by_image, by_caption, by_image, by_caption),
        out_specs=(by_image, by_caption),
        check_vma=False,
    )
```

```python
import functools
import math

import jax
import jax.numpy as jnp
from jax import lax
from jax.experimental import pallas as pl
from jax.experimental.pallas import tpu as pltpu
from jax.sharding import Mesh, PartitionSpec as P

logit_gain = 3.0
ROW_AXES = ("ilo", "chi")
COL_AXES = ("core", "clo", "ihi")
ROW_STAGES = (("ilo",), ("chi",))
COL_STAGES = (("ihi", "clo"), ("core",))
ROW_ORDER = ("ihi", "ilo", "core", "chi", "clo")
COL_ORDER = ("chi", "clo", "ihi", "ilo", "core")
LANES = 128
PEAK_S, TOTAL_S, PEAK_T, TOTAL_T, INDEX = range(5)


def swap(value, axis, mask):
    size = lax.axis_size(axis)
    return lax.ppermute(value, axis, [(j, j ^ mask) for j in range(size)])


def partners(names, axes):
    sizes = [lax.axis_size(a) for a in names]
    strides = [math.prod(lax.axis_size(a) for a in axes[axes.index(name) + 1 :]) for name in names]
    result = []
    for mask in range(1, math.prod(sizes)):
        distance, rest = 0, mask
        for size, stride in zip(reversed(sizes), reversed(strides)):
            distance += rest % size * stride
            rest //= size
        result.append((mask, distance))
    return result


def lines_of(columns):
    count = columns[0].shape[0]
    lane = lax.broadcasted_iota(jnp.int32, (count, LANES), 1)
    wide = jnp.zeros((count, LANES), jnp.float32)
    for k, column in enumerate(columns):
        wide = jnp.where(lane == k, column, wide)
    spare = -count % LANES
    if spare:
        wide = jnp.concatenate([wide, jnp.zeros((spare, LANES), jnp.float32)], axis=0)
    return wide.T[:8, :count]


def columns_of(lines):
    count = lines.shape[1]
    spare = -count % LANES
    if spare:
        lines = jnp.concatenate([lines, jnp.zeros((8, spare), jnp.float32)], axis=1)
    tall = jnp.concatenate([lines, jnp.zeros((LANES - 8, count + spare), jnp.float32)], axis=0)
    return tall.T[:count]


def store_slots(ref, lines, rows):
    ref[...] = jnp.zeros_like(ref)
    for s in range(ref.shape[0]):
        ref[s, :, :rows] = lines[:, s * rows : (s + 1) * rows]


def load_slots(blocks, rows):
    return jnp.concatenate([block[:, :rows] for block in blocks], axis=1)


def owners(axes, order):
    sizes = [lax.axis_size(a) for a in axes]
    result = []
    for s in range(math.prod(sizes)):
        place = {a: lax.axis_index(a) for a in order}
        for axis, size in zip(reversed(axes), reversed(sizes)):
            place[axis] = place[axis] ^ (s % size)
            s //= size
        owner = 0
        for axis in order:
            owner = owner * lax.axis_size(axis) + place[axis]
        result.append(owner)
    return result


def joined(refs, columns=slice(None)):
    values = [ref[:, columns] for ref in refs]
    return values[0] if len(values) == 1 else jnp.concatenate(values, axis=0)


def copy_all(pairs, sems):
    copies = [pltpu.make_async_copy(src, dst, sems.at[k]) for k, (src, dst) in enumerate(pairs)]
    for copy in copies:
        copy.start()
    for copy in copies:
        copy.wait()


def pack_kernel(image_s, image_t, caption_s, caption_t, image, caption, sems):
    width = image_s.shape[1]
    copy_all(
        [
            (image_s, image.at[:, :width]),
            (image_t, image.at[:, width:]),
            (caption_s, caption.at[:, :width]),
            (caption_t, caption.at[:, width:]),
        ],
        sems,
    )


def duplicate_kernel(*refs):
    count = len(refs) // 2
    for value, out in zip(refs[:count], refs[count:]):
        out[...] = value[...]


def assemble_kernel(*refs):
    refs[-1][...] = joined(refs[:-1])


def window(refs, start, stop, columns):
    values, first = [], 0
    for ref in refs:
        low, high = max(start - first, 0), min(stop - first, ref.shape[0])
        if low < high:
            values.append(ref[low:high, columns])
        first += ref.shape[0]
    return values[0] if len(values) == 1 else jnp.concatenate(values, axis=0)


def logits(left, right, out):
    gain = logit_gain / math.sqrt(left.shape[1])
    out[...] = gain * lax.dot_general(left, right, (((1,), (1,)), ((), ())), preferred_element_type=jnp.float32)
    matrix = out[...]
    peak = jnp.max(matrix, axis=1, keepdims=True)
    columns = [peak, jnp.sum(jnp.exp(matrix - peak), axis=1, keepdims=True)]
    peak = jnp.max(matrix, axis=0, keepdims=True)
    return columns, [peak, jnp.sum(jnp.exp(matrix - peak), axis=0, keepdims=True)]


def stacked(lines):
    count = lines[0].shape[1]
    row = lax.broadcasted_iota(jnp.int32, (8, count), 0)
    result = jnp.zeros((8, count), jnp.float32)
    for k, line in enumerate(lines):
        result = jnp.where(row == k, line, result)
    return result


def head_kernel(n_img, rows, width, *refs):
    img_parts, cap_parts = refs[:n_img], refs[n_img:-5]
    student_ref, teacher_ref, row_ref, lines_ref, images = refs[-5:]
    count = student_ref.shape[1]
    columns, lines = [], []
    for part, out in ((slice(0, width), student_ref), (slice(width, None), teacher_ref)):
        left = joined(img_parts, part)
        if out is student_ref:
            images[...] = left
        more = logits(left, window(cap_parts, 0, count, part), out)
        columns, lines = columns + more[0], lines + more[1]
    store_slots(row_ref, lines_of(columns), rows)
    lines_ref[...] = stacked(lines)


def tail_kernel(n_img, start, rows, width, head_ref, lines_ref, images, *refs):
    img_parts, cap_parts = refs[:n_img], refs[n_img:-4]
    student_ref, teacher_ref, row_ref, col_ref = refs[-4:]
    stop = start + student_ref.shape[1]
    columns, lines = [], []
    for part, out in ((slice(0, width), student_ref), (slice(width, None), teacher_ref)):
        left = images[...] if out is student_ref else joined(img_parts, part)
        more = logits(left, window(cap_parts, start, stop, part), out)
        columns, lines = columns + more[0], lines + more[1]
    store_slots(row_ref, lines_of(columns), rows)
    store_slots(col_ref, jnp.concatenate([lines_ref[...], stacked(lines)], axis=1), rows)
    row = lax.broadcasted_iota(jnp.int32, (8, LANES), 0)
    lane = lax.broadcasted_iota(jnp.int32, (8, LANES), 1)
    for ref, axes, order in ((row_ref, ROW_AXES, ROW_ORDER), (col_ref, COL_AXES, COL_ORDER)):
        for s, owner in enumerate(owners(axes, order)):
            block = merged(head_ref[s], ref[s]) if ref is row_ref else ref[s]
            ref[s] = jnp.where(row == INDEX, (owner * rows + lane).astype(jnp.float32), block)


def merged(x, y):
    line = lax.broadcasted_iota(jnp.int32, x.shape, 0)
    student = line <= TOTAL_S
    x_peak = jnp.where(student, x[PEAK_S : PEAK_S + 1], x[PEAK_T : PEAK_T + 1])
    y_peak = jnp.where(student, y[PEAK_S : PEAK_S + 1], y[PEAK_T : PEAK_T + 1])
    peak = jnp.maximum(x_peak, y_peak)
    total = x * jnp.exp(x_peak - peak) + y * jnp.exp(y_peak - peak)
    both = jnp.where((line == PEAK_S) | (line == PEAK_T), peak, total)
    return jnp.where(line < INDEX, both, x)


def merged_blocks(mine, others, distances):
    blocks = [mine[s] for s in range(mine.shape[0])]
    for other, distance in zip(others, distances):
        blocks = [merged(block, other[s ^ distance]) for s, block in enumerate(blocks)]
    return blocks


def take(refs, plan):
    result = []
    for distances in plan:
        mine, others = refs[0], refs[1 : 1 + len(distances)]
        del refs[: 1 + len(distances)]
        result.append(merged_blocks(mine, others, distances))
    return result


def merge_kernel(plan, *refs):
    refs = list(refs)
    results = take(refs, plan)
    for out, blocks in zip(refs, results):
        for s, block in enumerate(blocks):
            out[s] = block


def tile_kernel(plan, n_cap, rows, width, *refs):
    refs = list(refs)
    student_refs, teacher_refs = (refs.pop(0), refs.pop(0)), (refs.pop(0), refs.pop(0))
    blocks = take(refs, plan)
    captions = [refs.pop(0) for _ in range(n_cap)]
    tile_ref, send_ref, first_ref = refs
    total, count = tile_ref.shape

    def finish(blocks):
        lines = load_slots(blocks, rows)
        line = lax.broadcasted_iota(jnp.int32, lines.shape, 0)
        lse_s = lines[PEAK_S : PEAK_S + 1] + jnp.log(lines[TOTAL_S : TOTAL_S + 1])
        lse_t = lines[PEAK_T : PEAK_T + 1] + jnp.log(lines[TOTAL_T : TOTAL_T + 1])
        return jnp.where(line == 0, lse_s, jnp.where(line == 1, lse_t, lines))

    down, across = columns_of(finish(blocks[0])), finish(blocks[1])
    step = 64 if total % 64 == 0 else total
    for r in range(0, total, step):
        at = slice(r, r + step)
        s, t = (jnp.concatenate([ref[at] for ref in pair], axis=1) for pair in (student_refs, teacher_refs))
        grad = 0.5 * (jnp.exp(s - down[at, 0:1]) + jnp.exp(s - across[0:1]))
        grad = grad - 0.25 * (jnp.exp(t - down[at, 1:2]) + jnp.exp(t - across[1:2]))
        grad = grad - jnp.where(down[at, INDEX : INDEX + 1] == across[INDEX : INDEX + 1], 0.5, 0.0)
        tile_ref[at] = grad.astype(jnp.bfloat16)
    send_ref[...] = tile_ref[:, count // 2 :]
    right = joined(captions, slice(0, width))
    part = jnp.dot(tile_ref[total - first_ref.shape[0] :], right, preferred_element_type=jnp.float32)
    first_ref[...] = part.astype(jnp.bfloat16)


def spread(part, outs):
    start = 0
    for out in outs:
        out[...] = part[start : start + out.shape[0]].astype(out.dtype)
        start += out.shape[0]


def image_kernel(width, tile_ref, *refs):
    parts = [ref for ref in refs if ref.dtype == jnp.bfloat16 and ref.shape[1] > width]
    right = joined(parts, slice(0, width))
    outs = refs[len(parts) :]
    count = sum(out.shape[0] for out in outs)
    spread(jnp.dot(tile_ref[:count], right, preferred_element_type=jnp.float32), outs)


def caption_kernel(tile_ref, tile_other, images, images_other, *outs):
    half = tile_other.shape[1]
    part = 0.0
    for tile, rows in ((tile_ref[:, :half], images[...]), (tile_other[...], images_other[...])):
        part = part + lax.dot_general(tile, rows, (((0,), (0,)), ((), ())), preferred_element_type=jnp.float32)
    spread(part, outs)


def sum_kernel(counts, *refs):
    refs = list(refs)
    terms = [[refs.pop(0) for _ in range(count)] for count in counts]
    outs, held, sems = refs[: len(counts)], refs[len(counts) : -1], refs[-1]
    copies = []
    for k, (group, out, here) in enumerate(zip(terms, outs, held)):
        total = group[0][...]
        for term in group[1:]:
            total = total + term[...].astype(jnp.float32)
        here[...] = total
        copies.append(pltpu.make_async_copy(here, out, sems.at[k]))
        copies[-1].start()
    for copy in copies:
        copy.wait()


VMEM, HBM = pltpu.VMEM, pltpu.HBM


def call(kernel, outs, args, flops=0, scratch=(), in_hbm=0, out_space=VMEM):
    moved = sum(math.prod(a.shape) * a.dtype.itemsize for a in list(args) + list(outs))
    spaces = [HBM] * in_hbm + [VMEM] * (len(args) - in_hbm)
    return pl.pallas_call(
        kernel,
        out_shape=[out_space(out.shape, out.dtype) for out in outs],
        in_specs=[pl.BlockSpec(memory_space=space) for space in spaces],
        out_specs=[pl.BlockSpec(memory_space=out_space)] * len(outs),
        scratch_shapes=scratch,
        compiler_params=pltpu.CompilerParams(vmem_limit_bytes=16 * 2**20),
        cost_estimate=pl.CostEstimate(flops=flops, bytes_accessed=moved, transcendentals=0),
    )(*(pltpu.with_memory_space_constraint(arg, space) for arg, space in zip(args, spaces)))


def after(value, *others):
    return lax.optimization_barrier((value, others))[0]


def local(image_student, caption_student, image_teacher, caption_teacher):
    ilo, chi, core, clo, ihi = (lax.axis_size(a) for a in ROW_AXES + COL_AXES)
    rows, width = image_student.shape
    depth = image_teacher.shape[1]
    assert rows <= LANES and core == 2 and chi > 1 and clo > 1
    n_img, n_cap = ilo * chi, core * ihi * clo
    total, columns = n_img * rows, n_cap * rows
    f32, bf16 = jnp.float32, jnp.bfloat16
    shape = jax.ShapeDtypeStruct
    dma = pltpu.SemaphoreType.DMA

    aligned = rows % 16 == 0
    if aligned:
        image, caption = call(
            pack_kernel,
            [shape((rows, width + depth), bf16)] * 2,
            [image_student, image_teacher, caption_student, caption_teacher],
            scratch=[dma((4,))],
            in_hbm=4,
        )
    else:
        image = jnp.concatenate([image_student, image_teacher], axis=1)
        caption = jnp.concatenate([caption_student, caption_teacher], axis=1)

    def assemble(parts):
        if not aligned:
            return jnp.concatenate(parts, axis=0)
        return call(assemble_kernel, [shape((len(parts) * rows, width + depth), bf16)], parts)[0]

    if aligned:
        image_near, caption_near = call(
            duplicate_kernel, [shape((rows, width + depth), bf16)] * 2, [image, caption]
        )
    else:
        image_near, caption_near = image, caption

    def gather(own, own_near, far_axis, near_axis):
        parts = {(0, c): swap(own, far_axis, c) if c else own for c in range(lax.axis_size(far_axis))}
        for h in range(1, lax.axis_size(near_axis)):
            parts.update({(h, c): swap(parts[0, c] if c else own_near, near_axis, h) for c in range(lax.axis_size(far_axis))})
        return parts

    img, cap = gather(image, image_near, "chi", "ilo"), gather(caption, caption_near, "clo", "ihi")
    early = [cap[h, 0] for h in range(ihi)]
    early = assemble([after(early[0], img[1, 0], img[0, 1])] + early[1:])
    late = [cap[h, c] for c in range(1, clo) for h in range(ihi)]
    late = assemble(late[:-1] + [after(late[-1], img[1, 1])])
    img = [img[h, c] for h in range(ilo) for c in range(chi)]
    cap = [early, late, swap(early, "core", 1), swap(late, "core", 1)]
    if not aligned:
        img, cap = [assemble(img)], [assemble(cap)]

    row_shape, col_shape = shape((n_img, 8, LANES), f32), shape((n_cap, 8, LANES), f32)
    head = (columns - (cap[-1].shape[0] if aligned else rows)) // LANES * LANES
    ready = cap[:-1] if aligned else cap
    skipped = [part for k, part in enumerate(cap) if sum(p.shape[0] for p in cap[: k + 1]) <= head]
    needed = cap[len(skipped) :]
    start = head - sum(part.shape[0] for part in skipped)
    student, teacher, row_head, lines, images = call(
        functools.partial(head_kernel, len(img), rows, width),
        [shape((total, head), f32)] * 2 + [row_shape, shape((8, head), f32), shape((total, width), bf16)],
        img + ready,
        2 * total * head * (width + depth),
    )
    student_tail, teacher_tail, row_stats, col_stats = call(
        functools.partial(tail_kernel, len(img), start, rows, width),
        [shape((total, columns - head), f32)] * 2 + [row_shape, col_shape],
        [row_head, lines, images] + img + needed,
        2 * total * (columns - head) * (width + depth),
    )

    images_other = swap(after(images, row_stats), "core", 1)
    stats = [row_stats, col_stats]
    for row_names, col_names in zip(ROW_STAGES, COL_STAGES):
        plan, blocks = [], []
        for block, names, axes in zip(stats, (row_names, col_names), (ROW_AXES, COL_AXES)):
            others = partners(names, axes)
            plan.append([distance for _, distance in others])
            blocks += [block] + [swap(block, names, mask) for mask, _ in others]
        if row_names != ROW_STAGES[-1]:
            blocks[0] = after(blocks[0], images_other)
            stats = call(functools.partial(merge_kernel, plan), [row_shape, col_shape], blocks)

    image_blocks = [(h, c) for h in range(ilo) for c in range(chi)]
    caption_blocks = [(h, c) for c in range(clo) for h in range(ihi)]

    def pieces(blocks):
        return [shape((rows, width), bf16 if h else f32) for h, _ in blocks]

    tile, tile_send, image_first = call(
        functools.partial(tile_kernel, plan, len(cap), rows, width),
        [shape((total, columns), bf16), shape((total, columns // 2), bf16), shape((rows, width), bf16)],
        [student, student_tail, teacher, teacher_tail] + blocks + cap,
        2 * rows * columns * width,
    )
    tile_other = swap(tile_send, "core", 1)

    image_parts = call(
        functools.partial(image_kernel, width),
        pieces(image_blocks)[:-1],
        [tile] + cap,
        2 * total * columns * width,
    )
    image_parts = dict(zip(image_blocks, list(image_parts) + [image_first]))
    caption_parts = call(
        caption_kernel,
        pieces(caption_blocks),
        [tile, tile_other, images, images_other],
        2 * total * columns * width,
    )
    caption_parts = dict(zip(caption_blocks, caption_parts))

    def hop(parts, near, f):
        return [parts[0, f]] + [swap(parts[h, f], near, h) for h in range(1, lax.axis_size(near))]

    def rounded(terms):
        total = terms[0]
        for term in terms[1:]:
            total = total + term.astype(f32)
        return total.astype(bf16)

    image_far = [rounded(hop(image_parts, "ilo", f)) for f in range(1, chi)]
    caption_far = [rounded(hop(caption_parts, "ihi", f)) for f in range(1, clo)]
    image_terms, caption_terms = hop(image_parts, "ilo", 0), hop(caption_parts, "ihi", 0)
    image_terms += [swap(image_far[f - 1], "chi", f) for f in range(1, chi)]
    caption_terms += [swap(caption_far[f - 1], "clo", f) for f in range(1, clo)]
    out = shape((rows, width), f32)
    caption_grad, image_grad = call(
        functools.partial(sum_kernel, (len(caption_terms), len(image_terms))),
        [out, out],
        caption_terms + image_terms,
        scratch=[pltpu.VMEM((rows, width), f32)] * 2 + [dma((2,))],
        out_space=HBM,
    )
    return (image_grad, caption_grad)


def split(count):
    low = 1 << ((count.bit_length() - 1) // 2)
    return count // low, low


def solution(mesh):
    ihi, ilo = split(mesh.shape["img"] // 2)
    chi, clo = split(mesh.shape["cap"])
    fine = Mesh(mesh.devices.reshape(ihi, ilo, 2, chi, clo), ("ihi", "ilo", "core", "chi", "clo"))
    by_image = P(("ihi", "ilo", "core", "chi", "clo"), None)
    by_caption = P(("chi", "clo", "ihi", "ilo", "core"), None)
    return jax.shard_map(
        local,
        mesh=fine,
        in_specs=(by_image, by_caption, by_image, by_caption),
        out_specs=(by_image, by_caption),
        check_vma=False,
    )
```

```python
import functools
import math

import jax
import jax.numpy as jnp
from jax import lax
from jax.experimental import pallas as pl
from jax.experimental.pallas import tpu as pltpu
from jax.sharding import Mesh, PartitionSpec as P

logit_gain = 3.0
ROW_AXES = ("ilo", "chi")
COL_AXES = ("core", "clo", "ihi")
ROW_STAGES = (("ilo",), ("chi",))
COL_STAGES = (("ihi", "clo"), ("core",))
ROW_ORDER = ("ihi", "ilo", "core", "chi", "clo")
COL_ORDER = ("chi", "clo", "ihi", "ilo", "core")
LANES = 128
SLOT_LINES = 4
LSE_S, LSE_T, INDEX = range(3)


def swap(value, axis, mask):
    size = lax.axis_size(axis)
    return lax.ppermute(value, axis, [(j, j ^ mask) for j in range(size)])


def partners(names, axes):
    sizes = [lax.axis_size(a) for a in names]
    strides = [math.prod(lax.axis_size(a) for a in axes[axes.index(name) + 1 :]) for name in names]
    result = []
    for mask in range(1, math.prod(sizes)):
        distance, rest = 0, mask
        for size, stride in zip(reversed(sizes), reversed(strides)):
            distance += rest % size * stride
            rest //= size
        result.append((mask, distance))
    return result


def lines_of(columns):
    count = columns[0].shape[0]
    lane = lax.broadcasted_iota(jnp.int32, (count, LANES), 1)
    wide = jnp.zeros((count, LANES), jnp.float32)
    for k, column in enumerate(columns):
        wide = jnp.where(lane == k, column, wide)
    spare = -count % LANES
    if spare:
        wide = jnp.concatenate([wide, jnp.zeros((spare, LANES), jnp.float32)], axis=0)
    return wide.T[:8, :count]


def columns_of(lines):
    count = lines.shape[1]
    spare = -count % LANES
    if spare:
        lines = jnp.concatenate([lines, jnp.zeros((8, spare), jnp.float32)], axis=1)
    tall = jnp.concatenate([lines, jnp.zeros((LANES - 8, count + spare), jnp.float32)], axis=0)
    return tall.T[:count]


def store_slots(ref, lines, rows):
    ref[...] = jnp.zeros_like(ref)
    for s in range(2 * ref.shape[0]):
        first = s % 2 * SLOT_LINES
        ref[s // 2, first : first + SLOT_LINES, :rows] = lines[:SLOT_LINES, s * rows : (s + 1) * rows]


def load_slots(blocks, rows):
    halves = [block[first : first + SLOT_LINES, :rows] for block in blocks for first in (0, SLOT_LINES)]
    return jnp.concatenate(halves, axis=1)


def owners(axes, order):
    sizes = [lax.axis_size(a) for a in axes]
    result = []
    for s in range(math.prod(sizes)):
        place = {a: lax.axis_index(a) for a in order}
        for axis, size in zip(reversed(axes), reversed(sizes)):
            place[axis] = place[axis] ^ (s % size)
            s //= size
        owner = 0
        for axis in order:
            owner = owner * lax.axis_size(axis) + place[axis]
        result.append(owner)
    return result


def joined(refs, columns=slice(None)):
    values = [ref[:, columns] for ref in refs]
    return values[0] if len(values) == 1 else jnp.concatenate(values, axis=0)


def copy_all(pairs, sems):
    copies = [pltpu.make_async_copy(src, dst, sems.at[k]) for k, (src, dst) in enumerate(pairs)]
    for copy in copies:
        copy.start()
    for copy in copies:
        copy.wait()


def pack_kernel(image_s, image_t, caption_s, caption_t, image, caption, sems):
    width = image_s.shape[1]
    copy_all(
        [
            (image_s, image.at[:, :width]),
            (image_t, image.at[:, width:]),
            (caption_s, caption.at[:, :width]),
            (caption_t, caption.at[:, width:]),
        ],
        sems,
    )


def duplicate_kernel(*refs):
    count = len(refs) // 2
    for value, out in zip(refs[:count], refs[count:]):
        out[...] = value[...]


def assemble_kernel(*refs):
    refs[-1][...] = joined(refs[:-1])


def window(refs, start, stop, columns):
    values, first = [], 0
    for ref in refs:
        low, high = max(start - first, 0), min(stop - first, ref.shape[0])
        if low < high:
            values.append(ref[low:high, columns])
        first += ref.shape[0]
    return values[0] if len(values) == 1 else jnp.concatenate(values, axis=0)


def logits(left, right, out):
    gain = logit_gain / math.sqrt(left.shape[1])
    out[...] = gain * lax.dot_general(left, right, (((1,), (1,)), ((), ())), preferred_element_type=jnp.float32)
    matrix = out[...]
    peak = jnp.max(matrix, axis=1, keepdims=True)
    columns = [peak, jnp.sum(jnp.exp(matrix - peak), axis=1, keepdims=True)]
    peak = jnp.max(matrix, axis=0, keepdims=True)
    return columns, [peak, jnp.sum(jnp.exp(matrix - peak), axis=0, keepdims=True)]


def stacked(lines):
    count = lines[0].shape[1]
    row = lax.broadcasted_iota(jnp.int32, (8, count), 0)
    result = jnp.zeros((8, count), jnp.float32)
    for k, line in enumerate(lines):
        result = jnp.where(row == k, line, result)
    return result


def head_kernel(n_img, rows, width, *refs):
    img_parts, cap_parts = refs[:n_img], refs[n_img:-5]
    student_ref, teacher_ref, row_ref, lines_ref, images = refs[-5:]
    count = student_ref.shape[1]
    columns, lines = [], []
    for part, out in ((slice(0, width), student_ref), (slice(width, None), teacher_ref)):
        left = joined(img_parts, part)
        if out is student_ref:
            images[...] = left
        more = logits(left, window(cap_parts, 0, count, part), out)
        columns, lines = columns + more[0], lines + more[1]
    store_slots(row_ref, lines_of(columns), rows)
    lines_ref[...] = stacked(lines)


def tail_kernel(n_img, start, rows, width, head_ref, lines_ref, images, *refs):
    img_parts, cap_parts = refs[:n_img], refs[n_img:-4]
    student_ref, teacher_ref, row_ref, col_ref = refs[-4:]
    stop = start + student_ref.shape[1]
    columns, lines = [], []
    for part, out in ((slice(0, width), student_ref), (slice(width, None), teacher_ref)):
        left = images[...] if out is student_ref else joined(img_parts, part)
        more = logits(left, window(cap_parts, start, stop, part), out)
        columns, lines = columns + more[0], lines + more[1]
    store_slots(row_ref, lines_of(columns), rows)
    store_slots(col_ref, jnp.concatenate([lines_ref[...], stacked(lines)], axis=1), rows)
    for k in range(row_ref.shape[0]):
        row_ref[k] = merged(head_ref[k], row_ref[k])


def merged(x, y):
    even = lax.broadcasted_iota(jnp.int32, x.shape, 0) % 2 == 0
    x_peak, y_peak = (jnp.where(even, value, pltpu.roll(value, 1, 0)) for value in (x, y))
    peak = jnp.maximum(x_peak, y_peak)
    total = x * jnp.exp(x_peak - peak) + y * jnp.exp(y_peak - peak)
    return jnp.where(even, peak, total)


def merged_blocks(mine, others, distances):
    blocks = [mine[k] for k in range(mine.shape[0])]
    for other, distance in zip(others, distances):
        terms = [other[k ^ (distance // 2)] for k in range(len(blocks))]
        if distance % 2:
            terms = [pltpu.roll(term, SLOT_LINES, 0) for term in terms]
        blocks = [merged(block, term) for block, term in zip(blocks, terms)]
    return blocks


def take(refs, plan):
    result = []
    for distances in plan:
        mine, others = refs[0], refs[1 : 1 + len(distances)]
        del refs[: 1 + len(distances)]
        result.append(merged_blocks(mine, others, distances))
    return result


def merge_kernel(plan, *refs):
    refs = list(refs)
    results = take(refs, plan)
    for out, blocks in zip(refs, results):
        for s, block in enumerate(blocks):
            out[s] = block


def tile_kernel(plan, n_cap, rows, width, *refs):
    refs = list(refs)
    student_refs, teacher_refs = (refs.pop(0), refs.pop(0)), (refs.pop(0), refs.pop(0))
    blocks = take(refs, plan)
    captions = [refs.pop(0) for _ in range(n_cap)]
    tile_ref, send_ref, first_ref = refs
    total, count = tile_ref.shape

    lane = lax.broadcasted_iota(jnp.int32, (8, LANES), 1)[:1, :rows]

    def finish(blocks, axes, order):
        lines = load_slots(blocks, rows)
        index = jnp.concatenate([owner * rows + lane for owner in owners(axes, order)], axis=1)
        lse_s, lse_t = lines[0:1] + jnp.log(lines[1:2]), lines[2:3] + jnp.log(lines[3:4])
        return stacked([lse_s, lse_t, index.astype(jnp.float32)])

    down = columns_of(finish(blocks[0], ROW_AXES, ROW_ORDER))
    across = finish(blocks[1], COL_AXES, COL_ORDER)
    step = 64 if total % 64 == 0 else total
    for r in range(0, total, step):
        at = slice(r, r + step)
        s, t = (jnp.concatenate([ref[at] for ref in pair], axis=1) for pair in (student_refs, teacher_refs))
        grad = 0.5 * (jnp.exp(s - down[at, 0:1]) + jnp.exp(s - across[0:1]))
        grad = grad - 0.25 * (jnp.exp(t - down[at, 1:2]) + jnp.exp(t - across[1:2]))
        grad = grad - jnp.where(down[at, INDEX : INDEX + 1] == across[INDEX : INDEX + 1], 0.5, 0.0)
        tile_ref[at] = grad.astype(jnp.bfloat16)
    send_ref[...] = tile_ref[:, count // 2 :]
    right = joined(captions, slice(0, width))
    part = jnp.dot(tile_ref[total - first_ref.shape[0] :], right, preferred_element_type=jnp.float32)
    first_ref[...] = part.astype(jnp.bfloat16)


def spread(part, outs):
    start = 0
    for out in outs:
        out[...] = part[start : start + out.shape[0]].astype(out.dtype)
        start += out.shape[0]


def image_kernel(width, tile_ref, *refs):
    parts = [ref for ref in refs if ref.dtype == jnp.bfloat16 and ref.shape[1] > width]
    right = joined(parts, slice(0, width))
    outs = refs[len(parts) :]
    count = sum(out.shape[0] for out in outs)
    spread(jnp.dot(tile_ref[:count], right, preferred_element_type=jnp.float32), outs)


def caption_kernel(tile_ref, tile_other, images, images_other, *outs):
    half = tile_other.shape[1]
    part = 0.0
    for tile, rows in ((tile_ref[:, :half], images[...]), (tile_other[...], images_other[...])):
        part = part + lax.dot_general(tile, rows, (((0,), (0,)), ((), ())), preferred_element_type=jnp.float32)
    spread(part, outs)


def sum_kernel(counts, *refs):
    refs = list(refs)
    terms = [[refs.pop(0) for _ in range(count)] for count in counts]
    outs, held, sems = refs[: len(counts)], refs[len(counts) : -1], refs[-1]
    copies = []
    for k, (group, out, here) in enumerate(zip(terms, outs, held)):
        total = group[0][...]
        for term in group[1:]:
            total = total + term[...].astype(jnp.float32)
        here[...] = total
        copies.append(pltpu.make_async_copy(here, out, sems.at[k]))
        copies[-1].start()
    for copy in copies:
        copy.wait()


VMEM, HBM = pltpu.VMEM, pltpu.HBM


def call(kernel, outs, args, flops=0, scratch=(), in_hbm=0, out_space=VMEM):
    moved = sum(math.prod(a.shape) * a.dtype.itemsize for a in list(args) + list(outs))
    spaces = [HBM] * in_hbm + [VMEM] * (len(args) - in_hbm)
    return pl.pallas_call(
        kernel,
        out_shape=[out_space(out.shape, out.dtype) for out in outs],
        in_specs=[pl.BlockSpec(memory_space=space) for space in spaces],
        out_specs=[pl.BlockSpec(memory_space=out_space)] * len(outs),
        scratch_shapes=scratch,
        compiler_params=pltpu.CompilerParams(vmem_limit_bytes=16 * 2**20),
        cost_estimate=pl.CostEstimate(flops=flops, bytes_accessed=moved, transcendentals=0),
    )(*(pltpu.with_memory_space_constraint(arg, space) for arg, space in zip(args, spaces)))


def after(value, *others):
    return lax.optimization_barrier((value, others))[0]


def local(image_student, caption_student, image_teacher, caption_teacher):
    ilo, chi, core, clo, ihi = (lax.axis_size(a) for a in ROW_AXES + COL_AXES)
    rows, width = image_student.shape
    depth = image_teacher.shape[1]
    assert rows <= LANES and core == 2 and chi > 1 and clo > 1
    n_img, n_cap = ilo * chi, core * ihi * clo
    total, columns = n_img * rows, n_cap * rows
    f32, bf16 = jnp.float32, jnp.bfloat16
    shape = jax.ShapeDtypeStruct
    dma = pltpu.SemaphoreType.DMA

    aligned = rows % 16 == 0
    if aligned:
        image, caption = call(
            pack_kernel,
            [shape((rows, width + depth), bf16)] * 2,
            [image_student, image_teacher, caption_student, caption_teacher],
            scratch=[dma((4,))],
            in_hbm=4,
        )
    else:
        image = jnp.concatenate([image_student, image_teacher], axis=1)
        caption = jnp.concatenate([caption_student, caption_teacher], axis=1)

    def assemble(parts):
        if not aligned:
            return jnp.concatenate(parts, axis=0)
        return call(assemble_kernel, [shape((len(parts) * rows, width + depth), bf16)], parts)[0]

    if aligned:
        image_near, caption_near = call(
            duplicate_kernel, [shape((rows, width + depth), bf16)] * 2, [image, caption]
        )
    else:
        image_near, caption_near = image, caption

    def gather(own, own_near, far_axis, near_axis):
        parts = {(0, c): swap(own, far_axis, c) if c else own for c in range(lax.axis_size(far_axis))}
        for h in range(1, lax.axis_size(near_axis)):
            parts.update({(h, c): swap(parts[0, c] if c else own_near, near_axis, h) for c in range(lax.axis_size(far_axis))})
        return parts

    img, cap = gather(image, image_near, "chi", "ilo"), gather(caption, caption_near, "clo", "ihi")
    early = [cap[h, 0] for h in range(ihi)]
    early = assemble([after(early[0], img[1, 0], img[0, 1])] + early[1:])
    late = [cap[h, c] for c in range(1, clo) for h in range(ihi)]
    late = assemble(late[:-1] + [after(late[-1], img[1, 1])])
    img = [img[h, c] for h in range(ilo) for c in range(chi)]
    cap = [early, late, swap(early, "core", 1), swap(late, "core", 1)]
    if not aligned:
        img, cap = [assemble(img)], [assemble(cap)]

    row_shape, col_shape = shape((n_img // 2, 8, LANES), f32), shape((n_cap // 2, 8, LANES), f32)
    head = (columns - (cap[-1].shape[0] if aligned else rows)) // LANES * LANES
    ready = cap[:-1] if aligned else cap
    skipped = [part for k, part in enumerate(cap) if sum(p.shape[0] for p in cap[: k + 1]) <= head]
    needed = cap[len(skipped) :]
    start = head - sum(part.shape[0] for part in skipped)
    student, teacher, row_head, lines, images = call(
        functools.partial(head_kernel, len(img), rows, width),
        [shape((total, head), f32)] * 2 + [row_shape, shape((8, head), f32), shape((total, width), bf16)],
        img + ready,
        2 * total * head * (width + depth),
    )
    student_tail, teacher_tail, row_stats, col_stats = call(
        functools.partial(tail_kernel, len(img), start, rows, width),
        [shape((total, columns - head), f32)] * 2 + [row_shape, col_shape],
        [row_head, lines, images] + img + needed,
        2 * total * (columns - head) * (width + depth),
    )

    images_other = swap(after(images, row_stats), "core", 1)
    stats = [row_stats, col_stats]
    for row_names, col_names in zip(ROW_STAGES, COL_STAGES):
        plan, blocks = [], []
        for block, names, axes in zip(stats, (row_names, col_names), (ROW_AXES, COL_AXES)):
            others = partners(names, axes)
            plan.append([distance for _, distance in others])
            blocks += [block] + [swap(block, names, mask) for mask, _ in others]
        if row_names != ROW_STAGES[-1]:
            blocks[0] = after(blocks[0], images_other)
            stats = call(functools.partial(merge_kernel, plan), [row_shape, col_shape], blocks)

    image_blocks = [(h, c) for h in range(ilo) for c in range(chi)]
    caption_blocks = [(h, c) for c in range(clo) for h in range(ihi)]

    def pieces(blocks):
        return [shape((rows, width), bf16 if h else f32) for h, _ in blocks]

    tile, tile_send, image_first = call(
        functools.partial(tile_kernel, plan, len(cap), rows, width),
        [shape((total, columns), bf16), shape((total, columns // 2), bf16), shape((rows, width), bf16)],
        [student, student_tail, teacher, teacher_tail] + blocks + cap,
        2 * rows * columns * width,
    )
    tile_other = swap(tile_send, "core", 1)

    image_parts = call(
        functools.partial(image_kernel, width),
        pieces(image_blocks)[:-1],
        [tile] + cap,
        2 * total * columns * width,
    )
    image_parts = dict(zip(image_blocks, list(image_parts) + [image_first]))
    caption_parts = call(
        caption_kernel,
        pieces(caption_blocks),
        [tile, tile_other, images, images_other],
        2 * total * columns * width,
    )
    caption_parts = dict(zip(caption_blocks, caption_parts))

    def hop(parts, near, f):
        return [parts[0, f]] + [swap(parts[h, f], near, h) for h in range(1, lax.axis_size(near))]

    def rounded(terms):
        total = terms[0]
        for term in terms[1:]:
            total = total + term.astype(f32)
        return total.astype(bf16)

    image_far = [rounded(hop(image_parts, "ilo", f)) for f in range(1, chi)]
    caption_far = [rounded(hop(caption_parts, "ihi", f)) for f in range(1, clo)]
    image_terms, caption_terms = hop(image_parts, "ilo", 0), hop(caption_parts, "ihi", 0)
    image_terms += [swap(image_far[f - 1], "chi", f) for f in range(1, chi)]
    caption_terms += [swap(caption_far[f - 1], "clo", f) for f in range(1, clo)]
    out = shape((rows, width), f32)
    caption_grad, image_grad = call(
        functools.partial(sum_kernel, (len(caption_terms), len(image_terms))),
        [out, out],
        caption_terms + image_terms,
        scratch=[pltpu.VMEM((rows, width), f32)] * 2 + [dma((2,))],
        out_space=HBM,
    )
    return (image_grad, caption_grad)


def split(count):
    low = 1 << ((count.bit_length() - 1) // 2)
    return count // low, low


def solution(mesh):
    ihi, ilo = split(mesh.shape["img"] // 2)
    chi, clo = split(mesh.shape["cap"])
    fine = Mesh(mesh.devices.reshape(ihi, ilo, 2, chi, clo), ("ihi", "ilo", "core", "chi", "clo"))
    by_image = P(("ihi", "ilo", "core", "chi", "clo"), None)
    by_caption = P(("chi", "clo", "ihi", "ilo", "core"), None)
    return jax.shard_map(
        local,
        mesh=fine,
        in_specs=(by_image, by_caption, by_image, by_caption),
        out_specs=(by_image, by_caption),
        check_vma=False,
    )
```

```python
import functools
import math

import jax
import jax.numpy as jnp
from jax import lax
from jax.experimental import pallas as pl
from jax.experimental.pallas import tpu as pltpu
from jax.sharding import Mesh, PartitionSpec as P

logit_gain = 3.0
ROW_AXES = ("ilo", "chi")
COL_AXES = ("core", "clo", "ihi")
ROW_STAGES = (("ilo",), ("chi",))
COL_STAGES = (("ihi", "clo"), ("core",))
ROW_ORDER = ("ihi", "ilo", "core", "chi", "clo")
COL_ORDER = ("chi", "clo", "ihi", "ilo", "core")
LANES = 128
SLOT_LINES = 4
SCALE_S, SCALE_T, INDEX = range(3)


def swap(value, axis, mask):
    size = lax.axis_size(axis)
    return lax.ppermute(value, axis, [(j, j ^ mask) for j in range(size)])


def partners(names, axes):
    sizes = [lax.axis_size(a) for a in names]
    strides = [math.prod(lax.axis_size(a) for a in axes[axes.index(name) + 1 :]) for name in names]
    result = []
    for mask in range(1, math.prod(sizes)):
        distance, rest = 0, mask
        for size, stride in zip(reversed(sizes), reversed(strides)):
            distance += rest % size * stride
            rest //= size
        result.append((mask, distance))
    return result


def lines_of(columns):
    count = columns[0].shape[0]
    lane = lax.broadcasted_iota(jnp.int32, (count, LANES), 1)
    wide = jnp.zeros((count, LANES), jnp.float32)
    for k, column in enumerate(columns):
        wide = jnp.where(lane == k, column, wide)
    spare = -count % LANES
    if spare:
        wide = jnp.concatenate([wide, jnp.zeros((spare, LANES), jnp.float32)], axis=0)
    return wide.T[:8, :count]


def columns_of(lines):
    count = lines.shape[1]
    spare = -count % LANES
    if spare:
        lines = jnp.concatenate([lines, jnp.zeros((8, spare), jnp.float32)], axis=1)
    tall = jnp.concatenate([lines, jnp.zeros((LANES - 8, count + spare), jnp.float32)], axis=0)
    return tall.T[:count]


def store_slots(ref, lines, rows):
    ref[...] = jnp.zeros_like(ref)
    for s in range(2 * ref.shape[0]):
        first = s % 2 * SLOT_LINES
        ref[s // 2, first : first + SLOT_LINES, :rows] = lines[:SLOT_LINES, s * rows : (s + 1) * rows]


def load_slots(blocks, rows):
    halves = [block[first : first + SLOT_LINES, :rows] for block in blocks for first in (0, SLOT_LINES)]
    return jnp.concatenate(halves, axis=1)


def owners(axes, order):
    sizes = [lax.axis_size(a) for a in axes]
    result = []
    for s in range(math.prod(sizes)):
        place = {a: lax.axis_index(a) for a in order}
        for axis, size in zip(reversed(axes), reversed(sizes)):
            place[axis] = place[axis] ^ (s % size)
            s //= size
        owner = 0
        for axis in order:
            owner = owner * lax.axis_size(axis) + place[axis]
        result.append(owner)
    return result


def joined(refs, columns=slice(None)):
    values = [ref[:, columns] for ref in refs]
    return values[0] if len(values) == 1 else jnp.concatenate(values, axis=0)


def copy_all(pairs, sems):
    copies = [pltpu.make_async_copy(src, dst, sems.at[k]) for k, (src, dst) in enumerate(pairs)]
    for copy in copies:
        copy.start()
    for copy in copies:
        copy.wait()


def pack_kernel(image_s, image_t, caption_s, caption_t, image, caption, sems):
    width = image_s.shape[1]
    copy_all(
        [
            (image_s, image.at[:, :width]),
            (image_t, image.at[:, width:]),
            (caption_s, caption.at[:, :width]),
            (caption_t, caption.at[:, width:]),
        ],
        sems,
    )


def duplicate_kernel(*refs):
    count = len(refs) // 2
    for value, out in zip(refs[:count], refs[count:]):
        out[...] = value[...]


def assemble_kernel(*refs):
    refs[-1][...] = joined(refs[:-1])


def window(refs, start, stop, columns):
    values, first = [], 0
    for ref in refs:
        low, high = max(start - first, 0), min(stop - first, ref.shape[0])
        if low < high:
            values.append(ref[low:high, columns])
        first += ref.shape[0]
    return values[0] if len(values) == 1 else jnp.concatenate(values, axis=0)


def logits(left, right, out):
    gain = logit_gain / math.sqrt(left.shape[1])
    out[...] = gain * lax.dot_general(left, right, (((1,), (1,)), ((), ())), preferred_element_type=jnp.float32)
    matrix = out[...]
    peak = jnp.max(matrix, axis=1, keepdims=True)
    columns = [peak, jnp.sum(jnp.exp(matrix - peak), axis=1, keepdims=True)]
    peak = jnp.max(matrix, axis=0, keepdims=True)
    return columns, [peak, jnp.sum(jnp.exp(matrix - peak), axis=0, keepdims=True)]


def stacked(lines):
    count = lines[0].shape[1]
    row = lax.broadcasted_iota(jnp.int32, (8, count), 0)
    result = jnp.zeros((8, count), jnp.float32)
    for k, line in enumerate(lines):
        result = jnp.where(row == k, line, result)
    return result


def head_kernel(n_img, rows, width, *refs):
    *parts, student_ref, teacher_ref, row_ref, lines_ref, images = refs
    cap_parts, img_parts = parts[:-n_img], parts[-n_img:]
    count = student_ref.shape[1]
    columns, lines = [], []
    for part, out in ((slice(0, width), student_ref), (slice(width, None), teacher_ref)):
        left = joined(img_parts, part)
        if out is student_ref:
            images[...] = left
        more = logits(left, window(cap_parts, 0, count, part), out)
        columns, lines = columns + more[0], lines + more[1]
    store_slots(row_ref, lines_of(columns), rows)
    lines_ref[...] = stacked(lines)


def tail_kernel(n_img, start, rows, width, head_ref, lines_ref, images, *refs):
    img_parts, cap_parts = refs[:n_img], refs[n_img:-4]
    student_ref, teacher_ref, row_ref, col_ref = refs[-4:]
    stop = start + student_ref.shape[1]
    columns, lines = [], []
    for part, out in ((slice(0, width), student_ref), (slice(width, None), teacher_ref)):
        left = images[...] if out is student_ref else joined(img_parts, part)
        more = logits(left, window(cap_parts, start, stop, part), out)
        columns, lines = columns + more[0], lines + more[1]
    store_slots(row_ref, lines_of(columns), rows)
    store_slots(col_ref, jnp.concatenate([lines_ref[...], stacked(lines)], axis=1), rows)
    for k in range(row_ref.shape[0]):
        row_ref[k] = merged(head_ref[k], row_ref[k])


def merged(x, y):
    even = lax.broadcasted_iota(jnp.int32, x.shape, 0) % 2 == 0
    x_peak, y_peak = (jnp.where(even, value, pltpu.roll(value, 1, 0)) for value in (x, y))
    peak = jnp.maximum(x_peak, y_peak)
    total = x * jnp.exp(x_peak - peak) + y * jnp.exp(y_peak - peak)
    return jnp.where(even, peak, total)


def merged_blocks(mine, others, distances):
    blocks = [mine[k] for k in range(mine.shape[0])]
    for other, distance in zip(others, distances):
        terms = [other[k ^ (distance // 2)] for k in range(len(blocks))]
        if distance % 2:
            terms = [pltpu.roll(term, SLOT_LINES, 0) for term in terms]
        blocks = [merged(block, term) for block, term in zip(blocks, terms)]
    return blocks


def take(refs, plan):
    result = []
    for distances in plan:
        mine, others = refs[0], refs[1 : 1 + len(distances)]
        del refs[: 1 + len(distances)]
        result.append(merged_blocks(mine, others, distances))
    return result


def merge_kernel(plan, *refs):
    refs = list(refs)
    results = take(refs, plan)
    for out, blocks in zip(refs, results):
        for s, block in enumerate(blocks):
            out[s] = block


def exp_kernel(rows, student, student_tail, teacher, teacher_tail, row_ref, col_ref, *outs):
    down, across = (load_slots([ref[k] for k in range(ref.shape[0])], rows) for ref in (row_ref, col_ref))
    down = columns_of(stacked([down[0:1], down[2:3]]))
    total = student.shape[0]
    step = 64 if total % 64 == 0 else total
    for r in range(0, total, step):
        at = slice(r, r + step)
        for k, pair in enumerate(((student, student_tail), (teacher, teacher_tail))):
            matrix = jnp.concatenate([ref[at] for ref in pair], axis=1)
            outs[2 * k][at] = jnp.exp(matrix - down[at, k : k + 1])
            outs[2 * k + 1][at] = jnp.exp(matrix - across[2 * k : 2 * k + 1])


def tile_kernel(plan, n_cap, rows, width, *refs):
    refs = list(refs)
    student_row, student_col, teacher_row, teacher_col, own_row, own_col = (refs.pop(0) for _ in range(6))
    blocks = take(refs, plan)
    captions = [refs.pop(0) for _ in range(n_cap)]
    tile_ref, send_ref, first_ref = refs
    total, count = tile_ref.shape

    lane = lax.broadcasted_iota(jnp.int32, (8, LANES), 1)[:1, :rows]

    def finish(blocks, own_ref, axes, order):
        lines = load_slots(blocks, rows)
        own = load_slots([own_ref[k] for k in range(own_ref.shape[0])], rows)
        index = jnp.concatenate([owner * rows + lane for owner in owners(axes, order)], axis=1)
        lse_s, lse_t = lines[0:1] + jnp.log(lines[1:2]), lines[2:3] + jnp.log(lines[3:4])
        scale_s, scale_t = 0.5 * jnp.exp(own[0:1] - lse_s), 0.25 * jnp.exp(own[2:3] - lse_t)
        return stacked([scale_s, scale_t, index.astype(jnp.float32)])

    down = columns_of(finish(blocks[0], own_row, ROW_AXES, ROW_ORDER))
    across = finish(blocks[1], own_col, COL_AXES, COL_ORDER)
    step = 64 if total % 64 == 0 else total
    for r in range(0, total, step):
        at = slice(r, r + step)
        grad = student_row[at] * down[at, SCALE_S : SCALE_S + 1] + student_col[at] * across[SCALE_S : SCALE_S + 1]
        less = teacher_row[at] * down[at, SCALE_T : SCALE_T + 1] + teacher_col[at] * across[SCALE_T : SCALE_T + 1]
        grad = grad - less - jnp.where(down[at, INDEX : INDEX + 1] == across[INDEX : INDEX + 1], 0.5, 0.0)
        tile_ref[at] = grad.astype(jnp.bfloat16)
    send_ref[...] = tile_ref[:, count // 2 :]
    right = joined(captions, slice(0, width))
    part = jnp.dot(tile_ref[total - first_ref.shape[0] :], right, preferred_element_type=jnp.float32)
    first_ref[...] = part.astype(jnp.bfloat16)


def spread(part, outs):
    start = 0
    for out in outs:
        out[...] = part[start : start + out.shape[0]].astype(out.dtype)
        start += out.shape[0]


def image_kernel(width, tile_ref, *refs):
    parts = [ref for ref in refs if ref.dtype == jnp.bfloat16 and ref.shape[1] > width]
    right = joined(parts, slice(0, width))
    outs = refs[len(parts) :]
    count = sum(out.shape[0] for out in outs)
    spread(jnp.dot(tile_ref[:count], right, preferred_element_type=jnp.float32), outs)


def caption_kernel(tile_ref, tile_other, images, images_other, *outs):
    half = tile_other.shape[1]
    part = 0.0
    for tile, rows in ((tile_ref[:, :half], images[...]), (tile_other[...], images_other[...])):
        part = part + lax.dot_general(tile, rows, (((0,), (0,)), ((), ())), preferred_element_type=jnp.float32)
    spread(part, outs)


def sum_kernel(counts, *refs):
    refs = list(refs)
    terms = [[refs.pop(0) for _ in range(count)] for count in counts]
    outs, held, sems = refs[: len(counts)], refs[len(counts) : -1], refs[-1]
    copies = []
    for k, (group, out, here) in enumerate(zip(terms, outs, held)):
        total = group[0][...]
        for term in group[1:]:
            total = total + term[...].astype(jnp.float32)
        here[...] = total
        copies.append(pltpu.make_async_copy(here, out, sems.at[k]))
        copies[-1].start()
    for copy in copies:
        copy.wait()


VMEM, HBM = pltpu.VMEM, pltpu.HBM


def call(kernel, outs, args, flops=0, scratch=(), in_hbm=0, out_space=VMEM):
    moved = sum(math.prod(a.shape) * a.dtype.itemsize for a in list(args) + list(outs))
    spaces = [HBM] * in_hbm + [VMEM] * (len(args) - in_hbm)
    return pl.pallas_call(
        kernel,
        out_shape=[out_space(out.shape, out.dtype) for out in outs],
        in_specs=[pl.BlockSpec(memory_space=space) for space in spaces],
        out_specs=[pl.BlockSpec(memory_space=out_space)] * len(outs),
        scratch_shapes=scratch,
        compiler_params=pltpu.CompilerParams(vmem_limit_bytes=16 * 2**20),
        cost_estimate=pl.CostEstimate(flops=flops, bytes_accessed=moved, transcendentals=0),
    )(*(pltpu.with_memory_space_constraint(arg, space) for arg, space in zip(args, spaces)))


def after(value, *others):
    return lax.optimization_barrier((value, others))[0]


def local(image_student, caption_student, image_teacher, caption_teacher):
    ilo, chi, core, clo, ihi = (lax.axis_size(a) for a in ROW_AXES + COL_AXES)
    rows, width = image_student.shape
    depth = image_teacher.shape[1]
    assert rows <= LANES and core == 2 and chi > 1 and clo > 1
    n_img, n_cap = ilo * chi, core * ihi * clo
    total, columns = n_img * rows, n_cap * rows
    f32, bf16 = jnp.float32, jnp.bfloat16
    shape = jax.ShapeDtypeStruct
    dma = pltpu.SemaphoreType.DMA

    aligned = rows % 16 == 0
    if aligned:
        image, caption = call(
            pack_kernel,
            [shape((rows, width + depth), bf16)] * 2,
            [image_student, image_teacher, caption_student, caption_teacher],
            scratch=[dma((4,))],
            in_hbm=4,
        )
    else:
        image = jnp.concatenate([image_student, image_teacher], axis=1)
        caption = jnp.concatenate([caption_student, caption_teacher], axis=1)

    def assemble(parts):
        if not aligned:
            return jnp.concatenate(parts, axis=0)
        return call(assemble_kernel, [shape((len(parts) * rows, width + depth), bf16)], parts)[0]

    if aligned:
        image_near, caption_near = call(
            duplicate_kernel, [shape((rows, width + depth), bf16)] * 2, [image, caption]
        )
    else:
        image_near, caption_near = image, caption

    def gather(own, own_near, far_axis, near_axis):
        parts = {(0, c): swap(own, far_axis, c) if c else own for c in range(lax.axis_size(far_axis))}
        for h in range(1, lax.axis_size(near_axis)):
            parts.update({(h, c): swap(parts[0, c] if c else own_near, near_axis, h) for c in range(lax.axis_size(far_axis))})
        return parts

    img, cap = gather(image, image_near, "chi", "ilo"), gather(caption, caption_near, "clo", "ihi")
    early = [cap[h, 0] for h in range(ihi)]
    early = assemble([after(early[0], img[1, 0], img[0, 1])] + early[1:])
    late = [cap[h, c] for c in range(1, clo) for h in range(ihi)]
    late = assemble(late[:-1] + [after(late[-1], img[1, 1])])
    img = [img[h, c] for h in range(ilo) for c in range(chi)]
    cap = [early, late, swap(early, "core", 1), swap(late, "core", 1)]
    if not aligned:
        img, cap = [assemble(img)], [assemble(cap)]

    row_shape, col_shape = shape((n_img // 2, 8, LANES), f32), shape((n_cap // 2, 8, LANES), f32)
    head = (columns - (cap[-1].shape[0] if aligned else rows)) // LANES * LANES
    ready = cap[:-1] if aligned else cap
    skipped = [part for k, part in enumerate(cap) if sum(p.shape[0] for p in cap[: k + 1]) <= head]
    needed = cap[len(skipped) :]
    start = head - sum(part.shape[0] for part in skipped)
    student, teacher, row_head, lines, images = call(
        functools.partial(head_kernel, len(img), rows, width),
        [shape((total, head), f32)] * 2 + [row_shape, shape((8, head), f32), shape((total, width), bf16)],
        ready + img,
        2 * total * head * (width + depth),
    )
    student_tail, teacher_tail, row_stats, col_stats = call(
        functools.partial(tail_kernel, len(img), start, rows, width),
        [shape((total, columns - head), f32)] * 2 + [row_shape, col_shape],
        [row_head, lines, images] + img + needed,
        2 * total * (columns - head) * (width + depth),
    )

    images_other = swap(after(images, row_stats), "core", 1)
    exps = call(
        functools.partial(exp_kernel, rows),
        [shape((total, columns), f32)] * 4,
        [student, student_tail, teacher, teacher_tail, row_stats, col_stats],
        40 * total * columns,
    )
    exps = list(exps)
    stats = [row_stats, col_stats]
    for row_names, col_names in zip(ROW_STAGES, COL_STAGES):
        plan, blocks = [], []
        for block, names, axes in zip(stats, (row_names, col_names), (ROW_AXES, COL_AXES)):
            others = partners(names, axes)
            plan.append([distance for _, distance in others])
            blocks += [block] + [swap(block, names, mask) for mask, _ in others]
        if row_names != ROW_STAGES[-1]:
            blocks[0] = after(blocks[0], images_other)
            stats = call(functools.partial(merge_kernel, plan), [row_shape, col_shape], blocks)

    image_blocks = [(h, c) for h in range(ilo) for c in range(chi)]
    caption_blocks = [(h, c) for c in range(clo) for h in range(ihi)]

    def pieces(blocks):
        return [shape((rows, width), bf16 if h else f32) for h, _ in blocks]

    tile, tile_send, image_first = call(
        functools.partial(tile_kernel, plan, len(cap), rows, width),
        [shape((total, columns), bf16), shape((total, columns // 2), bf16), shape((rows, width), bf16)],
        exps + [row_stats, col_stats] + blocks + cap,
        2 * rows * columns * width,
    )
    tile_other = swap(tile_send, "core", 1)

    image_parts = call(
        functools.partial(image_kernel, width),
        pieces(image_blocks)[:-1],
        [tile] + cap,
        2 * total * columns * width,
    )
    image_parts = dict(zip(image_blocks, list(image_parts) + [image_first]))
    caption_parts = call(
        caption_kernel,
        pieces(caption_blocks),
        [tile, tile_other, images, images_other],
        2 * total * columns * width,
    )
    caption_parts = dict(zip(caption_blocks, caption_parts))

    def hop(parts, near, f):
        return [parts[0, f]] + [swap(parts[h, f], near, h) for h in range(1, lax.axis_size(near))]

    def rounded(terms):
        total = terms[0]
        for term in terms[1:]:
            total = total + term.astype(f32)
        return total.astype(bf16)

    image_far = [rounded(hop(image_parts, "ilo", f)) for f in range(1, chi)]
    caption_far = [rounded(hop(caption_parts, "ihi", f)) for f in range(1, clo)]
    image_terms, caption_terms = hop(image_parts, "ilo", 0), hop(caption_parts, "ihi", 0)
    image_terms += [swap(image_far[f - 1], "chi", f) for f in range(1, chi)]
    caption_terms += [swap(caption_far[f - 1], "clo", f) for f in range(1, clo)]
    out = shape((rows, width), f32)
    caption_grad, image_grad = call(
        functools.partial(sum_kernel, (len(caption_terms), len(image_terms))),
        [out, out],
        caption_terms + image_terms,
        scratch=[pltpu.VMEM((rows, width), f32)] * 2 + [dma((2,))],
        out_space=HBM,
    )
    return (image_grad, caption_grad)


def split(count):
    low = 1 << ((count.bit_length() - 1) // 2)
    return count // low, low


def solution(mesh):
    ihi, ilo = split(mesh.shape["img"] // 2)
    chi, clo = split(mesh.shape["cap"])
    fine = Mesh(mesh.devices.reshape(ihi, ilo, 2, chi, clo), ("ihi", "ilo", "core", "chi", "clo"))
    by_image = P(("ihi", "ilo", "core", "chi", "clo"), None)
    by_caption = P(("chi", "clo", "ihi", "ilo", "core"), None)
    return jax.shard_map(
        local,
        mesh=fine,
        in_specs=(by_image, by_caption, by_image, by_caption),
        out_specs=(by_image, by_caption),
        check_vma=False,
    )
```

```python
import functools
import math

import jax
import jax.numpy as jnp
from jax import lax
from jax.experimental import pallas as pl
from jax.experimental.pallas import tpu as pltpu
from jax.sharding import Mesh, PartitionSpec as P

logit_gain = 3.0
ROW_AXES = ("ilo", "chi")
COL_AXES = ("core", "clo", "ihi")
ROW_STAGES = (("ilo",), ("chi",))
COL_STAGES = (("ihi", "clo"), ("core",))
ROW_ORDER = ("ihi", "ilo", "core", "chi", "clo")
COL_ORDER = ("chi", "clo", "ihi", "ilo", "core")
LANES = 128
SLOT_LINES = 4
LSE_S, LSE_T, INDEX = range(3)


def swap(value, axis, mask):
    size = lax.axis_size(axis)
    return lax.ppermute(value, axis, [(j, j ^ mask) for j in range(size)])


def partners(names, axes):
    sizes = [lax.axis_size(a) for a in names]
    strides = [math.prod(lax.axis_size(a) for a in axes[axes.index(name) + 1 :]) for name in names]
    result = []
    for mask in range(1, math.prod(sizes)):
        distance, rest = 0, mask
        for size, stride in zip(reversed(sizes), reversed(strides)):
            distance += rest % size * stride
            rest //= size
        result.append((mask, distance))
    return result


def lines_of(columns):
    count = columns[0].shape[0]
    lane = lax.broadcasted_iota(jnp.int32, (count, LANES), 1)
    wide = jnp.zeros((count, LANES), jnp.float32)
    for k, column in enumerate(columns):
        wide = jnp.where(lane == k, column, wide)
    spare = -count % LANES
    if spare:
        wide = jnp.concatenate([wide, jnp.zeros((spare, LANES), jnp.float32)], axis=0)
    return wide.T[:8, :count]


def columns_of(lines):
    count = lines.shape[1]
    spare = -count % LANES
    if spare:
        lines = jnp.concatenate([lines, jnp.zeros((8, spare), jnp.float32)], axis=1)
    tall = jnp.concatenate([lines, jnp.zeros((LANES - 8, count + spare), jnp.float32)], axis=0)
    return tall.T[:count]


def store_slots(ref, lines, rows):
    ref[...] = jnp.zeros_like(ref)
    for s in range(2 * ref.shape[0]):
        first = s % 2 * SLOT_LINES
        ref[s // 2, first : first + SLOT_LINES, :rows] = lines[:SLOT_LINES, s * rows : (s + 1) * rows]


def load_slots(blocks, rows):
    halves = [block[first : first + SLOT_LINES, :rows] for block in blocks for first in (0, SLOT_LINES)]
    return jnp.concatenate(halves, axis=1)


def owners(axes, order):
    sizes = [lax.axis_size(a) for a in axes]
    result = []
    for s in range(math.prod(sizes)):
        place = {a: lax.axis_index(a) for a in order}
        for axis, size in zip(reversed(axes), reversed(sizes)):
            place[axis] = place[axis] ^ (s % size)
            s //= size
        owner = 0
        for axis in order:
            owner = owner * lax.axis_size(axis) + place[axis]
        result.append(owner)
    return result


def joined(refs, columns=slice(None)):
    values = [ref[:, columns] for ref in refs]
    return values[0] if len(values) == 1 else jnp.concatenate(values, axis=0)


def copy_all(pairs, sems):
    copies = [pltpu.make_async_copy(src, dst, sems.at[k]) for k, (src, dst) in enumerate(pairs)]
    for copy in copies:
        copy.start()
    for copy in copies:
        copy.wait()


def pack_kernel(image_s, image_t, caption_s, caption_t, image, caption, sems):
    width = image_s.shape[1]
    copy_all(
        [
            (image_s, image.at[:, :width]),
            (image_t, image.at[:, width:]),
            (caption_s, caption.at[:, :width]),
            (caption_t, caption.at[:, width:]),
        ],
        sems,
    )


def duplicate_kernel(*refs):
    count = len(refs) // 2
    for value, out in zip(refs[:count], refs[count:]):
        out[...] = value[...]


def assemble_kernel(*refs):
    refs[-1][...] = joined(refs[:-1])


def window(refs, start, stop, columns):
    values, first = [], 0
    for ref in refs:
        low, high = max(start - first, 0), min(stop - first, ref.shape[0])
        if low < high:
            values.append(ref[low:high, columns])
        first += ref.shape[0]
    return values[0] if len(values) == 1 else jnp.concatenate(values, axis=0)


def logits(left, right, out):
    gain = logit_gain / math.sqrt(left.shape[1])
    out[...] = gain * lax.dot_general(left, right, (((1,), (1,)), ((), ())), preferred_element_type=jnp.float32)
    matrix = out[...]
    peak = jnp.max(matrix, axis=1, keepdims=True)
    columns = [peak, jnp.sum(jnp.exp(matrix - peak), axis=1, keepdims=True)]
    peak = jnp.max(matrix, axis=0, keepdims=True)
    return columns, [peak, jnp.sum(jnp.exp(matrix - peak), axis=0, keepdims=True)]


def stacked(lines):
    count = lines[0].shape[1]
    row = lax.broadcasted_iota(jnp.int32, (8, count), 0)
    result = jnp.zeros((8, count), jnp.float32)
    for k, line in enumerate(lines):
        result = jnp.where(row == k, line, result)
    return result


def head_kernel(n_img, rows, width, *refs):
    img_parts, cap_parts = refs[:n_img], refs[n_img:-5]
    student_ref, teacher_ref, row_ref, lines_ref, images = refs[-5:]
    count = student_ref.shape[1]
    columns, lines = [], []
    for part, out in ((slice(0, width), student_ref), (slice(width, None), teacher_ref)):
        left = joined(img_parts, part)
        if out is student_ref:
            images[...] = left
        more = logits(left, window(cap_parts, 0, count, part), out)
        columns, lines = columns + more[0], lines + more[1]
    store_slots(row_ref, lines_of(columns), rows)
    lines_ref[...] = stacked(lines)


def tail_kernel(n_img, start, rows, width, head_ref, lines_ref, images, *refs):
    img_parts, cap_parts = refs[:n_img], refs[n_img:-4]
    student_ref, teacher_ref, row_ref, col_ref = refs[-4:]
    stop = start + student_ref.shape[1]
    columns, lines = [], []
    for part, out in ((slice(0, width), student_ref), (slice(width, None), teacher_ref)):
        left = images[...] if out is student_ref else joined(img_parts, part)
        more = logits(left, window(cap_parts, start, stop, part), out)
        columns, lines = columns + more[0], lines + more[1]
    store_slots(row_ref, lines_of(columns), rows)
    store_slots(col_ref, jnp.concatenate([lines_ref[...], stacked(lines)], axis=1), rows)
    for k in range(row_ref.shape[0]):
        row_ref[k] = merged(head_ref[k], row_ref[k])


def merged(x, y):
    even = lax.broadcasted_iota(jnp.int32, x.shape, 0) % 2 == 0
    x_peak, y_peak = (jnp.where(even, value, pltpu.roll(value, 1, 0)) for value in (x, y))
    peak = jnp.maximum(x_peak, y_peak)
    total = x * jnp.exp(x_peak - peak) + y * jnp.exp(y_peak - peak)
    return jnp.where(even, peak, total)


def merged_blocks(mine, others, distances, limit):
    blocks = [mine[k] for k in range(min(mine.shape[0], limit))]
    for other, distance in zip(others, distances):
        terms = [other[k ^ (distance // 2)] for k in range(len(blocks))]
        if distance % 2:
            terms = [pltpu.roll(term, SLOT_LINES, 0) for term in terms]
        blocks = [merged(block, term) for block, term in zip(blocks, terms)]
    return blocks


def take(refs, plan, limits):
    result = []
    for distances, limit in zip(plan, limits):
        mine, others = refs[0], refs[1 : 1 + len(distances)]
        del refs[: 1 + len(distances)]
        result.append(merged_blocks(mine, others, distances, limit))
    return result


def merge_kernel(plan, *refs):
    refs = list(refs)
    results = take(refs, plan, [ref.shape[0] for ref in refs[-2:]])
    for out, blocks in zip(refs, results):
        for s in range(out.shape[0]):
            out[s] = blocks[s] if s < len(blocks) else jnp.zeros_like(blocks[0])


def tile_kernel(plan, limits, n_cap, rows, width, *refs):
    refs = list(refs)
    student_refs, teacher_refs = (refs.pop(0), refs.pop(0)), (refs.pop(0), refs.pop(0))
    blocks = take(refs, plan, limits)
    captions = [refs.pop(0) for _ in range(n_cap)]
    tile_ref, send_ref, first_ref = refs
    total, count = tile_ref.shape

    lane = lax.broadcasted_iota(jnp.int32, (8, LANES), 1)[:1, :rows]

    def finish(blocks, axes, order):
        lines = load_slots(blocks, rows)
        index = jnp.concatenate([owner * rows + lane for owner in owners(axes, order)], axis=1)
        lse_s, lse_t = lines[0:1] + jnp.log(lines[1:2]), lines[2:3] + jnp.log(lines[3:4])
        return stacked([lse_s, lse_t, index.astype(jnp.float32)])

    down = columns_of(finish(blocks[0], ROW_AXES, ROW_ORDER))
    across = finish(blocks[1], COL_AXES, COL_ORDER)
    step = 64 if total % 64 == 0 else total
    for r in range(0, total, step):
        at = slice(r, r + step)
        s, t = (jnp.concatenate([ref[at] for ref in pair], axis=1) for pair in (student_refs, teacher_refs))
        grad = 0.5 * (jnp.exp(s - down[at, 0:1]) + jnp.exp(s - across[0:1]))
        grad = grad - 0.25 * (jnp.exp(t - down[at, 1:2]) + jnp.exp(t - across[1:2]))
        grad = grad - jnp.where(down[at, INDEX : INDEX + 1] == across[INDEX : INDEX + 1], 0.5, 0.0)
        tile_ref[at] = grad.astype(jnp.bfloat16)
    send_ref[...] = tile_ref[:, count // 2 :]
    right = joined(captions, slice(0, width))
    part = jnp.dot(tile_ref[total - first_ref.shape[0] :], right, preferred_element_type=jnp.float32)
    first_ref[...] = part.astype(jnp.bfloat16)


def spread(part, outs):
    start = 0
    for out in outs:
        out[...] = part[start : start + out.shape[0]].astype(out.dtype)
        start += out.shape[0]


def image_kernel(width, tile_ref, *refs):
    parts = [ref for ref in refs if ref.dtype == jnp.bfloat16 and ref.shape[1] > width]
    right = joined(parts, slice(0, width))
    outs = refs[len(parts) :]
    count = sum(out.shape[0] for out in outs)
    spread(jnp.dot(tile_ref[:count], right, preferred_element_type=jnp.float32), outs)


def caption_kernel(tile_ref, tile_other, images, images_other, *outs):
    half = tile_other.shape[1]
    part = 0.0
    for tile, rows in ((tile_ref[:, :half], images[...]), (tile_other[...], images_other[...])):
        part = part + lax.dot_general(tile, rows, (((0,), (0,)), ((), ())), preferred_element_type=jnp.float32)
    spread(part, outs)


def sum_kernel(counts, *refs):
    refs = list(refs)
    terms = [[refs.pop(0) for _ in range(count)] for count in counts]
    outs, held, sems = refs[: len(counts)], refs[len(counts) : -1], refs[-1]
    copies = []
    for k, (group, out, here) in enumerate(zip(terms, outs, held)):
        total = group[0][...]
        for term in group[1:]:
            total = total + term[...].astype(jnp.float32)
        here[...] = total
        copies.append(pltpu.make_async_copy(here, out, sems.at[k]))
        copies[-1].start()
    for copy in copies:
        copy.wait()


VMEM, HBM = pltpu.VMEM, pltpu.HBM


def call(kernel, outs, args, flops=0, scratch=(), in_hbm=0, out_space=VMEM):
    moved = sum(math.prod(a.shape) * a.dtype.itemsize for a in list(args) + list(outs))
    spaces = [HBM] * in_hbm + [VMEM] * (len(args) - in_hbm)
    return pl.pallas_call(
        kernel,
        out_shape=[out_space(out.shape, out.dtype) for out in outs],
        in_specs=[pl.BlockSpec(memory_space=space) for space in spaces],
        out_specs=[pl.BlockSpec(memory_space=out_space)] * len(outs),
        scratch_shapes=scratch,
        compiler_params=pltpu.CompilerParams(vmem_limit_bytes=16 * 2**20),
        cost_estimate=pl.CostEstimate(flops=flops, bytes_accessed=moved, transcendentals=0),
    )(*(pltpu.with_memory_space_constraint(arg, space) for arg, space in zip(args, spaces)))


def after(value, *others):
    return lax.optimization_barrier((value, others))[0]


def local(image_student, caption_student, image_teacher, caption_teacher):
    ilo, chi, core, clo, ihi = (lax.axis_size(a) for a in ROW_AXES + COL_AXES)
    rows, width = image_student.shape
    depth = image_teacher.shape[1]
    assert rows <= LANES and core == 2 and chi > 1 and clo > 1
    n_img, n_cap = ilo * chi, core * ihi * clo
    total, columns = n_img * rows, n_cap * rows
    f32, bf16 = jnp.float32, jnp.bfloat16
    shape = jax.ShapeDtypeStruct
    dma = pltpu.SemaphoreType.DMA

    aligned = rows % 16 == 0
    if aligned:
        image, caption = call(
            pack_kernel,
            [shape((rows, width + depth), bf16)] * 2,
            [image_student, image_teacher, caption_student, caption_teacher],
            scratch=[dma((4,))],
            in_hbm=4,
        )
    else:
        image = jnp.concatenate([image_student, image_teacher], axis=1)
        caption = jnp.concatenate([caption_student, caption_teacher], axis=1)

    def assemble(parts):
        if not aligned:
            return jnp.concatenate(parts, axis=0)
        return call(assemble_kernel, [shape((len(parts) * rows, width + depth), bf16)], parts)[0]

    if aligned:
        image_near, caption_near = call(
            duplicate_kernel, [shape((rows, width + depth), bf16)] * 2, [image, caption]
        )
    else:
        image_near, caption_near = image, caption

    def gather(own, own_near, far_axis, near_axis):
        parts = {(0, c): swap(own, far_axis, c) if c else own for c in range(lax.axis_size(far_axis))}
        for h in range(1, lax.axis_size(near_axis)):
            parts.update({(h, c): swap(parts[0, c] if c else own_near, near_axis, h) for c in range(lax.axis_size(far_axis))})
        return parts

    img, cap = gather(image, image_near, "chi", "ilo"), gather(caption, caption_near, "clo", "ihi")
    early = [cap[h, 0] for h in range(ihi)]
    early = assemble([after(early[0], img[1, 0], img[0, 1])] + early[1:])
    late = [cap[h, c] for c in range(1, clo) for h in range(ihi)]
    late = assemble(late[:-1] + [after(late[-1], img[1, 1])])
    img = [img[h, c] for h in range(ilo) for c in range(chi)]
    cap = [early, late, swap(early, "core", 1), swap(late, "core", 1)]
    if not aligned:
        img, cap = [assemble(img)], [assemble(cap)]

    row_shape, col_shape = shape((n_img // 2, 8, LANES), f32), shape((n_cap // 2, 8, LANES), f32)
    head = (columns - (cap[-1].shape[0] if aligned else rows)) // LANES * LANES
    ready = cap[:-1] if aligned else cap
    skipped = [part for k, part in enumerate(cap) if sum(p.shape[0] for p in cap[: k + 1]) <= head]
    needed = cap[len(skipped) :]
    start = head - sum(part.shape[0] for part in skipped)
    student, teacher, row_head, lines, images = call(
        functools.partial(head_kernel, len(img), rows, width),
        [shape((total, head), f32)] * 2 + [row_shape, shape((8, head), f32), shape((total, width), bf16)],
        img + ready,
        2 * total * head * (width + depth),
    )
    student_tail, teacher_tail, row_stats, col_stats = call(
        functools.partial(tail_kernel, len(img), start, rows, width),
        [shape((total, columns - head), f32)] * 2 + [row_shape, col_shape],
        [row_head, lines, images] + img + needed,
        2 * total * (columns - head) * (width + depth),
    )

    images_other = swap(after(images, row_stats), "core", 1)
    stats = [row_stats, col_stats]
    for row_names, col_names in zip(ROW_STAGES, COL_STAGES):
        plan, blocks = [], []
        for block, names, axes in zip(stats, (row_names, col_names), (ROW_AXES, COL_AXES)):
            others = partners(names, axes)
            plan.append([distance for _, distance in others])
            blocks += [block] + [swap(block, names, mask) for mask, _ in others]
        if row_names != ROW_STAGES[-1]:
            blocks[0] = after(blocks[0], images_other)
            row_wide = shape((max(n_img // 2, n_cap // 2), 8, LANES), f32)
            stats = call(functools.partial(merge_kernel, plan), [row_wide, col_shape], blocks)

    image_blocks = [(h, c) for h in range(ilo) for c in range(chi)]
    caption_blocks = [(h, c) for c in range(clo) for h in range(ihi)]

    def pieces(blocks):
        return [shape((rows, width), bf16 if h else f32) for h, _ in blocks]

    tile, tile_send, image_first = call(
        functools.partial(tile_kernel, plan, (n_img // 2, n_cap // 2), len(cap), rows, width),
        [shape((total, columns), bf16), shape((total, columns // 2), bf16), shape((rows, width), bf16)],
        [student, student_tail, teacher, teacher_tail] + blocks + cap,
        2 * rows * columns * width,
    )
    tile_other = swap(tile_send, "core", 1)

    image_parts = call(
        functools.partial(image_kernel, width),
        pieces(image_blocks)[:-1],
        [tile] + cap,
        2 * total * columns * width,
    )
    image_parts = dict(zip(image_blocks, list(image_parts) + [image_first]))
    caption_parts = call(
        caption_kernel,
        pieces(caption_blocks),
        [tile, tile_other, images, images_other],
        2 * total * columns * width,
    )
    caption_parts = dict(zip(caption_blocks, caption_parts))

    def hop(parts, near, f):
        return [parts[0, f]] + [swap(parts[h, f], near, h) for h in range(1, lax.axis_size(near))]

    def rounded(terms):
        total = terms[0]
        for term in terms[1:]:
            total = total + term.astype(f32)
        return total.astype(bf16)

    image_far = [rounded(hop(image_parts, "ilo", f)) for f in range(1, chi)]
    caption_far = [rounded(hop(caption_parts, "ihi", f)) for f in range(1, clo)]
    image_terms, caption_terms = hop(image_parts, "ilo", 0), hop(caption_parts, "ihi", 0)
    image_terms += [swap(image_far[f - 1], "chi", f) for f in range(1, chi)]
    caption_terms += [swap(caption_far[f - 1], "clo", f) for f in range(1, clo)]
    out = shape((rows, width), f32)
    caption_grad, image_grad = call(
        functools.partial(sum_kernel, (len(caption_terms), len(image_terms))),
        [out, out],
        caption_terms + image_terms,
        scratch=[pltpu.VMEM((rows, width), f32)] * 2 + [dma((2,))],
        out_space=HBM,
    )
    return (image_grad, caption_grad)


def split(count):
    low = 1 << ((count.bit_length() - 1) // 2)
    return count // low, low


def solution(mesh):
    ihi, ilo = split(mesh.shape["img"] // 2)
    chi, clo = split(mesh.shape["cap"])
    fine = Mesh(mesh.devices.reshape(ihi, ilo, 2, chi, clo), ("ihi", "ilo", "core", "chi", "clo"))
    by_image = P(("ihi", "ilo", "core", "chi", "clo"), None)
    by_caption = P(("chi", "clo", "ihi", "ilo", "core"), None)
    return jax.shard_map(
        local,
        mesh=fine,
        in_specs=(by_image, by_caption, by_image, by_caption),
        out_specs=(by_image, by_caption),
        check_vma=False,
    )
```

```python
import functools
import math

import jax
import jax.numpy as jnp
from jax import lax
from jax.experimental import pallas as pl
from jax.experimental.pallas import tpu as pltpu
from jax.sharding import Mesh, PartitionSpec as P

logit_gain = 3.0
ROW_AXES = ("ilo", "chi")
COL_AXES = ("core", "clo", "ihi")
ROW_STAGES = (("ilo",), ("chi",))
COL_STAGES = (("ihi", "clo"), ("core",))
ROW_ORDER = ("ihi", "ilo", "core", "chi", "clo")
COL_ORDER = ("chi", "clo", "ihi", "ilo", "core")
LANES = 128
SLOT_LINES = 4
LSE_S, LSE_T, INDEX = range(3)


def swap(value, axis, mask):
    size = lax.axis_size(axis)
    return lax.ppermute(value, axis, [(j, j ^ mask) for j in range(size)])


def partners(names, axes):
    sizes = [lax.axis_size(a) for a in names]
    strides = [math.prod(lax.axis_size(a) for a in axes[axes.index(name) + 1 :]) for name in names]
    result = []
    for mask in range(1, math.prod(sizes)):
        distance, rest = 0, mask
        for size, stride in zip(reversed(sizes), reversed(strides)):
            distance += rest % size * stride
            rest //= size
        result.append((mask, distance))
    return result


def lines_of(columns):
    count = columns[0].shape[0]
    lane = lax.broadcasted_iota(jnp.int32, (count, LANES), 1)
    wide = jnp.zeros((count, LANES), jnp.float32)
    for k, column in enumerate(columns):
        wide = jnp.where(lane == k, column, wide)
    spare = -count % LANES
    if spare:
        wide = jnp.concatenate([wide, jnp.zeros((spare, LANES), jnp.float32)], axis=0)
    return wide.T[:8, :count]


def columns_of(lines):
    count = lines.shape[1]
    spare = -count % LANES
    if spare:
        lines = jnp.concatenate([lines, jnp.zeros((8, spare), jnp.float32)], axis=1)
    tall = jnp.concatenate([lines, jnp.zeros((LANES - 8, count + spare), jnp.float32)], axis=0)
    return tall.T[:count]


def store_slots(ref, lines, rows):
    ref[...] = jnp.zeros_like(ref)
    for s in range(2 * ref.shape[0]):
        first = s % 2 * SLOT_LINES
        ref[s // 2, first : first + SLOT_LINES, :rows] = lines[:SLOT_LINES, s * rows : (s + 1) * rows]


def load_slots(blocks, rows):
    halves = [block[first : first + SLOT_LINES, :rows] for block in blocks for first in (0, SLOT_LINES)]
    return jnp.concatenate(halves, axis=1)


def owners(axes, order):
    sizes = [lax.axis_size(a) for a in axes]
    result = []
    for s in range(math.prod(sizes)):
        place = {a: lax.axis_index(a) for a in order}
        for axis, size in zip(reversed(axes), reversed(sizes)):
            place[axis] = place[axis] ^ (s % size)
            s //= size
        owner = 0
        for axis in order:
            owner = owner * lax.axis_size(axis) + place[axis]
        result.append(owner)
    return result


def joined(refs, columns=slice(None)):
    values = [ref[:, columns] for ref in refs]
    return values[0] if len(values) == 1 else jnp.concatenate(values, axis=0)


def copy_all(pairs, sems):
    copies = [pltpu.make_async_copy(src, dst, sems.at[k]) for k, (src, dst) in enumerate(pairs)]
    for copy in copies:
        copy.start()
    for copy in copies:
        copy.wait()


def pack_kernel(image_s, image_t, caption_s, caption_t, image, caption, sems):
    width = image_s.shape[1]
    copy_all(
        [
            (image_s, image.at[:, :width]),
            (image_t, image.at[:, width:]),
            (caption_s, caption.at[:, :width]),
            (caption_t, caption.at[:, width:]),
        ],
        sems,
    )


def duplicate_kernel(*refs):
    count = len(refs) // 2
    for value, out in zip(refs[:count], refs[count:]):
        out[...] = value[...]


def assemble_kernel(*refs):
    refs[-1][...] = joined(refs[:-1])


def window(refs, start, stop, columns):
    values, first = [], 0
    for ref in refs:
        low, high = max(start - first, 0), min(stop - first, ref.shape[0])
        if low < high:
            values.append(ref[low:high, columns])
        first += ref.shape[0]
    return values[0] if len(values) == 1 else jnp.concatenate(values, axis=0)


def logits(left, right, out):
    gain = logit_gain / math.sqrt(left.shape[1])
    out[...] = gain * lax.dot_general(left, right, (((1,), (1,)), ((), ())), preferred_element_type=jnp.float32)
    matrix = out[...]
    peak = jnp.max(matrix, axis=1, keepdims=True)
    columns = [peak, jnp.sum(jnp.exp(matrix - peak), axis=1, keepdims=True)]
    peak = jnp.max(matrix, axis=0, keepdims=True)
    return columns, [peak, jnp.sum(jnp.exp(matrix - peak), axis=0, keepdims=True)]


def stacked(lines):
    count = lines[0].shape[1]
    row = lax.broadcasted_iota(jnp.int32, (8, count), 0)
    result = jnp.zeros((8, count), jnp.float32)
    for k, line in enumerate(lines):
        result = jnp.where(row == k, line, result)
    return result


def head_kernel(n_img, rows, width, *refs):
    img_parts, cap_parts = refs[:n_img], refs[n_img:-5]
    student_ref, teacher_ref, row_ref, lines_ref, images = refs[-5:]
    count = student_ref.shape[1]
    columns, lines = [], []
    for part, out in ((slice(0, width), student_ref), (slice(width, None), teacher_ref)):
        left = joined(img_parts, part)
        if out is student_ref:
            images[...] = left
        more = logits(left, window(cap_parts, 0, count, part), out)
        columns, lines = columns + more[0], lines + more[1]
    store_slots(row_ref, lines_of(columns), rows)
    lines_ref[...] = stacked(lines)


def tail_kernel(n_img, start, rows, width, head_ref, lines_ref, images, *refs):
    img_parts, cap_parts = refs[:n_img], refs[n_img:-4]
    student_ref, teacher_ref, row_ref, col_ref = refs[-4:]
    stop = start + student_ref.shape[1]
    columns, lines = [], []
    for part, out in ((slice(0, width), student_ref), (slice(width, None), teacher_ref)):
        left = images[...] if out is student_ref else joined(img_parts, part)
        more = logits(left, window(cap_parts, start, stop, part), out)
        columns, lines = columns + more[0], lines + more[1]
    store_slots(row_ref, lines_of(columns), rows)
    store_slots(col_ref, jnp.concatenate([lines_ref[...], stacked(lines)], axis=1), rows)
    for k in range(row_ref.shape[0]):
        row_ref[k] = merged(head_ref[k], row_ref[k])


def merged(x, y):
    even = lax.broadcasted_iota(jnp.int32, x.shape, 0) % 2 == 0
    x_peak, y_peak = (jnp.where(even, value, pltpu.roll(value, 1, 0)) for value in (x, y))
    peak = jnp.maximum(x_peak, y_peak)
    total = x * jnp.exp(x_peak - peak) + y * jnp.exp(y_peak - peak)
    return jnp.where(even, peak, total)


def merged_blocks(mine, others, distances):
    blocks = [mine[k] for k in range(mine.shape[0])]
    for other, distance in zip(others, distances):
        terms = [other[k ^ (distance // 2)] for k in range(len(blocks))]
        if distance % 2:
            terms = [pltpu.roll(term, SLOT_LINES, 0) for term in terms]
        blocks = [merged(block, term) for block, term in zip(blocks, terms)]
    return blocks


def take(refs, plan):
    result = []
    for distances in plan:
        mine, others = refs[0], refs[1 : 1 + len(distances)]
        del refs[: 1 + len(distances)]
        result.append(merged_blocks(mine, others, distances))
    return result


def merge_kernel(plan, *refs):
    refs = list(refs)
    results = take(refs, plan)
    for out, blocks in zip(refs, results):
        for s, block in enumerate(blocks):
            out[s] = block


def tile_kernel(plan, n_cap, rows, width, *refs):
    refs = list(refs)
    student_refs, teacher_refs = (refs.pop(0), refs.pop(0)), (refs.pop(0), refs.pop(0))
    blocks = take(refs, plan)
    captions = [refs.pop(0) for _ in range(n_cap)]
    tile_ref, send_ref, send_more, first_ref = refs
    total, count = tile_ref.shape

    lane = lax.broadcasted_iota(jnp.int32, (8, LANES), 1)[:1, :rows]

    def finish(blocks, axes, order):
        lines = load_slots(blocks, rows)
        index = jnp.concatenate([owner * rows + lane for owner in owners(axes, order)], axis=1)
        lse_s, lse_t = lines[0:1] + jnp.log(lines[1:2]), lines[2:3] + jnp.log(lines[3:4])
        return stacked([lse_s, lse_t, index.astype(jnp.float32)])

    down = columns_of(finish(blocks[0], ROW_AXES, ROW_ORDER))
    across = finish(blocks[1], COL_AXES, COL_ORDER)
    step = 64 if total % 64 == 0 else total
    for r in range(0, total, step):
        at = slice(r, r + step)
        s, t = (jnp.concatenate([ref[at] for ref in pair], axis=1) for pair in (student_refs, teacher_refs))
        grad = 0.5 * (jnp.exp(s - down[at, 0:1]) + jnp.exp(s - across[0:1]))
        grad = grad - 0.25 * (jnp.exp(t - down[at, 1:2]) + jnp.exp(t - across[1:2]))
        grad = grad - jnp.where(down[at, INDEX : INDEX + 1] == across[INDEX : INDEX + 1], 0.5, 0.0)
        tile_ref[at] = grad.astype(jnp.bfloat16)
    send_ref[...] = tile_ref[: total // 2, count // 2 :]
    send_more[...] = tile_ref[total // 2 :, count // 2 :]
    right = joined(captions, slice(0, width))
    part = jnp.dot(tile_ref[total - first_ref.shape[0] :], right, preferred_element_type=jnp.float32)
    first_ref[...] = part.astype(jnp.bfloat16)


def spread(part, outs):
    start = 0
    for out in outs:
        out[...] = part[start : start + out.shape[0]].astype(out.dtype)
        start += out.shape[0]


def image_kernel(width, tile_ref, *refs):
    parts = [ref for ref in refs if ref.dtype == jnp.bfloat16 and ref.shape[1] > width]
    right = joined(parts, slice(0, width))
    outs = refs[len(parts) :]
    count = sum(out.shape[0] for out in outs)
    spread(jnp.dot(tile_ref[:count], right, preferred_element_type=jnp.float32), outs)


def caption_kernel(tile_ref, other, more, images, images_other, *outs):
    half = other.shape[1]
    tile = jnp.concatenate([other[...], more[...]], axis=0)
    part = 0.0
    for tile, rows in ((tile_ref[:, :half], images[...]), (tile, images_other[...])):
        part = part + lax.dot_general(tile, rows, (((0,), (0,)), ((), ())), preferred_element_type=jnp.float32)
    spread(part, outs)


def sum_kernel(counts, *refs):
    refs = list(refs)
    terms = [[refs.pop(0) for _ in range(count)] for count in counts]
    outs, held, sems = refs[: len(counts)], refs[len(counts) : -1], refs[-1]
    copies = []
    for k, (group, out, here) in enumerate(zip(terms, outs, held)):
        total = group[0][...]
        for term in group[1:]:
            total = total + term[...].astype(jnp.float32)
        here[...] = total
        copies.append(pltpu.make_async_copy(here, out, sems.at[k]))
        copies[-1].start()
    for copy in copies:
        copy.wait()


VMEM, HBM = pltpu.VMEM, pltpu.HBM


def call(kernel, outs, args, flops=0, scratch=(), in_hbm=0, out_space=VMEM):
    moved = sum(math.prod(a.shape) * a.dtype.itemsize for a in list(args) + list(outs))
    spaces = [HBM] * in_hbm + [VMEM] * (len(args) - in_hbm)
    return pl.pallas_call(
        kernel,
        out_shape=[out_space(out.shape, out.dtype) for out in outs],
        in_specs=[pl.BlockSpec(memory_space=space) for space in spaces],
        out_specs=[pl.BlockSpec(memory_space=out_space)] * len(outs),
        scratch_shapes=scratch,
        compiler_params=pltpu.CompilerParams(vmem_limit_bytes=16 * 2**20),
        cost_estimate=pl.CostEstimate(flops=flops, bytes_accessed=moved, transcendentals=0),
    )(*(pltpu.with_memory_space_constraint(arg, space) for arg, space in zip(args, spaces)))


def after(value, *others):
    return lax.optimization_barrier((value, others))[0]


def local(image_student, caption_student, image_teacher, caption_teacher):
    ilo, chi, core, clo, ihi = (lax.axis_size(a) for a in ROW_AXES + COL_AXES)
    rows, width = image_student.shape
    depth = image_teacher.shape[1]
    assert rows <= LANES and core == 2 and chi > 1 and clo > 1
    n_img, n_cap = ilo * chi, core * ihi * clo
    total, columns = n_img * rows, n_cap * rows
    f32, bf16 = jnp.float32, jnp.bfloat16
    shape = jax.ShapeDtypeStruct
    dma = pltpu.SemaphoreType.DMA

    aligned = rows % 16 == 0
    if aligned:
        image, caption = call(
            pack_kernel,
            [shape((rows, width + depth), bf16)] * 2,
            [image_student, image_teacher, caption_student, caption_teacher],
            scratch=[dma((4,))],
            in_hbm=4,
        )
    else:
        image = jnp.concatenate([image_student, image_teacher], axis=1)
        caption = jnp.concatenate([caption_student, caption_teacher], axis=1)

    def assemble(parts):
        if not aligned:
            return jnp.concatenate(parts, axis=0)
        return call(assemble_kernel, [shape((len(parts) * rows, width + depth), bf16)], parts)[0]

    if aligned:
        image_near, caption_near = call(
            duplicate_kernel, [shape((rows, width + depth), bf16)] * 2, [image, caption]
        )
    else:
        image_near, caption_near = image, caption

    def gather(own, own_near, far_axis, near_axis):
        parts = {(0, c): swap(own, far_axis, c) if c else own for c in range(lax.axis_size(far_axis))}
        for h in range(1, lax.axis_size(near_axis)):
            parts.update({(h, c): swap(parts[0, c] if c else own_near, near_axis, h) for c in range(lax.axis_size(far_axis))})
        return parts

    img, cap = gather(image, image_near, "chi", "ilo"), gather(caption, caption_near, "clo", "ihi")
    early = [cap[h, 0] for h in range(ihi)]
    early = assemble([after(early[0], img[1, 0], img[0, 1])] + early[1:])
    late = [cap[h, c] for c in range(1, clo) for h in range(ihi)]
    late = assemble(late[:-1] + [after(late[-1], img[1, 1])])
    img = [img[h, c] for h in range(ilo) for c in range(chi)]
    cap = [early, late, swap(early, "core", 1), swap(late, "core", 1)]
    if not aligned:
        img, cap = [assemble(img)], [assemble(cap)]

    row_shape, col_shape = shape((n_img // 2, 8, LANES), f32), shape((n_cap // 2, 8, LANES), f32)
    head = (columns - (cap[-1].shape[0] if aligned else rows)) // LANES * LANES
    ready = cap[:-1] if aligned else cap
    skipped = [part for k, part in enumerate(cap) if sum(p.shape[0] for p in cap[: k + 1]) <= head]
    needed = cap[len(skipped) :]
    start = head - sum(part.shape[0] for part in skipped)
    student, teacher, row_head, lines, images = call(
        functools.partial(head_kernel, len(img), rows, width),
        [shape((total, head), f32)] * 2 + [row_shape, shape((8, head), f32), shape((total, width), bf16)],
        img + ready,
        2 * total * head * (width + depth),
    )
    student_tail, teacher_tail, row_stats, col_stats = call(
        functools.partial(tail_kernel, len(img), start, rows, width),
        [shape((total, columns - head), f32)] * 2 + [row_shape, col_shape],
        [row_head, lines, images] + img + needed,
        2 * total * (columns - head) * (width + depth),
    )

    images_other = swap(after(images, row_stats), "core", 1)
    stats = [row_stats, col_stats]
    for row_names, col_names in zip(ROW_STAGES, COL_STAGES):
        plan, blocks = [], []
        for block, names, axes in zip(stats, (row_names, col_names), (ROW_AXES, COL_AXES)):
            others = partners(names, axes)
            plan.append([distance for _, distance in others])
            blocks += [block] + [swap(block, names, mask) for mask, _ in others]
        if row_names != ROW_STAGES[-1]:
            blocks[0] = after(blocks[0], images_other)
            stats = call(functools.partial(merge_kernel, plan), [row_shape, col_shape], blocks)

    image_blocks = [(h, c) for h in range(ilo) for c in range(chi)]
    caption_blocks = [(h, c) for c in range(clo) for h in range(ihi)]

    def pieces(blocks):
        return [shape((rows, width), bf16 if h else f32) for h, _ in blocks]

    tile, tile_send, tile_more, image_first = call(
        functools.partial(tile_kernel, plan, len(cap), rows, width),
        [shape((total, columns), bf16)] + [shape((total // 2, columns // 2), bf16)] * 2 + [shape((rows, width), bf16)],
        [student, student_tail, teacher, teacher_tail] + blocks + cap,
        2 * rows * columns * width,
    )
    tile_other, tile_other_more = swap(tile_send, "core", 1), swap(tile_more, "core", 1)

    image_parts = call(
        functools.partial(image_kernel, width),
        pieces(image_blocks)[:-1],
        [tile] + cap,
        2 * total * columns * width,
    )
    image_parts = dict(zip(image_blocks, list(image_parts) + [image_first]))
    caption_parts = call(
        caption_kernel,
        pieces(caption_blocks),
        [tile, tile_other, tile_other_more, images, images_other],
        2 * total * columns * width,
    )
    caption_parts = dict(zip(caption_blocks, caption_parts))

    def hop(parts, near, f):
        return [parts[0, f]] + [swap(parts[h, f], near, h) for h in range(1, lax.axis_size(near))]

    def rounded(terms):
        total = terms[0]
        for term in terms[1:]:
            total = total + term.astype(f32)
        return total.astype(bf16)

    image_far = [rounded(hop(image_parts, "ilo", f)) for f in range(1, chi)]
    caption_far = [rounded(hop(caption_parts, "ihi", f)) for f in range(1, clo)]
    image_terms, caption_terms = hop(image_parts, "ilo", 0), hop(caption_parts, "ihi", 0)
    image_terms += [swap(image_far[f - 1], "chi", f) for f in range(1, chi)]
    caption_terms += [swap(caption_far[f - 1], "clo", f) for f in range(1, clo)]
    out = shape((rows, width), f32)
    caption_grad, image_grad = call(
        functools.partial(sum_kernel, (len(caption_terms), len(image_terms))),
        [out, out],
        caption_terms + image_terms,
        scratch=[pltpu.VMEM((rows, width), f32)] * 2 + [dma((2,))],
        out_space=HBM,
    )
    return (image_grad, caption_grad)


def split(count):
    low = 1 << ((count.bit_length() - 1) // 2)
    return count // low, low


def solution(mesh):
    ihi, ilo = split(mesh.shape["img"] // 2)
    chi, clo = split(mesh.shape["cap"])
    fine = Mesh(mesh.devices.reshape(ihi, ilo, 2, chi, clo), ("ihi", "ilo", "core", "chi", "clo"))
    by_image = P(("ihi", "ilo", "core", "chi", "clo"), None)
    by_caption = P(("chi", "clo", "ihi", "ilo", "core"), None)
    return jax.shard_map(
        local,
        mesh=fine,
        in_specs=(by_image, by_caption, by_image, by_caption),
        out_specs=(by_image, by_caption),
        check_vma=False,
    )
```
